32 devices in a mesh: expert: 8 (over y, x, core), dp: 4 (over z).
Axes of the slice: x: 2, y: 2, z: 4, core: 2. Of those that a mesh axis runs over, the one named last changes fastest.
Arguments:
- frames_in: bfloat16 [8, 512, 1536], P('expert', 'dp'), may hold values from -6 to 6
- conv_kernel: bfloat16 [31, 1536], replicated, may hold values from -1 to 1
- norm_gain: bfloat16 [1536], replicated, may hold values from 0.099609375 to 1.8984375
- router: bfloat16 [1536, 8], replicated, may hold values from -0.15625 to 0.15625
- w_in: bfloat16 [8, 3072, 1536], P('expert', 'dp'), may hold values from -0.15625 to 0.15625
- w_out: bfloat16 [8, 3072, 1536], P('expert', 'dp'), may hold values from -0.109375 to 0.109375
- routes: int32 [8, 512, 2], P('expert', 'dp'), may hold values from 0 to 7, all different within a row; in each aligned block of 128 rows (0 to 127, 128 to 255, ..., all dimensions but the last counted through in order) at most 36 rows name the same one
Outputs:
- block_output: bfloat16 [8, 512, 1536], P('expert', 'dp')
The draws below stay inside these ranges and needn't reach their ends.
Inputs may be any that keep to these rules, and one draw needn't show every extreme that they name: `routes`: each frame names 2 different experts. In each aligned block of 128 frames of an utterance (the frames of one device) no expert is named more than 36 times, a bound that some block reaches.
All inputs are finite; a program needn't handle non-finite values.
Results may differ from the reference program's by a relative error of at most 0.007.
Values may be sent and summed in bfloat16 or wider, within the bound.
A program may use at most 64 MiB of HBM per device.

```python
import math
import jax
import jax.numpy as jnp
import numpy as np
from jax import lax

D = 1536
FF = 3072
KSIZE = 31
TOP = 2
TOK_DEV = 128
EXPERTS = 8
UTTS = 8
FRAMES = 512
CAP = 36
N_DP = 4


def steps_of(key, shape, pieces, least, high):
    def one(axis_at, shards_of):
        draws = jax.random.uniform(jax.random.fold_in(jax.random.fold_in(key, 6), axis_at), (shards_of,), jnp.float32, least / len(pieces), high / len(pieces))
        return jnp.repeat(jnp.exp(draws), shape[axis_at] // shards_of).reshape((-1,) + (1,) * (len(shape) - axis_at - 1))

    gain = one(*pieces[0])
    for cut in pieces[1:]:
        gain = gain * one(*cut)
    return gain


def shared_out(own_key, own, number, rows, amount, top, reach, lean):
    sequence = jax.random.permutation(own_key, amount)
    crowded, usual = load_shares(amount, rows * top, reach, lean, True), load_shares(amount, rows * top, reach, lean, False)
    places = jnp.arange(amount)

    def named(lengths, turn):
        used = int((lengths > 0).sum())
        fixed = max(1, used // 4)
        shifted = fixed + (places - fixed + turn * (used - fixed)) % max(1, amount - fixed)
        return jnp.zeros((amount,), jnp.int32).at[sequence[jnp.where(places < fixed, places, shifted)]].set(jnp.asarray(lengths, jnp.int32))

    lengths = jnp.where(number % 4 == 0, named(crowded, number // 4), named(usual, number - number // 4 - 1))
    mixed = jax.random.permutation(jax.random.fold_in(own, 3), amount)
    giver, taker = mixed[0:amount // 2 * 2:2], mixed[1:amount // 2 * 2:2]
    slack = jnp.minimum(lengths[giver] - 1, reach - lengths[taker]) // 2
    slack = jnp.where((giver == sequence[0]) | (taker == sequence[0]) | (lengths[taker] == 0), 0, jnp.maximum(slack, 0))
    shifted = jax.random.randint(jax.random.fold_in(own, 4), (amount // 2,), 0, 1 << 20) % (slack + 1)
    lengths = lengths.at[giver].add(-shifted).at[taker].add(shifted)
    items = jnp.searchsorted(jnp.cumsum(lengths), jnp.arange(rows * top), side="right").astype(jnp.int32)
    listing = items.reshape(top, rows).T
    listing = listing[jax.random.permutation(jax.random.fold_in(own, 1), rows)]
    turn = jax.random.randint(jax.random.fold_in(own, 2), (rows, 1), 0, top)
    return jnp.take_along_axis(listing, (jnp.arange(top)[None, :] + turn) % top, axis=1)


def load_shares(amount, total, reach, skew, full):
    portions = [(1 << 20) // math.isqrt(rank ** skew) + 1 for rank in range(1, amount + 1)]
    largest = reach if full else min(reach, max(-(-total // amount), total * portions[0] // sum(portions)))
    least = 1 if total - largest >= amount - 1 else 0
    given, rest = [largest] + [least] * (amount - 1), total - largest - least * (amount - 1)
    while rest > 0:
        movable = [i for i in range(1, amount) if given[i] < largest] or [i for i in range(1, amount) if given[i] < reach]
        pool, remaining = sum([portions[i] for i in movable]), rest
        for i in movable:
            more = min(reach - given[i], max(1, remaining * portions[i] // pool), rest)
            given[i] = given[i] + more
            rest = rest - more
    return np.array(given)


def normal_values(rng, extent, width, limit, pieces=(), kind=jnp.bfloat16):
    factor_of = steps_of(rng, extent, pieces, -0.22, 0.18) if pieces else 1.0
    array = jax.random.normal(rng, extent, jnp.float32) * width * factor_of
    return jnp.minimum(jnp.maximum(array, -limit), limit).astype(kind)


def setup_inputs(seed: int = 0) -> dict:
    key_list = jax.random.split(jax.random.key(seed), 8)
    frames_in = normal_values(key_list[0], (UTTS, FRAMES, D), 1.0, 6.0, ((0, 8), (1, 4)))
    conv_kernel = normal_values(key_list[1], (KSIZE, D), KSIZE ** -0.5, 1.0)
    norm_gain = jnp.clip(1.0 + 0.18 * jax.random.normal(key_list[2], (D,), jnp.float32), 0.099609375, 1.8984375).astype(jnp.bfloat16)
    router = normal_values(key_list[3], (D, EXPERTS), D ** -0.5, 0.15625)
    w_in = normal_values(key_list[4], (EXPERTS, FF, D), D ** -0.5, 0.15625, ((0, 8), (1, 4)))
    w_out = normal_values(key_list[5], (EXPERTS, FF, D), FF ** -0.5, 0.109375, ((0, 8), (1, 4)))
    routes_keys = jax.random.split(jax.random.fold_in(key_list[6], 1), UTTS * FRAMES // TOK_DEV)
    routes_turns = jax.random.permutation(jax.random.fold_in(key_list[6], 3), UTTS * FRAMES // TOK_DEV)
    routes = jax.vmap(lambda own, number: shared_out(jax.random.fold_in(key_list[6], 2), own, number, TOK_DEV, EXPERTS, TOP, CAP, 2))(routes_keys, routes_turns).reshape((UTTS, FRAMES, TOP))
    return {"frames_in": frames_in, "conv_kernel": conv_kernel, "norm_gain": norm_gain, "router": router, "w_in": w_in, "w_out": w_out, "routes": routes}


def reference(frames_in, conv_kernel, norm_gain, router, w_in, w_out, routes):
    margin = (KSIZE - 1) // 2
    frames_f = frames_in.astype(jnp.float32)
    padded = jnp.pad(frames_f, ((0, 0), (margin, margin), (0, 0)))
    convolved = jnp.zeros_like(frames_f)
    for offset in range(KSIZE):
        convolved = convolved + conv_kernel[offset].astype(jnp.float32) * padded[:, offset:offset + FRAMES]
    residual = frames_f + jax.nn.silu(convolved)
    scale_rms = lax.rsqrt(lax.optimization_barrier(jnp.mean(residual * residual, axis=-1, keepdims=True)) + 1e-06)
    normed = (residual * scale_rms * norm_gain.astype(jnp.float32)).astype(jnp.bfloat16)
    logits = jnp.einsum('utd,de->ute', normed.astype(jnp.float32), router.astype(jnp.float32))
    onehot = (routes[..., None] == jnp.arange(EXPERTS, dtype=jnp.int32)).astype(jnp.float32)
    gating = jax.nn.sigmoid(lax.optimization_barrier(jnp.sum(onehot * logits[:, :, None, :], axis=-1)))
    pair_count = TOK_DEV * TOP
    block_hot = onehot.reshape(UTTS, N_DP, pair_count, EXPERTS)
    earlier = jnp.cumsum(block_hot, axis=2) - block_hot
    slot_float = lax.optimization_barrier(jnp.sum(earlier * block_hot, axis=-1))
    slot_of = slot_float.astype(jnp.int32)
    slot_hot = (slot_of[..., None] == jnp.arange(CAP, dtype=jnp.int32)).astype(jnp.float32)
    normed_rep = jnp.broadcast_to(normed[:, :, None, :], (UTTS, FRAMES, TOP, D)).reshape(UTTS, N_DP, pair_count, D).astype(jnp.float32)

    def one_expert(packed):
        expert_idx, first_w, second_w = packed
        column = (jnp.arange(EXPERTS, dtype=jnp.int32) == expert_idx).astype(jnp.float32)
        mine = lax.optimization_barrier(jnp.sum(block_hot * column, axis=-1))
        chooser = mine[..., None] * slot_hot
        normed_rows = jnp.einsum('uvrc,uvrd->uvcd', chooser, normed_rep).astype(jnp.bfloat16).reshape(-1, D)
        preact = jnp.dot(normed_rows, first_w.T, preferred_element_type=jnp.float32)
        hidden = jax.nn.silu(preact).astype(jnp.bfloat16)
        expert_out = jnp.dot(hidden, second_w, preferred_element_type=jnp.float32).astype(jnp.bfloat16)
        return expert_out.reshape(UTTS, N_DP, CAP, D)
    expert_outs = lax.map(one_expert, (jnp.arange(EXPERTS, dtype=jnp.int32), w_in, w_out))
    route_flat = routes.reshape(UTTS, N_DP, pair_count).astype(jnp.int32)
    utt_idx = jnp.arange(UTTS, dtype=jnp.int32)[:, None, None]
    dev_idx = jnp.arange(N_DP, dtype=jnp.int32)[None, :, None]
    picked = expert_outs[route_flat, utt_idx, dev_idx, slot_of]
    picked = picked.astype(jnp.float32).reshape(UTTS, FRAMES, TOP, D)
    combined = (residual + lax.optimization_barrier(jnp.sum(gating[..., None] * picked, axis=2))).astype(jnp.bfloat16)
    return combined
```

```python
import functools

import jax
import jax.numpy as jnp
from jax import lax
from jax.experimental import pallas as pl
from jax.experimental.pallas import tpu as pltpu
from jax.sharding import PartitionSpec as P


def swapped(value, axis, distance):
    mask = 2**distance
    pairs = [(source, source ^ mask) for source in range(lax.axis_size(axis))]
    return lax.ppermute(value, axis, pairs)


def extended(block, sides, width):
    for axis, dim in sides:
        count = lax.axis_size(axis)
        forward = [(i, i + 1) for i in range(count - 1)]
        backward = [(target, source) for source, target in forward]
        low = lax.ppermute(
            lax.slice_in_dim(block, block.shape[dim] - width, None, axis=dim), axis, forward
        )
        high = lax.ppermute(lax.slice_in_dim(block, 0, width, axis=dim), axis, backward)
        block = jnp.concatenate([low, block, high], axis=dim)
    return block


def expert_block(rows, first_w, second_w, row_bits, bit_count):
    place = lax.axis_index("dp")
    for bit in range(row_bits):
        other = swapped(rows, "dp", bit)
        upper = place >> bit & 1 == 1
        rows = jnp.concatenate(
            [jnp.where(upper, other, rows), jnp.where(upper, rows, other)], axis=0
        )
    stacked = jnp.stack([first_w, second_w])
    for bit in range(row_bits, bit_count):
        other = swapped(stacked, "dp", bit)
        stacked = jnp.concatenate([stacked, other], axis=1)
    preact = lax.dot_general(
        rows, stacked[0], (((1,), (1,)), ((), ())), preferred_element_type=jnp.float32
    )
    hidden = jax.nn.silu(preact).astype(jnp.bfloat16)
    partial_value = jnp.dot(hidden, stacked[1], preferred_element_type=jnp.float32)
    for bit in reversed(range(row_bits)):
        half_rows = partial_value.shape[0] // 2
        first_half = partial_value[:half_rows]
        second_half = partial_value[half_rows:]
        upper = place >> bit & 1 == 1
        outgoing = jnp.where(upper, first_half, second_half)
        kept = jnp.where(upper, second_half, first_half)
        partial_value = kept + swapped(outgoing.astype(jnp.bfloat16), "dp", bit).astype(
            outgoing.dtype
        )
    return partial_value


def shards(frames_in, conv_kernel, norm_gain, router, w_in, w_out, routes):
    tok_rows = frames_in.shape[1]
    features = frames_in.shape[2]
    kernel_len = conv_kernel.shape[0]
    margin = (kernel_len - 1) // 2
    padded = extended(frames_in, (("dp", 1),), margin)
    frames_f = frames_in[0].astype(jnp.float32)
    convolved = jnp.zeros((tok_rows, features), jnp.float32)
    for offset in range(kernel_len):
        convolved = convolved + conv_kernel[offset].astype(jnp.float32) * padded[
            0, offset : offset + tok_rows
        ].astype(jnp.float32)
    residual = frames_f + jax.nn.silu(convolved)
    scale_rms = lax.rsqrt(jnp.mean(residual * residual, axis=-1, keepdims=True) + 1e-06)
    normed = (residual * scale_rms * norm_gain.astype(jnp.float32)).astype(jnp.bfloat16)
    logits = jnp.dot(normed, router, preferred_element_type=jnp.float32)
    expert_count = router.shape[1]
    chosen = routes[0]
    top_k = chosen.shape[1]
    onehot = (chosen[:, :, None] == jnp.arange(expert_count, dtype=jnp.int32)).astype(jnp.float32)
    gating = jax.nn.sigmoid(jnp.sum(onehot * logits[:, None, :], axis=-1))
    pair_count = tok_rows * top_k
    flat_hot = onehot.reshape(pair_count, expert_count)
    positions = jnp.arange(pair_count, dtype=jnp.int32)
    earlier = (positions[:, None] > positions[None, :]).astype(jnp.float32)
    counts = jnp.dot(earlier, flat_hot, precision=lax.Precision.HIGHEST)
    slot_of = jnp.sum(counts * flat_hot, axis=-1).astype(jnp.int32)
    capacity = max(2, 9 * top_k * tok_rows // (8 * lax.axis_size("expert")))
    target = chosen.reshape(pair_count) * capacity + slot_of
    placing = (
        jnp.arange(expert_count * capacity, dtype=jnp.int32)[:, None] == target[None, :]
    ).astype(jnp.bfloat16)
    normed_rep = jnp.repeat(normed, top_k, axis=0)
    sent_normed = (
        jnp.dot(placing, normed_rep, preferred_element_type=jnp.float32)
        .astype(jnp.bfloat16)
        .reshape(expert_count, capacity, features)
    )
    received = lax.all_to_all(sent_normed, "expert", split_axis=0, concat_axis=0, tiled=True)
    slot_block = received.reshape(expert_count * capacity, features)
    bit_count = lax.axis_size("dp").bit_length() - 1
    row_bits = bit_count // 2
    summed = expert_block(slot_block, w_in[0], w_out[0], row_bits, bit_count)
    expert_out = summed.astype(jnp.bfloat16).reshape(expert_count, capacity, features)
    returned = lax.all_to_all(
        expert_out, "expert", split_axis=0, concat_axis=0, tiled=True
    ).reshape(expert_count * capacity, features)
    pulled_back = lax.dot_general(
        placing, returned, (((0,), (0,)), ((), ())), preferred_element_type=jnp.float32
    )
    pulled_back = pulled_back.reshape(tok_rows, top_k, features)
    combined = (residual + jnp.sum(gating[:, :, None] * pulled_back, axis=1)).astype(jnp.bfloat16)
    return combined[None]


COL = 256
LANE = 128
HALO = 16
BF = jnp.bfloat16
F32 = jnp.float32
MESH = pl.DeviceIdType.MESH


def silu(v):
    return v / (1.0 + jnp.exp(-v))


def moe_kernel(
    n_ex, n_dp, cap,
    x_ref, ck_ref, gain_ref, rout_ref, routes_ref, w_in_ref, w_out_ref,
    o_ref,
    xp, xf, res, info, place, gate, frames, rows_out, rows_in, acc, hid, part_out, part_in,
    comb_out, comb_in, w1, w2, logit,
    w1_sem, w2_sem, halo_s, halo_r, info_s, info_r, zs, zr, xs, xr, ys, yr, rs, rr,
):
    tok, width = x_ref.shape[1], x_ref.shape[2]
    ff = w_in_ref.shape[1]
    cols = width // COL
    ffb = ff // COL
    margin = (ck_ref.shape[0] - 1) // 2
    seg = n_dp * cap
    slots = n_ex * seg
    ex = lax.axis_index("expert")
    dp = lax.axis_index("dp")
    blk = slots // 4

    def dp_peer(d):
        return lax.rem(dp + d, n_dp)

    def ex_peer(d):
        return lax.rem(ex + d, n_ex)

    def rem_copy(src, dst, ssem, rsem, e, v):
        return pltpu.make_async_remote_copy(
            src_ref=src, dst_ref=dst, send_sem=ssem, recv_sem=rsem,
            device_id=(e, v), device_id_type=MESH,
        )

    barrier = pltpu.get_barrier_semaphore()
    for d in range(1, n_dp):
        pl.semaphore_signal(barrier, inc=1, device_id=(ex, dp_peer(d)), device_id_type=MESH)
    for d in range(1, n_ex):
        pl.semaphore_signal(barrier, inc=1, device_id=(ex_peer(d), dp), device_id_type=MESH)

    def w1_copy(k):
        return pltpu.make_async_copy(
            w_in_ref.at[0, :, pl.ds(k * COL, COL)], w1.at[k], w1_sem.at[k]
        )

    def w2_copy(k):
        return pltpu.make_async_copy(
            w_out_ref.at[0, :, pl.ds(k * COL, COL)], w2.at[k], w2_sem.at[k]
        )

    for k in range(cols):
        w1_copy(k).start()
        w2_copy(k).start()

    xp[HALO : HALO + tok, :] = x_ref[0]
    expert_of = lax.broadcasted_iota(jnp.int32, (n_ex, tok), 0)
    hot = [(expert_of == routes_ref[k : k + 1, :]).astype(F32) for k in range(2)]
    before = (
        lax.broadcasted_iota(jnp.int32, (tok, tok), 0)
        < lax.broadcasted_iota(jnp.int32, (tok, tok), 1)
    ).astype(BF)
    count = jnp.dot((hot[0] + hot[1]).astype(BF), before, preferred_element_type=F32)
    counts = [count, count + hot[0]]
    rows8 = lax.broadcasted_iota(jnp.int32, (8, tok), 0)
    targets = [
        routes_ref[k : k + 1, :].astype(F32) * seg
        + (dp * cap).astype(F32)
        + jnp.sum(counts[k] * hot[k], axis=0, keepdims=True)
        for k in range(2)
    ]
    info[0, dp] = jnp.where(rows8 == 0, targets[0], targets[1])

    pl.semaphore_wait(barrier, n_dp - 1 + n_ex - 1)

    def up_copy():
        return rem_copy(
            x_ref.at[0, pl.ds(tok - HALO, HALO)], xp.at[pl.ds(0, HALO)],
            halo_s.at[0], halo_r.at[0], ex, dp_peer(1),
        )

    def down_copy():
        return rem_copy(
            x_ref.at[0, pl.ds(0, HALO)], xp.at[pl.ds(HALO + tok, HALO)],
            halo_s.at[1], halo_r.at[1], ex, dp_peer(n_dp - 1),
        )

    @pl.when(dp < n_dp - 1)
    def _():
        up_copy().start()

    @pl.when(dp > 0)
    def _():
        down_copy().start()

    def info_copy(i, d, src):
        return rem_copy(
            info.at[i, src], info.at[i, src], info_s.at[i, d], info_r.at[i, d], ex, dp_peer(d)
        )

    for d in range(1, n_dp):
        info_copy(0, d, dp).start()

    @pl.when(dp == 0)
    def _():
        xp[0:HALO, :] = jnp.zeros((HALO, width), BF)

    @pl.when(dp == n_dp - 1)
    def _():
        xp[HALO + tok :, :] = jnp.zeros((HALO, width), BF)

    @pl.when(dp > 0)
    def _():
        up_copy().wait_recv()

    @pl.when(dp < n_dp - 1)
    def _():
        down_copy().wait_recv()

    def conv_step(c, total):
        at = pl.ds(pl.multiple_of(c * LANE, LANE), LANE)
        xf[...] = xp[:, at].astype(F32)
        taps = ck_ref[:, at].astype(F32)
        conv = jnp.zeros((tok, LANE), F32)
        for j in range(ck_ref.shape[0]):
            first = HALO - margin + j
            conv = conv + taps[j : j + 1, :] * xf[first : first + tok, :]
        value = xf[HALO : HALO + tok, :] + silu(conv)
        res[:, at] = value
        return total + jnp.sum(value * value, axis=1, keepdims=True)

    total = lax.fori_loop(0, width // LANE, conv_step, jnp.zeros((tok, 1), F32))
    scale = lax.rsqrt(total * (1.0 / width) + 1e-6)

    own = pl.ds(pl.multiple_of(dp * tok, tok), tok)

    def z_copy(k, d):
        return rem_copy(
            frames.at[k, own], frames.at[k, own], zs.at[k, d], zr.at[k, d], ex, dp_peer(d)
        )

    logit[...] = jnp.zeros_like(logit)

    def norm_step(k, carry):
        at = pl.ds(pl.multiple_of(k * COL, COL), COL)
        normed = (res[:, at] * scale * gain_ref[:, at].astype(F32)).astype(BF)
        frames[k, own] = normed
        for d in range(1, n_dp):
            z_copy(k, d).start()
        logit[...] += lax.dot_general(
            rout_ref[:, at], normed, (((1,), (1,)), ((), ())), preferred_element_type=F32
        )
        return carry

    lax.fori_loop(0, cols, norm_step, 0)
    gating = [
        1.0 / (1.0 + jnp.exp(-jnp.sum(hot[k] * logit[...], axis=0, keepdims=True)))
        for k in range(2)
    ]
    info[1, dp] = jnp.where(rows8 == 0, gating[0], gating[1])
    for d in range(1, n_dp):
        info_copy(1, d, dp).start()
    for d in range(1, n_dp):
        info_copy(0, d, dp).wait_recv()

    def place_step(b, carry):
        at = pl.ds(pl.multiple_of(b * blk, 16), blk)
        index = (lax.broadcasted_iota(jnp.int32, (blk, tok), 0) + b * blk).astype(F32)
        for v in range(n_dp):
            first, second = info[0, v, 0:1, :], info[0, v, 1:2, :]
            hits = jnp.where(index == first, 1.0, 0.0) + jnp.where(index == second, 1.0, 0.0)
            place[at, v * tok : (v + 1) * tok] = hits.astype(BF)
        return carry

    lax.fori_loop(0, 4, place_step, 0)

    mine_seg = pl.ds(pl.multiple_of(ex * seg, 16), seg)

    def seg_of(e):
        return pl.ds(pl.multiple_of(e * seg, 16), seg)

    def x_copy(k, d):
        return rem_copy(
            rows_out.at[k, seg_of(ex_peer(d))], rows_in.at[k, mine_seg],
            xs.at[k, d], xr.at[k, d], ex_peer(d), dp,
        )

    def y_copy(k, d):
        return rem_copy(
            part_out.at[k, seg_of(ex_peer(d))], part_in.at[k, mine_seg],
            ys.at[k, d], yr.at[k, d], ex_peer(d), dp,
        )

    for k in range(cols):
        w1_copy(k).wait()
    lag = 2

    def in_step(s, carry):
        @pl.when(s < cols)
        def _():
            for d in range(1, n_dp):
                z_copy(s, d).wait_recv()

            def rows_step(b, c2):
                at = pl.ds(pl.multiple_of(b * blk, 16), blk)
                rows_out[s, at] = jnp.dot(
                    place[at, :], frames[s], preferred_element_type=F32
                ).astype(BF)
                return c2

            lax.fori_loop(0, 4, rows_step, 0)
            for d in range(1, n_ex):
                x_copy(s, d).start()
            rows_in[s, mine_seg] = rows_out[s, mine_seg]

        @pl.when(s >= lag)
        def _():
            k = s - lag
            for d in range(1, n_ex):
                x_copy(k, d).wait_recv()

            def ff_step(n, c2):
                at = pl.ds(pl.multiple_of(n * COL, COL), COL)
                got = lax.dot_general(
                    rows_in[k], w1[k, at], (((1,), (1,)), ((), ())), preferred_element_type=F32
                )

                @pl.when(k == 0)
                def _():
                    acc[n] = got

                @pl.when(k > 0)
                def _():
                    acc[n] += got

                return c2

            lax.fori_loop(0, ffb, ff_step, 0)

        return carry

    lax.fori_loop(0, cols + lag, in_step, 0)

    def silu_step(b, carry):
        at = pl.ds(pl.multiple_of(b * blk, 16), blk)
        for n in range(ffb):
            hid[n, at] = silu(acc[n, at]).astype(BF)
        return carry

    lax.fori_loop(0, 4, silu_step, 0)

    for d in range(1, n_dp):
        info_copy(1, d, dp).wait_recv()
    eye = (
        lax.broadcasted_iota(jnp.int32, (tok, tok), 0)
        == lax.broadcasted_iota(jnp.int32, (tok, tok), 1)
    ).astype(F32)

    def gate_step(v, carry):
        turn = [
            lax.dot_general(
                eye, info[i, v], (((1,), (1,)), ((), ())),
                precision=lax.Precision.HIGHEST, preferred_element_type=F32,
            )
            for i in range(2)
        ]
        index = lax.broadcasted_iota(jnp.int32, (tok, slots), 1).astype(F32)
        gate[v] = (
            jnp.where(index == turn[0][:, 0:1], turn[1][:, 0:1], 0.0)
            + jnp.where(index == turn[0][:, 1:2], turn[1][:, 1:2], 0.0)
        ).astype(BF)
        return carry

    for k in range(cols):
        w2_copy(k).wait()

    def r_copy(k, d):
        return rem_copy(
            comb_out.at[k, dp_peer(d)], comb_in.at[k, dp], rs.at[k, d], rr.at[k, d],
            ex, dp_peer(d),
        )

    def out_step(s, carry):
        @pl.when(s < cols)
        def _():
            def rows_step(b, c2):
                at = pl.ds(pl.multiple_of(b * blk, 16), blk)
                value = jnp.dot(hid[0, at], w2[s, 0:COL], preferred_element_type=F32)
                for n in range(1, ffb):
                    value = value + jnp.dot(
                        hid[n, at], w2[s, n * COL : (n + 1) * COL], preferred_element_type=F32
                    )
                part_out[s, at] = value.astype(BF)
                return c2

            lax.fori_loop(0, 4, rows_step, 0)
            for d in range(1, n_ex):
                y_copy(s, d).start()
            part_in[s, mine_seg] = part_out[s, mine_seg]

        @pl.when(s == lag - 1)
        def _():
            lax.fori_loop(0, n_dp, gate_step, 0)

        @pl.when(s >= lag)
        def _():
            k = s - lag
            at = pl.ds(pl.multiple_of(k * COL, COL), COL)
            for d in range(1, n_ex):
                y_copy(k, d).wait_recv()

            def comb_step(v, c2):
                value = jnp.dot(gate[v], part_in[k], preferred_element_type=F32)

                @pl.when(v == dp)
                def _():
                    res[:, at] += value

                @pl.when(v != dp)
                def _():
                    comb_out[k, v] = value.astype(BF)

                return c2

            lax.fori_loop(0, n_dp, comb_step, 0)
            for d in range(1, n_dp):
                r_copy(k, d).start()

        return carry

    lax.fori_loop(0, cols + lag, out_step, 0)

    def final_step(k, carry):
        at = pl.ds(pl.multiple_of(k * COL, COL), COL)
        value = res[:, at]
        for d in range(1, n_dp):
            r_copy(k, d).wait_recv()
        for d in range(1, n_dp):
            value = value + comb_in[k, dp_peer(d)].astype(F32)
        o_ref[0, :, at] = value.astype(BF)
        for d in range(1, n_dp):
            z_copy(k, d).wait_send()
            r_copy(k, d).wait_send()
        for d in range(1, n_ex):
            x_copy(k, d).wait_send()
            y_copy(k, d).wait_send()
        return carry

    lax.fori_loop(0, cols, final_step, 0)
    for d in range(1, n_dp):
        info_copy(0, d, dp).wait_send()
        info_copy(1, d, dp).wait_send()

    @pl.when(dp < n_dp - 1)
    def _():
        up_copy().wait_send()

    @pl.when(dp > 0)
    def _():
        down_copy().wait_send()


def kernel_shards(n_ex, n_dp, cap, frames_in, conv_kernel, norm_gain, router, w_in, w_out, routes):
    tok, width = frames_in.shape[1], frames_in.shape[2]
    ff = w_in.shape[1]
    cols, ffb = width // COL, ff // COL
    slots = n_ex * n_dp * cap
    dma = pltpu.SemaphoreType.DMA
    vmem = pl.BlockSpec(memory_space=pltpu.VMEM)
    hbm = pl.BlockSpec(memory_space=pl.ANY)
    return pl.pallas_call(
        functools.partial(moe_kernel, n_ex, n_dp, cap),
        out_shape=jax.ShapeDtypeStruct(frames_in.shape, BF),
        in_specs=[vmem] * 5 + [hbm] * 2,
        out_specs=vmem,
        scratch_shapes=[
            pltpu.VMEM((tok + 2 * HALO, width), BF),
            pltpu.VMEM((tok + 2 * HALO, LANE), F32),
            pltpu.VMEM((tok, width), F32),
            pltpu.VMEM((2, n_dp, 8, tok), F32),
            pltpu.VMEM((slots, n_dp * tok), BF),
            pltpu.VMEM((n_dp, tok, slots), BF),
            pltpu.VMEM((cols, n_dp * tok, COL), BF),
            pltpu.VMEM((cols, slots, COL), BF),
            pltpu.VMEM((cols, slots, COL), BF),
            pltpu.VMEM((ffb, slots, COL), F32),
            pltpu.VMEM((ffb, slots, COL), BF),
            pltpu.VMEM((cols, slots, COL), BF),
            pltpu.VMEM((cols, slots, COL), BF),
            pltpu.VMEM((cols, n_dp, tok, COL), BF),
            pltpu.VMEM((cols, n_dp, tok, COL), BF),
            pltpu.VMEM((cols, ff, COL), BF),
            pltpu.VMEM((cols, ff, COL), BF),
            pltpu.VMEM((n_ex, tok), F32),
            dma((cols,)), dma((cols,)),
            dma((2,)), dma((2,)),
            dma((2, n_dp)), dma((2, n_dp)),
            dma((cols, n_dp)), dma((cols, n_dp)),
            dma((cols, n_ex)), dma((cols, n_ex)),
            dma((cols, n_ex)), dma((cols, n_ex)),
            dma((cols, n_dp)), dma((cols, n_dp)),
        ],
        compiler_params=pltpu.CompilerParams(
            collective_id=0, has_side_effects=True, vmem_limit_bytes=56 * 2**20
        ),
    )(frames_in, conv_kernel, norm_gain[None], router.T, routes[0].T, w_in, w_out)


def kernel_fits(n_ex, n_dp, cap, tok, width, ff, top_k, kernel_len):
    seg = n_dp * cap
    return (
        n_ex == 8 and n_dp > 1 and top_k == 2 and tok % LANE == 0 and width % COL == 0
        and ff % COL == 0 and seg % 16 == 0 and (n_ex * seg) % 64 == 0
        and kernel_len <= 2 * HALO and kernel_len % 2 == 1
        and 8 * n_ex * seg * (width + ff) + 4 * ff * width < 40 * 2**20
    )


def body(mesh, *args):
    frames_in, conv_kernel, w_in, routes = args[0], args[1], args[4], args[6]
    n_ex, n_dp = mesh.shape["expert"], mesh.shape["dp"]
    tok, width, top_k = frames_in.shape[1], frames_in.shape[2], routes.shape[2]
    cap = max(2, 9 * top_k * tok // (8 * n_ex))
    if kernel_fits(n_ex, n_dp, cap, tok, width, w_in.shape[1], top_k, conv_kernel.shape[0]):
        return kernel_shards(n_ex, n_dp, cap, *args)
    return shards(*args)


def solution(mesh):
    return jax.shard_map(
        functools.partial(body, mesh),
        mesh=mesh,
        in_specs=(
            P("expert", "dp", None),
            P(),
            P(),
            P(),
            P("expert", "dp", None),
            P("expert", "dp", None),
            P("expert", "dp", None),
        ),
        out_specs=P("expert", "dp", None),
        check_vma=False,
    )
```

```python
import functools

import jax
import jax.numpy as jnp
from jax import lax
from jax.experimental import pallas as pl
from jax.experimental.pallas import tpu as pltpu
from jax.sharding import PartitionSpec as P


def swapped(value, axis, distance):
    mask = 2**distance
    pairs = [(source, source ^ mask) for source in range(lax.axis_size(axis))]
    return lax.ppermute(value, axis, pairs)


def extended(block, sides, width):
    for axis, dim in sides:
        count = lax.axis_size(axis)
        forward = [(i, i + 1) for i in range(count - 1)]
        backward = [(target, source) for source, target in forward]
        low = lax.ppermute(
            lax.slice_in_dim(block, block.shape[dim] - width, None, axis=dim), axis, forward
        )
        high = lax.ppermute(lax.slice_in_dim(block, 0, width, axis=dim), axis, backward)
        block = jnp.concatenate([low, block, high], axis=dim)
    return block


def expert_block(rows, first_w, second_w, row_bits, bit_count):
    place = lax.axis_index("dp")
    for bit in range(row_bits):
        other = swapped(rows, "dp", bit)
        upper = place >> bit & 1 == 1
        rows = jnp.concatenate(
            [jnp.where(upper, other, rows), jnp.where(upper, rows, other)], axis=0
        )
    stacked = jnp.stack([first_w, second_w])
    for bit in range(row_bits, bit_count):
        other = swapped(stacked, "dp", bit)
        stacked = jnp.concatenate([stacked, other], axis=1)
    preact = lax.dot_general(
        rows, stacked[0], (((1,), (1,)), ((), ())), preferred_element_type=jnp.float32
    )
    hidden = jax.nn.silu(preact).astype(jnp.bfloat16)
    partial_value = jnp.dot(hidden, stacked[1], preferred_element_type=jnp.float32)
    for bit in reversed(range(row_bits)):
        half_rows = partial_value.shape[0] // 2
        first_half = partial_value[:half_rows]
        second_half = partial_value[half_rows:]
        upper = place >> bit & 1 == 1
        outgoing = jnp.where(upper, first_half, second_half)
        kept = jnp.where(upper, second_half, first_half)
        partial_value = kept + swapped(outgoing.astype(jnp.bfloat16), "dp", bit).astype(
            outgoing.dtype
        )
    return partial_value


def shards(frames_in, conv_kernel, norm_gain, router, w_in, w_out, routes):
    tok_rows = frames_in.shape[1]
    features = frames_in.shape[2]
    kernel_len = conv_kernel.shape[0]
    margin = (kernel_len - 1) // 2
    padded = extended(frames_in, (("dp", 1),), margin)
    frames_f = frames_in[0].astype(jnp.float32)
    convolved = jnp.zeros((tok_rows, features), jnp.float32)
    for offset in range(kernel_len):
        convolved = convolved + conv_kernel[offset].astype(jnp.float32) * padded[
            0, offset : offset + tok_rows
        ].astype(jnp.float32)
    residual = frames_f + jax.nn.silu(convolved)
    scale_rms = lax.rsqrt(jnp.mean(residual * residual, axis=-1, keepdims=True) + 1e-06)
    normed = (residual * scale_rms * norm_gain.astype(jnp.float32)).astype(jnp.bfloat16)
    logits = jnp.dot(normed, router, preferred_element_type=jnp.float32)
    expert_count = router.shape[1]
    chosen = routes[0]
    top_k = chosen.shape[1]
    onehot = (chosen[:, :, None] == jnp.arange(expert_count, dtype=jnp.int32)).astype(jnp.float32)
    gating = jax.nn.sigmoid(jnp.sum(onehot * logits[:, None, :], axis=-1))
    pair_count = tok_rows * top_k
    flat_hot = onehot.reshape(pair_count, expert_count)
    positions = jnp.arange(pair_count, dtype=jnp.int32)
    earlier = (positions[:, None] > positions[None, :]).astype(jnp.float32)
    counts = jnp.dot(earlier, flat_hot, precision=lax.Precision.HIGHEST)
    slot_of = jnp.sum(counts * flat_hot, axis=-1).astype(jnp.int32)
    capacity = max(2, 9 * top_k * tok_rows // (8 * lax.axis_size("expert")))
    target = chosen.reshape(pair_count) * capacity + slot_of
    placing = (
        jnp.arange(expert_count * capacity, dtype=jnp.int32)[:, None] == target[None, :]
    ).astype(jnp.bfloat16)
    normed_rep = jnp.repeat(normed, top_k, axis=0)
    sent_normed = (
        jnp.dot(placing, normed_rep, preferred_element_type=jnp.float32)
        .astype(jnp.bfloat16)
        .reshape(expert_count, capacity, features)
    )
    received = lax.all_to_all(sent_normed, "expert", split_axis=0, concat_axis=0, tiled=True)
    slot_block = received.reshape(expert_count * capacity, features)
    bit_count = lax.axis_size("dp").bit_length() - 1
    row_bits = bit_count // 2
    summed = expert_block(slot_block, w_in[0], w_out[0], row_bits, bit_count)
    expert_out = summed.astype(jnp.bfloat16).reshape(expert_count, capacity, features)
    returned = lax.all_to_all(
        expert_out, "expert", split_axis=0, concat_axis=0, tiled=True
    ).reshape(expert_count * capacity, features)
    pulled_back = lax.dot_general(
        placing, returned, (((0,), (0,)), ((), ())), preferred_element_type=jnp.float32
    )
    pulled_back = pulled_back.reshape(tok_rows, top_k, features)
    combined = (residual + jnp.sum(gating[:, :, None] * pulled_back, axis=1)).astype(jnp.bfloat16)
    return combined[None]


COL = 256
FFB = 256
LANE = 128
HALO = 16
BF = jnp.bfloat16
F32 = jnp.float32
MESH = pl.DeviceIdType.MESH


def silu(v):
    half = 0.5 * v
    return half + half * jnp.tanh(half)


def moe_kernel(
    n_ex, n_dp, cap,
    x_ref, ck_ref, gain_ref, rout_ref, routes_ref, w_in_ref, w_out_ref,
    o_ref,
    xp, xf, res, info, place, gate, frames, rows_out, rows_in, acc, hid, part_out, part_in,
    comb_out, comb_in, w1, w2, logit,
    w1_sem, w2_sem, halo_s, halo_r, info_s, info_r, zs, zr, xs, xr, ys, yr, rs, rr,
):
    tok, width = x_ref.shape[1], x_ref.shape[2]
    ff = w_in_ref.shape[1]
    cols = width // COL
    ffb = ff // FFB
    taps_count = ck_ref.shape[0]
    margin = (taps_count - 1) // 2
    seg = n_dp * cap
    slots = n_ex * seg
    ex = lax.axis_index("expert")
    dp = lax.axis_index("dp")
    blk = slots // 4

    def dp_peer(d):
        return lax.rem(dp + d, n_dp)

    def ex_peer(d):
        return lax.rem(ex + d, n_ex)

    def rem_copy(src, dst, ssem, rsem, e, v):
        return pltpu.make_async_remote_copy(
            src_ref=src, dst_ref=dst, send_sem=ssem, recv_sem=rsem,
            device_id=(e, v), device_id_type=MESH,
        )

    barrier = pltpu.get_barrier_semaphore()
    for d in range(1, n_dp):
        pl.semaphore_signal(barrier, inc=1, device_id=(ex, dp_peer(d)), device_id_type=MESH)
    for d in range(1, n_ex):
        pl.semaphore_signal(barrier, inc=1, device_id=(ex_peer(d), dp), device_id_type=MESH)

    def w1_copy(k):
        return pltpu.make_async_copy(
            w_in_ref.at[0, :, pl.ds(k * COL, COL)], w1.at[k], w1_sem.at[k]
        )

    def w2_copy(k):
        return pltpu.make_async_copy(
            w_out_ref.at[0, :, pl.ds(k * COL, COL)], w2.at[k], w2_sem.at[k]
        )

    for k in range(cols):
        w1_copy(k).start()
        w2_copy(k).start()

    xp[HALO : HALO + tok, :] = x_ref[0]
    expert_of = lax.broadcasted_iota(jnp.int32, (n_ex, tok), 0)
    hot = [(expert_of == routes_ref[k : k + 1, :]).astype(F32) for k in range(2)]
    before = (
        lax.broadcasted_iota(jnp.int32, (tok, tok), 0)
        < lax.broadcasted_iota(jnp.int32, (tok, tok), 1)
    ).astype(BF)
    count = jnp.dot((hot[0] + hot[1]).astype(BF), before, preferred_element_type=F32)
    counts = [count, count + hot[0]]
    rows8 = lax.broadcasted_iota(jnp.int32, (8, tok), 0)
    targets = [
        routes_ref[k : k + 1, :].astype(F32) * seg
        + (dp * cap).astype(F32)
        + jnp.sum(counts[k] * hot[k], axis=0, keepdims=True)
        for k in range(2)
    ]
    info[0, dp] = jnp.where(rows8 == 0, targets[0], targets[1])

    def conv_rows(first, count):
        def step(c, carry):
            at = pl.ds(pl.multiple_of(c * LANE, LANE), LANE)
            span = count + 2 * HALO
            xf[0:span, :] = xp[first : first + span, at].astype(F32)
            taps = ck_ref[:, at].astype(F32)
            conv = jnp.zeros((count, LANE), F32)
            for r in range(8):
                begin = HALO - margin + r
                size = min(count + 24, span - begin)
                shifted = xf[begin : begin + size, :]
                for j in range(r, taps_count, 8):
                    conv = conv + taps[j : j + 1, :] * shifted[j - r : j - r + count, :]
            res[first : first + count, at] = xf[HALO : HALO + count, :] + silu(conv)
            return carry

        lax.fori_loop(0, width // LANE, step, 0)

    conv_rows(HALO, tok - 2 * HALO)

    pl.semaphore_wait(barrier, n_dp - 1 + n_ex - 1)

    def up_copy():
        return rem_copy(
            x_ref.at[0, pl.ds(tok - HALO, HALO)], xp.at[pl.ds(0, HALO)],
            halo_s.at[0], halo_r.at[0], ex, dp_peer(1),
        )

    def down_copy():
        return rem_copy(
            x_ref.at[0, pl.ds(0, HALO)], xp.at[pl.ds(HALO + tok, HALO)],
            halo_s.at[1], halo_r.at[1], ex, dp_peer(n_dp - 1),
        )

    @pl.when(dp < n_dp - 1)
    def _():
        up_copy().start()

    @pl.when(dp > 0)
    def _():
        down_copy().start()

    def info_copy(i, d, src):
        return rem_copy(
            info.at[i, src], info.at[i, src], info_s.at[i, d], info_r.at[i, d], ex, dp_peer(d)
        )

    for d in range(1, n_dp):
        info_copy(0, d, dp).start()

    @pl.when(dp == 0)
    def _():
        xp[0:HALO, :] = jnp.zeros((HALO, width), BF)

    @pl.when(dp == n_dp - 1)
    def _():
        xp[HALO + tok :, :] = jnp.zeros((HALO, width), BF)

    @pl.when(dp > 0)
    def _():
        up_copy().wait_recv()

    @pl.when(dp < n_dp - 1)
    def _():
        down_copy().wait_recv()

    conv_rows(0, HALO)
    conv_rows(tok - HALO, HALO)

    def square_step(k, total):
        at = pl.ds(pl.multiple_of(k * COL, COL), COL)
        return total + jnp.sum(res[:, at] * res[:, at], axis=1, keepdims=True)

    total = lax.fori_loop(0, cols, square_step, jnp.zeros((tok, 1), F32))
    scale = lax.rsqrt(total * (1.0 / width) + 1e-6)

    own = pl.ds(pl.multiple_of(dp * tok, tok), tok)

    def z_copy(k, d):
        return rem_copy(
            frames.at[k, own], frames.at[k, own], zs.at[k, d], zr.at[k, d], ex, dp_peer(d)
        )

    logit[...] = jnp.zeros_like(logit)
    ahead = 2

    def norm_step(k, carry):
        at = pl.ds(pl.multiple_of(k * COL, COL), COL)
        normed = (res[:, at] * scale * gain_ref[:, at].astype(F32)).astype(BF)
        frames[k, own] = normed

        @pl.when(k < ahead)
        def _():
            for d in range(1, n_dp):
                z_copy(k, d).start()

        logit[...] += lax.dot_general(
            rout_ref[:, at], normed, (((1,), (1,)), ((), ())), preferred_element_type=F32
        )
        return carry

    lax.fori_loop(0, cols, norm_step, 0)
    gating = [
        1.0 / (1.0 + jnp.exp(-jnp.sum(hot[k] * logit[...], axis=0, keepdims=True)))
        for k in range(2)
    ]
    info[1, dp] = jnp.where(rows8 == 0, gating[0], gating[1])
    for d in range(1, n_dp):
        info_copy(1, d, dp).start()
    for d in range(1, n_dp):
        info_copy(0, d, dp).wait_recv()

    def place_step(b, carry):
        at = pl.ds(pl.multiple_of(b * blk, 16), blk)
        index = (lax.broadcasted_iota(jnp.int32, (blk, tok), 0) + b * blk).astype(F32)
        for v in range(n_dp):
            first, second = info[0, v, 0:1, :], info[0, v, 1:2, :]
            hits = jnp.where(index == first, 1.0, 0.0) + jnp.where(index == second, 1.0, 0.0)
            place[at, v * tok : (v + 1) * tok] = hits.astype(BF)
        return carry

    lax.fori_loop(0, 4, place_step, 0)

    mine_seg = pl.ds(pl.multiple_of(ex * seg, 16), seg)

    def seg_of(e):
        return pl.ds(pl.multiple_of(e * seg, 16), seg)

    def x_copy(k, d):
        return rem_copy(
            rows_out.at[k, seg_of(ex_peer(d))], rows_in.at[k, mine_seg],
            xs.at[k, d], xr.at[k, d], ex_peer(d), dp,
        )

    def y_copy(k, d):
        return rem_copy(
            part_out.at[k, seg_of(ex_peer(d))], part_in.at[k, mine_seg],
            ys.at[k, d], yr.at[k, d], ex_peer(d), dp,
        )

    for k in range(cols):
        w1_copy(k).wait()
    lag = 2

    def in_step(s, carry):
        @pl.when(s < cols)
        def _():
            for d in range(1, n_dp):
                z_copy(s, d).wait_recv()

            @pl.when(s < cols - ahead)
            def _():
                for d in range(1, n_dp):
                    z_copy(s + ahead, d).start()

            def rows_step(b, c2):
                at = pl.ds(pl.multiple_of(b * blk, 16), blk)
                rows_out[s, at] = jnp.dot(
                    place[at, :], frames[s], preferred_element_type=F32
                ).astype(BF)
                return c2

            lax.fori_loop(0, 4, rows_step, 0)
            for d in range(1, n_ex):
                x_copy(s, d).start()
            rows_in[s, mine_seg] = rows_out[s, mine_seg]

        @pl.when(s >= lag)
        def _():
            k = s - lag
            for d in range(1, n_ex):
                x_copy(k, d).wait_recv()

            def ff_step(n, c2):
                at = pl.ds(pl.multiple_of(n * FFB, FFB), FFB)
                got = lax.dot_general(
                    rows_in[k], w1[k, at], (((1,), (1,)), ((), ())), preferred_element_type=F32
                )

                @pl.when(k == 0)
                def _():
                    acc[n] = got

                @pl.when(k > 0)
                def _():
                    acc[n] += got

                return c2

            lax.fori_loop(0, ffb, ff_step, 0)

        return carry

    lax.fori_loop(0, cols + lag, in_step, 0)

    def silu_step(b, carry):
        at = pl.ds(pl.multiple_of(b * blk, 16), blk)
        for n in range(ffb):
            hid[n, at] = silu(acc[n, at]).astype(BF)
        return carry

    lax.fori_loop(0, 4, silu_step, 0)

    for d in range(1, n_dp):
        info_copy(1, d, dp).wait_recv()
    eye = (
        lax.broadcasted_iota(jnp.int32, (tok, tok), 0)
        == lax.broadcasted_iota(jnp.int32, (tok, tok), 1)
    ).astype(F32)

    def gate_step(v, carry):
        turn = [
            lax.dot_general(
                eye, info[i, v], (((1,), (1,)), ((), ())),
                precision=lax.Precision.HIGHEST, preferred_element_type=F32,
            )
            for i in range(2)
        ]
        index = lax.broadcasted_iota(jnp.int32, (tok, slots), 1).astype(F32)
        gate[v] = (
            jnp.where(index == turn[0][:, 0:1], turn[1][:, 0:1], 0.0)
            + jnp.where(index == turn[0][:, 1:2], turn[1][:, 1:2], 0.0)
        ).astype(BF)
        return carry

    for k in range(cols):
        w2_copy(k).wait()

    def r_copy(k, d):
        return rem_copy(
            comb_out.at[k, dp_peer(d)], comb_in.at[k, dp], rs.at[k, d], rr.at[k, d],
            ex, dp_peer(d),
        )

    def out_step(s, carry):
        @pl.when(s < cols)
        def _():
            def rows_step(b, c2):
                at = pl.ds(pl.multiple_of(b * blk, 16), blk)
                value = jnp.dot(hid[0, at], w2[s, 0:FFB], preferred_element_type=F32)
                for n in range(1, ffb):
                    value = value + jnp.dot(
                        hid[n, at], w2[s, n * FFB : (n + 1) * FFB], preferred_element_type=F32
                    )
                part_out[s, at] = value.astype(BF)
                return c2

            lax.fori_loop(0, 4, rows_step, 0)
            for d in range(1, n_ex):
                y_copy(s, d).start()
            part_in[s, mine_seg] = part_out[s, mine_seg]

        @pl.when(s == lag - 1)
        def _():
            lax.fori_loop(0, n_dp, gate_step, 0)

        @pl.when(s >= lag)
        def _():
            k = s - lag
            at = pl.ds(pl.multiple_of(k * COL, COL), COL)
            for d in range(1, n_ex):
                y_copy(k, d).wait_recv()

            def comb_step(v, c2):
                value = jnp.dot(gate[v], part_in[k], preferred_element_type=F32)

                @pl.when(v == dp)
                def _():
                    res[:, at] += value

                @pl.when(v != dp)
                def _():
                    comb_out[k, v] = value.astype(BF)

                return c2

            lax.fori_loop(0, n_dp, comb_step, 0)
            for d in range(1, n_dp):
                r_copy(k, d).start()

        return carry

    lax.fori_loop(0, cols + lag, out_step, 0)

    def final_step(k, carry):
        at = pl.ds(pl.multiple_of(k * COL, COL), COL)
        value = res[:, at]
        for d in range(1, n_dp):
            r_copy(k, d).wait_recv()
        for d in range(1, n_dp):
            value = value + comb_in[k, dp_peer(d)].astype(F32)
        o_ref[0, :, at] = value.astype(BF)
        for d in range(1, n_dp):
            z_copy(k, d).wait_send()
            r_copy(k, d).wait_send()
        for d in range(1, n_ex):
            x_copy(k, d).wait_send()
            y_copy(k, d).wait_send()
        return carry

    lax.fori_loop(0, cols, final_step, 0)
    for d in range(1, n_dp):
        info_copy(0, d, dp).wait_send()
        info_copy(1, d, dp).wait_send()

    @pl.when(dp < n_dp - 1)
    def _():
        up_copy().wait_send()

    @pl.when(dp > 0)
    def _():
        down_copy().wait_send()


def kernel_shards(n_ex, n_dp, cap, frames_in, conv_kernel, norm_gain, router, w_in, w_out, routes):
    tok, width = frames_in.shape[1], frames_in.shape[2]
    ff = w_in.shape[1]
    cols, ffb = width // COL, ff // FFB
    slots = n_ex * n_dp * cap
    dma = pltpu.SemaphoreType.DMA
    vmem = pl.BlockSpec(memory_space=pltpu.VMEM)
    hbm = pl.BlockSpec(memory_space=pl.ANY)
    return pl.pallas_call(
        functools.partial(moe_kernel, n_ex, n_dp, cap),
        out_shape=jax.ShapeDtypeStruct(frames_in.shape, BF),
        in_specs=[vmem] * 5 + [hbm] * 2,
        out_specs=vmem,
        scratch_shapes=[
            pltpu.VMEM((tok + 2 * HALO, width), BF),
            pltpu.VMEM((tok + 2 * HALO, LANE), F32),
            pltpu.VMEM((tok, width), F32),
            pltpu.VMEM((2, n_dp, 8, tok), F32),
            pltpu.VMEM((slots, n_dp * tok), BF),
            pltpu.VMEM((n_dp, tok, slots), BF),
            pltpu.VMEM((cols, n_dp * tok, COL), BF),
            pltpu.VMEM((cols, slots, COL), BF),
            pltpu.VMEM((cols, slots, COL), BF),
            pltpu.VMEM((ffb, slots, FFB), F32),
            pltpu.VMEM((ffb, slots, FFB), BF),
            pltpu.VMEM((cols, slots, COL), BF),
            pltpu.VMEM((cols, slots, COL), BF),
            pltpu.VMEM((cols, n_dp, tok, COL), BF),
            pltpu.VMEM((cols, n_dp, tok, COL), BF),
            pltpu.VMEM((cols, ff, COL), BF),
            pltpu.VMEM((cols, ff, COL), BF),
            pltpu.VMEM((n_ex, tok), F32),
            dma((cols,)), dma((cols,)),
            dma((2,)), dma((2,)),
            dma((2, n_dp)), dma((2, n_dp)),
            dma((cols, n_dp)), dma((cols, n_dp)),
            dma((cols, n_ex)), dma((cols, n_ex)),
            dma((cols, n_ex)), dma((cols, n_ex)),
            dma((cols, n_dp)), dma((cols, n_dp)),
        ],
        compiler_params=pltpu.CompilerParams(
            collective_id=0, has_side_effects=True, vmem_limit_bytes=56 * 2**20
        ),
    )(frames_in, conv_kernel, norm_gain[None], router.T, routes[0].T, w_in, w_out)


def kernel_fits(n_ex, n_dp, cap, tok, width, ff, top_k, kernel_len):
    seg = n_dp * cap
    return (
        n_ex == 8 and n_dp > 1 and top_k == 2 and tok % LANE == 0 and width % COL == 0
        and ff % FFB == 0 and seg % 16 == 0 and (n_ex * seg) % 64 == 0
        and kernel_len < 2 * HALO and kernel_len % 2 == 1
        and 8 * n_ex * seg * (width + ff) + 4 * ff * width < 40 * 2**20
    )


def body(mesh, *args):
    frames_in, conv_kernel, w_in, routes = args[0], args[1], args[4], args[6]
    n_ex, n_dp = mesh.shape["expert"], mesh.shape["dp"]
    tok, width, top_k = frames_in.shape[1], frames_in.shape[2], routes.shape[2]
    cap = max(2, 9 * top_k * tok // (8 * n_ex))
    if kernel_fits(n_ex, n_dp, cap, tok, width, w_in.shape[1], top_k, conv_kernel.shape[0]):
        return kernel_shards(n_ex, n_dp, cap, *args)
    return shards(*args)


def solution(mesh):
    return jax.shard_map(
        functools.partial(body, mesh),
        mesh=mesh,
        in_specs=(
            P("expert", "dp", None),
            P(),
            P(),
            P(),
            P("expert", "dp", None),
            P("expert", "dp", None),
            P("expert", "dp", None),
        ),
        out_specs=P("expert", "dp", None),
        check_vma=False,
    )
```

```python
import functools

import jax
import jax.numpy as jnp
from jax import lax
from jax.experimental import pallas as pl
from jax.experimental.pallas import tpu as pltpu
from jax.sharding import PartitionSpec as P


def swapped(value, axis, distance):
    mask = 2**distance
    pairs = [(source, source ^ mask) for source in range(lax.axis_size(axis))]
    return lax.ppermute(value, axis, pairs)


def extended(block, sides, width):
    for axis, dim in sides:
        count = lax.axis_size(axis)
        forward = [(i, i + 1) for i in range(count - 1)]
        backward = [(target, source) for source, target in forward]
        low = lax.ppermute(
            lax.slice_in_dim(block, block.shape[dim] - width, None, axis=dim), axis, forward
        )
        high = lax.ppermute(lax.slice_in_dim(block, 0, width, axis=dim), axis, backward)
        block = jnp.concatenate([low, block, high], axis=dim)
    return block


def expert_block(rows, first_w, second_w, row_bits, bit_count):
    place = lax.axis_index("dp")
    for bit in range(row_bits):
        other = swapped(rows, "dp", bit)
        upper = place >> bit & 1 == 1
        rows = jnp.concatenate(
            [jnp.where(upper, other, rows), jnp.where(upper, rows, other)], axis=0
        )
    stacked = jnp.stack([first_w, second_w])
    for bit in range(row_bits, bit_count):
        other = swapped(stacked, "dp", bit)
        stacked = jnp.concatenate([stacked, other], axis=1)
    preact = lax.dot_general(
        rows, stacked[0], (((1,), (1,)), ((), ())), preferred_element_type=jnp.float32
    )
    hidden = jax.nn.silu(preact).astype(jnp.bfloat16)
    partial_value = jnp.dot(hidden, stacked[1], preferred_element_type=jnp.float32)
    for bit in reversed(range(row_bits)):
        half_rows = partial_value.shape[0] // 2
        first_half = partial_value[:half_rows]
        second_half = partial_value[half_rows:]
        upper = place >> bit & 1 == 1
        outgoing = jnp.where(upper, first_half, second_half)
        kept = jnp.where(upper, second_half, first_half)
        partial_value = kept + swapped(outgoing.astype(jnp.bfloat16), "dp", bit).astype(
            outgoing.dtype
        )
    return partial_value


def shards(frames_in, conv_kernel, norm_gain, router, w_in, w_out, routes):
    tok_rows = frames_in.shape[1]
    features = frames_in.shape[2]
    kernel_len = conv_kernel.shape[0]
    margin = (kernel_len - 1) // 2
    padded = extended(frames_in, (("dp", 1),), margin)
    frames_f = frames_in[0].astype(jnp.float32)
    convolved = jnp.zeros((tok_rows, features), jnp.float32)
    for offset in range(kernel_len):
        convolved = convolved + conv_kernel[offset].astype(jnp.float32) * padded[
            0, offset : offset + tok_rows
        ].astype(jnp.float32)
    residual = frames_f + jax.nn.silu(convolved)
    scale_rms = lax.rsqrt(jnp.mean(residual * residual, axis=-1, keepdims=True) + 1e-06)
    normed = (residual * scale_rms * norm_gain.astype(jnp.float32)).astype(jnp.bfloat16)
    logits = jnp.dot(normed, router, preferred_element_type=jnp.float32)
    expert_count = router.shape[1]
    chosen = routes[0]
    top_k = chosen.shape[1]
    onehot = (chosen[:, :, None] == jnp.arange(expert_count, dtype=jnp.int32)).astype(jnp.float32)
    gating = jax.nn.sigmoid(jnp.sum(onehot * logits[:, None, :], axis=-1))
    pair_count = tok_rows * top_k
    flat_hot = onehot.reshape(pair_count, expert_count)
    positions = jnp.arange(pair_count, dtype=jnp.int32)
    earlier = (positions[:, None] > positions[None, :]).astype(jnp.float32)
    counts = jnp.dot(earlier, flat_hot, precision=lax.Precision.HIGHEST)
    slot_of = jnp.sum(counts * flat_hot, axis=-1).astype(jnp.int32)
    capacity = max(2, 9 * top_k * tok_rows // (8 * lax.axis_size("expert")))
    target = chosen.reshape(pair_count) * capacity + slot_of
    placing = (
        jnp.arange(expert_count * capacity, dtype=jnp.int32)[:, None] == target[None, :]
    ).astype(jnp.bfloat16)
    normed_rep = jnp.repeat(normed, top_k, axis=0)
    sent_normed = (
        jnp.dot(placing, normed_rep, preferred_element_type=jnp.float32)
        .astype(jnp.bfloat16)
        .reshape(expert_count, capacity, features)
    )
    received = lax.all_to_all(sent_normed, "expert", split_axis=0, concat_axis=0, tiled=True)
    slot_block = received.reshape(expert_count * capacity, features)
    bit_count = lax.axis_size("dp").bit_length() - 1
    row_bits = bit_count // 2
    summed = expert_block(slot_block, w_in[0], w_out[0], row_bits, bit_count)
    expert_out = summed.astype(jnp.bfloat16).reshape(expert_count, capacity, features)
    returned = lax.all_to_all(
        expert_out, "expert", split_axis=0, concat_axis=0, tiled=True
    ).reshape(expert_count * capacity, features)
    pulled_back = lax.dot_general(
        placing, returned, (((0,), (0,)), ((), ())), preferred_element_type=jnp.float32
    )
    pulled_back = pulled_back.reshape(tok_rows, top_k, features)
    combined = (residual + jnp.sum(gating[:, :, None] * pulled_back, axis=1)).astype(jnp.bfloat16)
    return combined[None]


COL = 128
FFB = 256
LANE = 128
HALO = 16
BF = jnp.bfloat16
F32 = jnp.float32
MESH = pl.DeviceIdType.MESH


def silu(v):
    half = 0.5 * v
    return half + half * jnp.tanh(half)


def moe_kernel(
    n_ex, n_dp, cap,
    x_ref, ck_ref, gain_ref, rout_ref, routes_ref, w_in_ref, w_out_ref,
    o_ref,
    xp, xf, res, info, place, gate, frames, rows_out, rows_in, acc, hid, part_out, part_in,
    comb_out, comb_in, w1, w2, logit,
    w1_sem, w2_sem, halo_s, halo_r, info_s, info_r, zs, zr, xs, xr, ys, yr, rs, rr,
):
    tok, width = x_ref.shape[1], x_ref.shape[2]
    ff = w_in_ref.shape[1]
    cols = width // COL
    ffb = ff // FFB
    taps_count = ck_ref.shape[0]
    margin = (taps_count - 1) // 2
    seg = n_dp * cap
    slots = n_ex * seg
    ex = lax.axis_index("expert")
    dp = lax.axis_index("dp")
    blk = slots // 4

    def dp_peer(d):
        return lax.rem(dp + d, n_dp)

    def ex_peer(d):
        return lax.rem(ex + d, n_ex)

    def rem_copy(src, dst, ssem, rsem, e, v):
        return pltpu.make_async_remote_copy(
            src_ref=src, dst_ref=dst, send_sem=ssem, recv_sem=rsem,
            device_id=(e, v), device_id_type=MESH,
        )

    barrier = pltpu.get_barrier_semaphore()
    for d in range(1, n_dp):
        pl.semaphore_signal(barrier, inc=1, device_id=(ex, dp_peer(d)), device_id_type=MESH)
    for d in range(1, n_ex):
        pl.semaphore_signal(barrier, inc=1, device_id=(ex_peer(d), dp), device_id_type=MESH)

    def w1_copy(k):
        return pltpu.make_async_copy(
            w_in_ref.at[0, :, pl.ds(k * COL, COL)], w1.at[k], w1_sem.at[k]
        )

    def w2_copy(k):
        return pltpu.make_async_copy(
            w_out_ref.at[0, :, pl.ds(k * COL, COL)], w2.at[k], w2_sem.at[k]
        )

    for k in range(cols):
        w1_copy(k).start()
        w2_copy(k).start()

    xp[HALO : HALO + tok, :] = x_ref[0]
    expert_of = lax.broadcasted_iota(jnp.int32, (n_ex, tok), 0)
    hot = [(expert_of == routes_ref[k : k + 1, :]).astype(F32) for k in range(2)]
    before = (
        lax.broadcasted_iota(jnp.int32, (tok, tok), 0)
        < lax.broadcasted_iota(jnp.int32, (tok, tok), 1)
    ).astype(BF)
    count = jnp.dot((hot[0] + hot[1]).astype(BF), before, preferred_element_type=F32)
    counts = [count, count + hot[0]]
    rows8 = lax.broadcasted_iota(jnp.int32, (8, tok), 0)
    targets = [
        routes_ref[k : k + 1, :].astype(F32) * seg
        + (dp * cap).astype(F32)
        + jnp.sum(counts[k] * hot[k], axis=0, keepdims=True)
        for k in range(2)
    ]
    info[0, dp] = jnp.where(rows8 == 0, targets[0], targets[1])

    def conv_rows(first, count):
        def step(c, carry):
            at = pl.ds(pl.multiple_of(c * LANE, LANE), LANE)
            span = count + 2 * HALO
            xf[0:span, :] = xp[first : first + span, at].astype(F32)
            taps = ck_ref[:, at].astype(F32)
            conv = jnp.zeros((count, LANE), F32)
            for r in range(8):
                begin = HALO - margin + r
                size = min(count + 24, span - begin)
                shifted = xf[begin : begin + size, :]
                for j in range(r, taps_count, 8):
                    conv = conv + taps[j : j + 1, :] * shifted[j - r : j - r + count, :]
            res[first : first + count, at] = xf[HALO : HALO + count, :] + silu(conv)
            return carry

        lax.fori_loop(0, width // LANE, step, 0)

    conv_rows(HALO, tok - 2 * HALO)

    pl.semaphore_wait(barrier, n_dp - 1 + n_ex - 1)

    def up_copy():
        return rem_copy(
            x_ref.at[0, pl.ds(tok - HALO, HALO)], xp.at[pl.ds(0, HALO)],
            halo_s.at[0], halo_r.at[0], ex, dp_peer(1),
        )

    def down_copy():
        return rem_copy(
            x_ref.at[0, pl.ds(0, HALO)], xp.at[pl.ds(HALO + tok, HALO)],
            halo_s.at[1], halo_r.at[1], ex, dp_peer(n_dp - 1),
        )

    @pl.when(dp < n_dp - 1)
    def _():
        up_copy().start()

    @pl.when(dp > 0)
    def _():
        down_copy().start()

    def info_copy(i, d, src):
        return rem_copy(
            info.at[i, src], info.at[i, src], info_s.at[i, d], info_r.at[i, d], ex, dp_peer(d)
        )

    for d in range(1, n_dp):
        info_copy(0, d, dp).start()

    @pl.when(dp == 0)
    def _():
        xp[0:HALO, :] = jnp.zeros((HALO, width), BF)

    @pl.when(dp == n_dp - 1)
    def _():
        xp[HALO + tok :, :] = jnp.zeros((HALO, width), BF)

    @pl.when(dp > 0)
    def _():
        up_copy().wait_recv()

    @pl.when(dp < n_dp - 1)
    def _():
        down_copy().wait_recv()

    conv_rows(0, HALO)
    conv_rows(tok - HALO, HALO)

    def square_step(k, total):
        at = pl.ds(pl.multiple_of(k * COL, COL), COL)
        return total + jnp.sum(res[:, at] * res[:, at], axis=1, keepdims=True)

    total = lax.fori_loop(0, cols, square_step, jnp.zeros((tok, 1), F32))
    scale = lax.rsqrt(total * (1.0 / width) + 1e-6)

    own = pl.ds(pl.multiple_of(dp * tok, tok), tok)

    def z_copy(k, d):
        return rem_copy(
            frames.at[k, own], frames.at[k, own], zs.at[k, d], zr.at[k, d], ex, dp_peer(d)
        )

    logit[...] = jnp.zeros_like(logit)
    ahead = 4

    def norm_step(k, carry):
        at = pl.ds(pl.multiple_of(k * COL, COL), COL)
        normed = (res[:, at] * scale * gain_ref[:, at].astype(F32)).astype(BF)
        frames[k, own] = normed

        @pl.when(k < ahead)
        def _():
            for d in range(1, n_dp):
                z_copy(k, d).start()

        logit[...] += lax.dot_general(
            rout_ref[:, at], normed, (((1,), (1,)), ((), ())), preferred_element_type=F32
        )
        return carry

    lax.fori_loop(0, cols, norm_step, 0)
    gating = [
        1.0 / (1.0 + jnp.exp(-jnp.sum(hot[k] * logit[...], axis=0, keepdims=True)))
        for k in range(2)
    ]
    info[1, dp] = jnp.where(rows8 == 0, gating[0], gating[1])
    for d in range(1, n_dp):
        info_copy(1, d, dp).start()
    for d in range(1, n_dp):
        info_copy(0, d, dp).wait_recv()

    def place_step(b, carry):
        at = pl.ds(pl.multiple_of(b * blk, 16), blk)
        index = (lax.broadcasted_iota(jnp.int32, (blk, tok), 0) + b * blk).astype(F32)
        for v in range(n_dp):
            first, second = info[0, v, 0:1, :], info[0, v, 1:2, :]
            hits = jnp.where(index == first, 1.0, 0.0) + jnp.where(index == second, 1.0, 0.0)
            place[at, v * tok : (v + 1) * tok] = hits.astype(BF)
        return carry

    lax.fori_loop(0, 4, place_step, 0)

    mine_seg = pl.ds(pl.multiple_of(ex * seg, 16), seg)

    def seg_of(e):
        return pl.ds(pl.multiple_of(e * seg, 16), seg)

    def x_copy(k, d):
        return rem_copy(
            rows_out.at[k, seg_of(ex_peer(d))], rows_in.at[k, mine_seg],
            xs.at[k, d], xr.at[k, d], ex_peer(d), dp,
        )

    def y_copy(k, d):
        return rem_copy(
            part_out.at[k, seg_of(ex_peer(d))], part_in.at[k, mine_seg],
            ys.at[k, d], yr.at[k, d], ex_peer(d), dp,
        )

    for k in range(cols):
        w1_copy(k).wait()
    lag = 3

    def in_step(s, carry):
        @pl.when(s < cols)
        def _():
            for d in range(1, n_dp):
                z_copy(s, d).wait_recv()

            @pl.when(s < cols - ahead)
            def _():
                for d in range(1, n_dp):
                    z_copy(s + ahead, d).start()

            def rows_step(b, c2):
                at = pl.ds(pl.multiple_of(b * blk, 16), blk)
                rows_out[s, at] = jnp.dot(
                    place[at, :], frames[s], preferred_element_type=F32
                ).astype(BF)
                return c2

            lax.fori_loop(0, 4, rows_step, 0)
            for d in range(1, n_ex):
                x_copy(s, d).start()
            rows_in[s, mine_seg] = rows_out[s, mine_seg]

        @pl.when(s >= lag)
        def _():
            k = s - lag
            for d in range(1, n_ex):
                x_copy(k, d).wait_recv()

            def ff_step(n, c2):
                at = pl.ds(pl.multiple_of(n * FFB, FFB), FFB)
                got = lax.dot_general(
                    rows_in[k], w1[k, at], (((1,), (1,)), ((), ())), preferred_element_type=F32
                )

                @pl.when(k == 0)
                def _():
                    acc[n] = got

                @pl.when(k > 0)
                def _():
                    acc[n] += got

                return c2

            lax.fori_loop(0, ffb, ff_step, 0)

        return carry

    lax.fori_loop(0, cols + lag, in_step, 0)

    def silu_step(b, carry):
        at = pl.ds(pl.multiple_of(b * blk, 16), blk)
        for n in range(ffb):
            hid[n, at] = silu(acc[n, at]).astype(BF)
        return carry

    lax.fori_loop(0, 4, silu_step, 0)

    for d in range(1, n_dp):
        info_copy(1, d, dp).wait_recv()
    eye = (
        lax.broadcasted_iota(jnp.int32, (tok, tok), 0)
        == lax.broadcasted_iota(jnp.int32, (tok, tok), 1)
    ).astype(F32)

    def gate_step(v, carry):
        turn = [
            lax.dot_general(
                eye, info[i, v], (((1,), (1,)), ((), ())),
                precision=lax.Precision.HIGHEST, preferred_element_type=F32,
            )
            for i in range(2)
        ]
        index = lax.broadcasted_iota(jnp.int32, (tok, slots), 1).astype(F32)
        gate[v] = (
            jnp.where(index == turn[0][:, 0:1], turn[1][:, 0:1], 0.0)
            + jnp.where(index == turn[0][:, 1:2], turn[1][:, 1:2], 0.0)
        ).astype(BF)
        return carry

    for k in range(cols):
        w2_copy(k).wait()

    def r_copy(k, d):
        return rem_copy(
            comb_out.at[k, dp_peer(d)], comb_in.at[k, dp], rs.at[k, d], rr.at[k, d],
            ex, dp_peer(d),
        )

    def out_step(s, carry):
        @pl.when(s < cols)
        def _():
            def rows_step(b, c2):
                at = pl.ds(pl.multiple_of(b * blk, 16), blk)
                value = jnp.dot(hid[0, at], w2[s, 0:FFB], preferred_element_type=F32)
                for n in range(1, ffb):
                    value = value + jnp.dot(
                        hid[n, at], w2[s, n * FFB : (n + 1) * FFB], preferred_element_type=F32
                    )
                part_out[s, at] = value.astype(BF)
                return c2

            lax.fori_loop(0, 4, rows_step, 0)
            for d in range(1, n_ex):
                y_copy(s, d).start()
            part_in[s, mine_seg] = part_out[s, mine_seg]

        @pl.when(s == lag - 1)
        def _():
            lax.fori_loop(0, n_dp, gate_step, 0)

        @pl.when(s >= lag)
        def _():
            k = s - lag
            at = pl.ds(pl.multiple_of(k * COL, COL), COL)
            for d in range(1, n_ex):
                y_copy(k, d).wait_recv()

            def comb_step(v, c2):
                value = jnp.dot(gate[v], part_in[k], preferred_element_type=F32)

                @pl.when(v == dp)
                def _():
                    res[:, at] += value

                @pl.when(v != dp)
                def _():
                    comb_out[k, v] = value.astype(BF)

                return c2

            lax.fori_loop(0, n_dp, comb_step, 0)
            for d in range(1, n_dp):
                r_copy(k, d).start()

        return carry

    lax.fori_loop(0, cols + lag, out_step, 0)

    def final_step(k, carry):
        at = pl.ds(pl.multiple_of(k * COL, COL), COL)
        value = res[:, at]
        for d in range(1, n_dp):
            r_copy(k, d).wait_recv()
        for d in range(1, n_dp):
            value = value + comb_in[k, dp_peer(d)].astype(F32)
        o_ref[0, :, at] = value.astype(BF)
        for d in range(1, n_dp):
            z_copy(k, d).wait_send()
            r_copy(k, d).wait_send()
        for d in range(1, n_ex):
            x_copy(k, d).wait_send()
            y_copy(k, d).wait_send()
        return carry

    lax.fori_loop(0, cols, final_step, 0)
    for d in range(1, n_dp):
        info_copy(0, d, dp).wait_send()
        info_copy(1, d, dp).wait_send()

    @pl.when(dp < n_dp - 1)
    def _():
        up_copy().wait_send()

    @pl.when(dp > 0)
    def _():
        down_copy().wait_send()


def kernel_shards(n_ex, n_dp, cap, frames_in, conv_kernel, norm_gain, router, w_in, w_out, routes):
    tok, width = frames_in.shape[1], frames_in.shape[2]
    ff = w_in.shape[1]
    cols, ffb = width // COL, ff // FFB
    slots = n_ex * n_dp * cap
    dma = pltpu.SemaphoreType.DMA
    vmem = pl.BlockSpec(memory_space=pltpu.VMEM)
    hbm = pl.BlockSpec(memory_space=pl.ANY)
    return pl.pallas_call(
        functools.partial(moe_kernel, n_ex, n_dp, cap),
        out_shape=jax.ShapeDtypeStruct(frames_in.shape, BF),
        in_specs=[vmem] * 5 + [hbm] * 2,
        out_specs=vmem,
        scratch_shapes=[
            pltpu.VMEM((tok + 2 * HALO, width), BF),
            pltpu.VMEM((tok + 2 * HALO, LANE), F32),
            pltpu.VMEM((tok, width), F32),
            pltpu.VMEM((2, n_dp, 8, tok), F32),
            pltpu.VMEM((slots, n_dp * tok), BF),
            pltpu.VMEM((n_dp, tok, slots), BF),
            pltpu.VMEM((cols, n_dp * tok, COL), BF),
            pltpu.VMEM((cols, slots, COL), BF),
            pltpu.VMEM((cols, slots, COL), BF),
            pltpu.VMEM((ffb, slots, FFB), F32),
            pltpu.VMEM((ffb, slots, FFB), BF),
            pltpu.VMEM((cols, slots, COL), BF),
            pltpu.VMEM((cols, slots, COL), BF),
            pltpu.VMEM((cols, n_dp, tok, COL), BF),
            pltpu.VMEM((cols, n_dp, tok, COL), BF),
            pltpu.VMEM((cols, ff, COL), BF),
            pltpu.VMEM((cols, ff, COL), BF),
            pltpu.VMEM((n_ex, tok), F32),
            dma((cols,)), dma((cols,)),
            dma((2,)), dma((2,)),
            dma((2, n_dp)), dma((2, n_dp)),
            dma((cols, n_dp)), dma((cols, n_dp)),
            dma((cols, n_ex)), dma((cols, n_ex)),
            dma((cols, n_ex)), dma((cols, n_ex)),
            dma((cols, n_dp)), dma((cols, n_dp)),
        ],
        compiler_params=pltpu.CompilerParams(
            collective_id=0, has_side_effects=True, vmem_limit_bytes=56 * 2**20
        ),
    )(frames_in, conv_kernel, norm_gain[None], router.T, routes[0].T, w_in, w_out)


def kernel_fits(n_ex, n_dp, cap, tok, width, ff, top_k, kernel_len):
    seg = n_dp * cap
    return (
        n_ex == 8 and n_dp > 1 and top_k == 2 and tok % LANE == 0 and width % COL == 0
        and ff % FFB == 0 and seg % 16 == 0 and (n_ex * seg) % 64 == 0
        and kernel_len < 2 * HALO and kernel_len % 2 == 1
        and 8 * n_ex * seg * (width + ff) + 4 * ff * width < 40 * 2**20
    )


def body(mesh, *args):
    frames_in, conv_kernel, w_in, routes = args[0], args[1], args[4], args[6]
    n_ex, n_dp = mesh.shape["expert"], mesh.shape["dp"]
    tok, width, top_k = frames_in.shape[1], frames_in.shape[2], routes.shape[2]
    cap = max(2, 9 * top_k * tok // (8 * n_ex))
    if kernel_fits(n_ex, n_dp, cap, tok, width, w_in.shape[1], top_k, conv_kernel.shape[0]):
        return kernel_shards(n_ex, n_dp, cap, *args)
    return shards(*args)


def solution(mesh):
    return jax.shard_map(
        functools.partial(body, mesh),
        mesh=mesh,
        in_specs=(
            P("expert", "dp", None),
            P(),
            P(),
            P(),
            P("expert", "dp", None),
            P("expert", "dp", None),
            P("expert", "dp", None),
        ),
        out_specs=P("expert", "dp", None),
        check_vma=False,
    )
```

```python
import functools

import jax
import jax.numpy as jnp
from jax import lax
from jax.experimental import pallas as pl
from jax.experimental.pallas import tpu as pltpu
from jax.sharding import PartitionSpec as P


def swapped(value, axis, distance):
    mask = 2**distance
    pairs = [(source, source ^ mask) for source in range(lax.axis_size(axis))]
    return lax.ppermute(value, axis, pairs)


def extended(block, sides, width):
    for axis, dim in sides:
        count = lax.axis_size(axis)
        forward = [(i, i + 1) for i in range(count - 1)]
        backward = [(target, source) for source, target in forward]
        low = lax.ppermute(
            lax.slice_in_dim(block, block.shape[dim] - width, None, axis=dim), axis, forward
        )
        high = lax.ppermute(lax.slice_in_dim(block, 0, width, axis=dim), axis, backward)
        block = jnp.concatenate([low, block, high], axis=dim)
    return block


def expert_block(rows, first_w, second_w, row_bits, bit_count):
    place = lax.axis_index("dp")
    for bit in range(row_bits):
        other = swapped(rows, "dp", bit)
        upper = place >> bit & 1 == 1
        rows = jnp.concatenate(
            [jnp.where(upper, other, rows), jnp.where(upper, rows, other)], axis=0
        )
    stacked = jnp.stack([first_w, second_w])
    for bit in range(row_bits, bit_count):
        other = swapped(stacked, "dp", bit)
        stacked = jnp.concatenate([stacked, other], axis=1)
    preact = lax.dot_general(
        rows, stacked[0], (((1,), (1,)), ((), ())), preferred_element_type=jnp.float32
    )
    hidden = jax.nn.silu(preact).astype(jnp.bfloat16)
    partial_value = jnp.dot(hidden, stacked[1], preferred_element_type=jnp.float32)
    for bit in reversed(range(row_bits)):
        half_rows = partial_value.shape[0] // 2
        first_half = partial_value[:half_rows]
        second_half = partial_value[half_rows:]
        upper = place >> bit & 1 == 1
        outgoing = jnp.where(upper, first_half, second_half)
        kept = jnp.where(upper, second_half, first_half)
        partial_value = kept + swapped(outgoing.astype(jnp.bfloat16), "dp", bit).astype(
            outgoing.dtype
        )
    return partial_value


def shards(frames_in, conv_kernel, norm_gain, router, w_in, w_out, routes):
    tok_rows = frames_in.shape[1]
    features = frames_in.shape[2]
    kernel_len = conv_kernel.shape[0]
    margin = (kernel_len - 1) // 2
    padded = extended(frames_in, (("dp", 1),), margin)
    frames_f = frames_in[0].astype(jnp.float32)
    convolved = jnp.zeros((tok_rows, features), jnp.float32)
    for offset in range(kernel_len):
        convolved = convolved + conv_kernel[offset].astype(jnp.float32) * padded[
            0, offset : offset + tok_rows
        ].astype(jnp.float32)
    residual = frames_f + jax.nn.silu(convolved)
    scale_rms = lax.rsqrt(jnp.mean(residual * residual, axis=-1, keepdims=True) + 1e-06)
    normed = (residual * scale_rms * norm_gain.astype(jnp.float32)).astype(jnp.bfloat16)
    logits = jnp.dot(normed, router, preferred_element_type=jnp.float32)
    expert_count = router.shape[1]
    chosen = routes[0]
    top_k = chosen.shape[1]
    onehot = (chosen[:, :, None] == jnp.arange(expert_count, dtype=jnp.int32)).astype(jnp.float32)
    gating = jax.nn.sigmoid(jnp.sum(onehot * logits[:, None, :], axis=-1))
    pair_count = tok_rows * top_k
    flat_hot = onehot.reshape(pair_count, expert_count)
    positions = jnp.arange(pair_count, dtype=jnp.int32)
    earlier = (positions[:, None] > positions[None, :]).astype(jnp.float32)
    counts = jnp.dot(earlier, flat_hot, precision=lax.Precision.HIGHEST)
    slot_of = jnp.sum(counts * flat_hot, axis=-1).astype(jnp.int32)
    capacity = max(2, 9 * top_k * tok_rows // (8 * lax.axis_size("expert")))
    target = chosen.reshape(pair_count) * capacity + slot_of
    placing = (
        jnp.arange(expert_count * capacity, dtype=jnp.int32)[:, None] == target[None, :]
    ).astype(jnp.bfloat16)
    normed_rep = jnp.repeat(normed, top_k, axis=0)
    sent_normed = (
        jnp.dot(placing, normed_rep, preferred_element_type=jnp.float32)
        .astype(jnp.bfloat16)
        .reshape(expert_count, capacity, features)
    )
    received = lax.all_to_all(sent_normed, "expert", split_axis=0, concat_axis=0, tiled=True)
    slot_block = received.reshape(expert_count * capacity, features)
    bit_count = lax.axis_size("dp").bit_length() - 1
    row_bits = bit_count // 2
    summed = expert_block(slot_block, w_in[0], w_out[0], row_bits, bit_count)
    expert_out = summed.astype(jnp.bfloat16).reshape(expert_count, capacity, features)
    returned = lax.all_to_all(
        expert_out, "expert", split_axis=0, concat_axis=0, tiled=True
    ).reshape(expert_count * capacity, features)
    pulled_back = lax.dot_general(
        placing, returned, (((0,), (0,)), ((), ())), preferred_element_type=jnp.float32
    )
    pulled_back = pulled_back.reshape(tok_rows, top_k, features)
    combined = (residual + jnp.sum(gating[:, :, None] * pulled_back, axis=1)).astype(jnp.bfloat16)
    return combined[None]


COL = 256
FFB = 256
LANE = 128
HALO = 16
BF = jnp.bfloat16
F32 = jnp.float32
MESH = pl.DeviceIdType.MESH


def silu(v):
    half = 0.5 * v
    return half + half * jnp.tanh(half)


def pad_of(cap):
    return -(-cap // 16) * 16


def moe_kernel(
    n_ex, n_dp, cap,
    x_ref, ck_ref, gain_ref, rout_ref, routes_ref, w_in_ref, w_out_ref,
    o_ref,
    xp, xf, res, info, place, gate, frames, rows_out, rows_in, acc, hid, part_out, part_in,
    comb_out, comb_in, w1, w2, logit,
    info2, place2, gate2, spread, gather, rows2_out, rows2_in, z2_out, z2_in, y2_out, y2_in,
    w1_sem, w2_sem, halo_s, halo_r, info_s, info_r, zs, zr, xs, xr, ys, yr, rs, rr,
    x2s, x2r, zxs, zxr, z2s, z2r, y2s, y2r,
):
    tok, width = x_ref.shape[1], x_ref.shape[2]
    ff = w_in_ref.shape[1]
    cols = width // COL
    ffb = ff // FFB
    taps_count = ck_ref.shape[0]
    margin = (taps_count - 1) // 2
    seg = n_dp * cap
    slots = n_ex * seg
    ex = lax.axis_index("expert")
    dp = lax.axis_index("dp")
    blk = slots // 4
    pad = pad_of(cap)
    last = cols - 1

    def dp_peer(d):
        return lax.rem(dp + d, n_dp)

    def ex_peer(d):
        return lax.rem(ex + d, n_ex)

    def rem_copy(src, dst, ssem, rsem, e, v):
        return pltpu.make_async_remote_copy(
            src_ref=src, dst_ref=dst, send_sem=ssem, recv_sem=rsem,
            device_id=(e, v), device_id_type=MESH,
        )

    barrier = pltpu.get_barrier_semaphore()
    for d in range(1, n_dp):
        pl.semaphore_signal(barrier, inc=1, device_id=(ex, dp_peer(d)), device_id_type=MESH)
    for d in range(1, n_ex):
        pl.semaphore_signal(barrier, inc=1, device_id=(ex_peer(d), dp), device_id_type=MESH)

    def w1_copy(k):
        return pltpu.make_async_copy(
            w_in_ref.at[0, :, pl.ds(k * COL, COL)], w1.at[k], w1_sem.at[k]
        )

    def w2_copy(k):
        return pltpu.make_async_copy(
            w_out_ref.at[0, :, pl.ds(k * COL, COL)], w2.at[k], w2_sem.at[k]
        )

    for k in range(cols):
        w1_copy(k).start()
        w2_copy(k).start()

    xp[HALO : HALO + tok, :] = x_ref[0]
    expert_of = lax.broadcasted_iota(jnp.int32, (n_ex, tok), 0)
    hot = [(expert_of == routes_ref[k : k + 1, :]).astype(F32) for k in range(2)]
    before = (
        lax.broadcasted_iota(jnp.int32, (tok, tok), 0)
        < lax.broadcasted_iota(jnp.int32, (tok, tok), 1)
    ).astype(BF)
    count = jnp.dot((hot[0] + hot[1]).astype(BF), before, preferred_element_type=F32)
    counts = [count, count + hot[0]]
    rows8 = lax.broadcasted_iota(jnp.int32, (8, tok), 0)
    slot = [jnp.sum(counts[k] * hot[k], axis=0, keepdims=True) for k in range(2)]
    named = [routes_ref[k : k + 1, :].astype(F32) for k in range(2)]
    targets = [named[k] * seg + (dp * cap).astype(F32) + slot[k] for k in range(2)]
    targets2 = [named[k] * pad + slot[k] for k in range(2)]
    info2[...] = jnp.where(rows8 == 0, targets2[0], targets2[1])
    index2 = lax.broadcasted_iota(jnp.int32, (n_ex * pad, tok), 0).astype(F32)
    place2[...] = (
        jnp.where(index2 == targets2[0], 1.0, 0.0) + jnp.where(index2 == targets2[1], 1.0, 0.0)
    ).astype(BF)

    def spread_of(shape, seg_dim):
        i = lax.broadcasted_iota(jnp.int32, shape, seg_dim)
        j = lax.broadcasted_iota(jnp.int32, shape, 1 - seg_dim)
        hits = jnp.zeros(shape, F32)
        for v in range(n_dp):
            inside = (i >= v * cap) & (i < (v + 1) * cap)
            hits = hits + jnp.where(inside & (j - i == v * (pad - cap)), 1.0, 0.0)
        return hits.astype(BF)

    spread[...] = spread_of((seg, n_dp * pad), 0)
    gather[...] = spread_of((n_dp * pad, seg), 1)
    info[0, dp] = jnp.where(rows8 == 0, targets[0], targets[1])

    def conv_rows(first, count):
        def step(c, carry):
            at = pl.ds(pl.multiple_of(c * LANE, LANE), LANE)
            span = count + 2 * HALO
            xf[0:span, :] = xp[first : first + span, at].astype(F32)
            taps = ck_ref[:, at].astype(F32)
            conv = jnp.zeros((count, LANE), F32)
            for r in range(8):
                begin = HALO - margin + r
                size = min(count + 24, span - begin)
                shifted = xf[begin : begin + size, :]
                for j in range(r, taps_count, 8):
                    conv = conv + taps[j : j + 1, :] * shifted[j - r : j - r + count, :]
            res[first : first + count, at] = xf[HALO : HALO + count, :] + silu(conv)
            return carry

        lax.fori_loop(0, width // LANE, step, 0)

    conv_rows(HALO, tok - 2 * HALO)

    pl.semaphore_wait(barrier, n_dp - 1 + n_ex - 1)

    def up_copy():
        return rem_copy(
            x_ref.at[0, pl.ds(tok - HALO, HALO)], xp.at[pl.ds(0, HALO)],
            halo_s.at[0], halo_r.at[0], ex, dp_peer(1),
        )

    def down_copy():
        return rem_copy(
            x_ref.at[0, pl.ds(0, HALO)], xp.at[pl.ds(HALO + tok, HALO)],
            halo_s.at[1], halo_r.at[1], ex, dp_peer(n_dp - 1),
        )

    @pl.when(dp < n_dp - 1)
    def _():
        up_copy().start()

    @pl.when(dp > 0)
    def _():
        down_copy().start()

    def info_copy(i, d, src):
        return rem_copy(
            info.at[i, src], info.at[i, src], info_s.at[i, d], info_r.at[i, d], ex, dp_peer(d)
        )

    for d in range(1, n_dp):
        info_copy(0, d, dp).start()

    @pl.when(dp == 0)
    def _():
        xp[0:HALO, :] = jnp.zeros((HALO, width), BF)

    @pl.when(dp == n_dp - 1)
    def _():
        xp[HALO + tok :, :] = jnp.zeros((HALO, width), BF)

    @pl.when(dp > 0)
    def _():
        up_copy().wait_recv()

    @pl.when(dp < n_dp - 1)
    def _():
        down_copy().wait_recv()

    conv_rows(0, HALO)
    conv_rows(tok - HALO, HALO)

    def square_step(k, total):
        at = pl.ds(pl.multiple_of(k * COL, COL), COL)
        return total + jnp.sum(res[:, at] * res[:, at], axis=1, keepdims=True)

    total = lax.fori_loop(0, cols, square_step, jnp.zeros((tok, 1), F32))
    scale = lax.rsqrt(total * (1.0 / width) + 1e-6)

    own = pl.ds(pl.multiple_of(dp * tok, tok), tok)

    def z_copy(k, d):
        return rem_copy(
            frames.at[k, own], frames.at[k, own], zs.at[k, d], zr.at[k, d], ex, dp_peer(d)
        )

    logit[...] = jnp.zeros_like(logit)
    ahead = 2

    def norm_step(k, carry):
        at = pl.ds(pl.multiple_of(k * COL, COL), COL)
        normed = (res[:, at] * scale * gain_ref[:, at].astype(F32)).astype(BF)
        frames[k, own] = normed

        @pl.when(k < ahead)
        def _():
            for d in range(1, n_dp):
                z_copy(k, d).start()

        logit[...] += lax.dot_general(
            rout_ref[:, at], normed, (((1,), (1,)), ((), ())), preferred_element_type=F32
        )
        return carry

    lax.fori_loop(0, cols, norm_step, 0)
    mine_pad = pl.ds(pl.multiple_of(ex * pad, 16), pad)

    def pad_at(e):
        return pl.ds(pl.multiple_of(e * pad, 16), pad)

    def x2_copy(d):
        return rem_copy(
            rows2_out.at[pad_at(ex_peer(d))], rows2_in.at[dp, mine_pad],
            x2s.at[d], x2r.at[d], ex_peer(d), dp,
        )

    def zx_copy(d):
        return rem_copy(
            rows2_in.at[dp], rows2_in.at[dp], zxs.at[d], zxr.at[d], ex, dp_peer(d)
        )

    def z2_copy(d):
        return rem_copy(
            z2_out.at[dp_peer(d)], z2_in.at[dp], z2s.at[d], z2r.at[d], ex, dp_peer(d)
        )

    def y2_copy(d):
        return rem_copy(
            y2_out.at[pad_at(ex_peer(d))], y2_in.at[mine_pad],
            y2s.at[d], y2r.at[d], ex_peer(d), dp,
        )

    rows2_out[...] = jnp.dot(
        place2[...], frames[last, own], preferred_element_type=F32
    ).astype(BF)
    for d in range(1, n_ex):
        x2_copy(d).start()
    rows2_in[dp, mine_pad] = rows2_out[mine_pad, :]
    gating = [
        1.0 / (1.0 + jnp.exp(-jnp.sum(hot[k] * logit[...], axis=0, keepdims=True)))
        for k in range(2)
    ]
    info[1, dp] = jnp.where(rows8 == 0, gating[0], gating[1])
    for d in range(1, n_dp):
        info_copy(1, d, dp).start()
    for d in range(1, n_dp):
        info_copy(0, d, dp).wait_recv()

    def place_step(b, carry):
        at = pl.ds(pl.multiple_of(b * blk, 16), blk)
        index = (lax.broadcasted_iota(jnp.int32, (blk, tok), 0) + b * blk).astype(F32)
        for v in range(n_dp):
            first, second = info[0, v, 0:1, :], info[0, v, 1:2, :]
            hits = jnp.where(index == first, 1.0, 0.0) + jnp.where(index == second, 1.0, 0.0)
            place[at, v * tok : (v + 1) * tok] = hits.astype(BF)
        return carry

    lax.fori_loop(0, 4, place_step, 0)

    mine_seg = pl.ds(pl.multiple_of(ex * seg, 16), seg)

    def seg_of(e):
        return pl.ds(pl.multiple_of(e * seg, 16), seg)

    def x_copy(k, d):
        return rem_copy(
            rows_out.at[k, seg_of(ex_peer(d))], rows_in.at[k, mine_seg],
            xs.at[k, d], xr.at[k, d], ex_peer(d), dp,
        )

    def y_copy(k, d):
        return rem_copy(
            part_out.at[k, seg_of(ex_peer(d))], part_in.at[k, mine_seg],
            ys.at[k, d], yr.at[k, d], ex_peer(d), dp,
        )

    for k in range(cols):
        w1_copy(k).wait()
    lag = 2

    def first_matmul(k):
        def ff_step(n, c2):
            at = pl.ds(pl.multiple_of(n * FFB, FFB), FFB)
            got = lax.dot_general(
                rows_in[k], w1[k, at], (((1,), (1,)), ((), ())), preferred_element_type=F32
            )

            @pl.when(k == 0)
            def _():
                acc[n] = got

            @pl.when(k > 0)
            def _():
                acc[n] += got

            return c2

        lax.fori_loop(0, ffb, ff_step, 0)

    def in_step(s, carry):
        @pl.when(s < last)
        def _():
            for d in range(1, n_dp):
                z_copy(s, d).wait_recv()

            @pl.when(s < last - ahead)
            def _():
                for d in range(1, n_dp):
                    z_copy(s + ahead, d).start()

            @pl.when(s == last - ahead - 1)
            def _():
                for d in range(1, n_ex):
                    x2_copy(d).wait_recv()
                for d in range(1, n_dp):
                    zx_copy(d).start()

            def rows_step(b, c2):
                at = pl.ds(pl.multiple_of(b * blk, 16), blk)
                rows_out[s, at] = jnp.dot(
                    place[at, :], frames[s], preferred_element_type=F32
                ).astype(BF)
                return c2

            lax.fori_loop(0, 4, rows_step, 0)
            for d in range(1, n_ex):
                x_copy(s, d).start()
            rows_in[s, mine_seg] = rows_out[s, mine_seg]

        @pl.when(s >= lag)
        def _():
            for d in range(1, n_ex):
                x_copy(s - lag, d).wait_recv()
            first_matmul(s - lag)

        return carry

    lax.fori_loop(0, last + lag, in_step, 0)
    for d in range(1, n_dp):
        zx_copy(d).wait_recv()

    def spread_step(u, carry):
        got = jnp.concatenate([rows2_in[v, pad_at(u)] for v in range(n_dp)], axis=0)
        rows_in[last, seg_of(u)] = jnp.dot(
            spread[...], got, preferred_element_type=F32
        ).astype(BF)
        return carry

    lax.fori_loop(0, n_ex, spread_step, 0)
    first_matmul(jnp.int32(last))

    def silu_step(b, carry):
        at = pl.ds(pl.multiple_of(b * blk, 16), blk)
        for n in range(ffb):
            hid[n, at] = silu(acc[n, at]).astype(BF)
        return carry

    lax.fori_loop(0, 4, silu_step, 0)

    for d in range(1, n_dp):
        info_copy(1, d, dp).wait_recv()
    eye = (
        lax.broadcasted_iota(jnp.int32, (tok, tok), 0)
        == lax.broadcasted_iota(jnp.int32, (tok, tok), 1)
    ).astype(F32)

    def gate_step(v, carry):
        turn = [
            lax.dot_general(
                eye, info[i, v], (((1,), (1,)), ((), ())),
                precision=lax.Precision.HIGHEST, preferred_element_type=F32,
            )
            for i in range(2)
        ]
        index = lax.broadcasted_iota(jnp.int32, (tok, slots), 1).astype(F32)
        gate[v] = (
            jnp.where(index == turn[0][:, 0:1], turn[1][:, 0:1], 0.0)
            + jnp.where(index == turn[0][:, 1:2], turn[1][:, 1:2], 0.0)
        ).astype(BF)
        return carry

    for k in range(cols):
        w2_copy(k).wait()

    def r_copy(k, d):
        return rem_copy(
            comb_out.at[k, dp_peer(d)], comb_in.at[k, dp], rs.at[k, d], rr.at[k, d],
            ex, dp_peer(d),
        )

    def second_matmul(k):
        def rows_step(b, c2):
            at = pl.ds(pl.multiple_of(b * blk, 16), blk)
            value = jnp.dot(hid[0, at], w2[k, 0:FFB], preferred_element_type=F32)
            for n in range(1, ffb):
                value = value + jnp.dot(
                    hid[n, at], w2[k, n * FFB : (n + 1) * FFB], preferred_element_type=F32
                )
            part_out[k, at] = value.astype(BF)
            return c2

        lax.fori_loop(0, 4, rows_step, 0)

    def gather_step(u, carry):
        got = jnp.dot(
            gather[...], part_out[last, seg_of(u)], preferred_element_type=F32
        ).astype(BF)
        for v in range(n_dp):
            z2_out[v, pad_at(u)] = got[v * pad : (v + 1) * pad]
        return carry

    def out_step(s, carry):
        @pl.when(s < last)
        def _():
            second_matmul(s)
            for d in range(1, n_ex):
                y_copy(s, d).start()
            part_in[s, mine_seg] = part_out[s, mine_seg]

        @pl.when(s == 0)
        def _():
            second_matmul(jnp.int32(last))
            lax.fori_loop(0, n_ex, gather_step, 0)
            for d in range(1, n_dp):
                z2_copy(d).start()

        @pl.when(s == last - 1)
        def _():
            total2 = z2_out[dp].astype(F32)
            for d in range(1, n_dp):
                z2_copy(d).wait_recv()
            for d in range(1, n_dp):
                total2 = total2 + z2_in[dp_peer(d)].astype(F32)
            y2_out[...] = total2.astype(BF)
            for d in range(1, n_ex):
                y2_copy(d).start()
            y2_in[mine_pad, :] = y2_out[mine_pad, :]

        @pl.when(s == lag - 1)
        def _():
            lax.fori_loop(0, n_dp, gate_step, 0)
            turn = [
                lax.dot_general(
                    eye, mat, (((1,), (1,)), ((), ())),
                    precision=lax.Precision.HIGHEST, preferred_element_type=F32,
                )
                for mat in (info2[...], info[1, dp])
            ]
            across = lax.broadcasted_iota(jnp.int32, (tok, n_ex * pad), 1).astype(F32)
            gate2[...] = (
                jnp.where(across == turn[0][:, 0:1], turn[1][:, 0:1], 0.0)
                + jnp.where(across == turn[0][:, 1:2], turn[1][:, 1:2], 0.0)
            ).astype(BF)

        @pl.when(s >= lag)
        def _():
            k = s - lag
            at = pl.ds(pl.multiple_of(k * COL, COL), COL)
            for d in range(1, n_ex):
                y_copy(k, d).wait_recv()

            def comb_step(v, c2):
                value = jnp.dot(gate[v], part_in[k], preferred_element_type=F32)

                @pl.when(v == dp)
                def _():
                    res[:, at] += value

                @pl.when(v != dp)
                def _():
                    comb_out[k, v] = value.astype(BF)

                return c2

            lax.fori_loop(0, n_dp, comb_step, 0)
            for d in range(1, n_dp):
                r_copy(k, d).start()

        return carry

    lax.fori_loop(0, last + lag, out_step, 0)
    for d in range(1, n_ex):
        y2_copy(d).wait_recv()
    ending = slice(last * COL, width)
    o_ref[0, :, ending] = (
        res[:, ending] + jnp.dot(gate2[...], y2_in[...], preferred_element_type=F32)
    ).astype(BF)

    def final_step(k, carry):
        at = pl.ds(pl.multiple_of(k * COL, COL), COL)
        value = res[:, at]
        for d in range(1, n_dp):
            r_copy(k, d).wait_recv()
        for d in range(1, n_dp):
            value = value + comb_in[k, dp_peer(d)].astype(F32)
        o_ref[0, :, at] = value.astype(BF)
        for d in range(1, n_dp):
            z_copy(k, d).wait_send()
            r_copy(k, d).wait_send()
        for d in range(1, n_ex):
            x_copy(k, d).wait_send()
            y_copy(k, d).wait_send()
        return carry

    lax.fori_loop(0, last, final_step, 0)
    for d in range(1, n_dp):
        zx_copy(d).wait_send()
        z2_copy(d).wait_send()
    for d in range(1, n_ex):
        x2_copy(d).wait_send()
        y2_copy(d).wait_send()
    for d in range(1, n_dp):
        info_copy(0, d, dp).wait_send()
        info_copy(1, d, dp).wait_send()

    @pl.when(dp < n_dp - 1)
    def _():
        up_copy().wait_send()

    @pl.when(dp > 0)
    def _():
        down_copy().wait_send()


def kernel_shards(n_ex, n_dp, cap, frames_in, conv_kernel, norm_gain, router, w_in, w_out, routes):
    tok, width = frames_in.shape[1], frames_in.shape[2]
    ff = w_in.shape[1]
    cols, ffb = width // COL, ff // FFB
    slots = n_ex * n_dp * cap
    pad = pad_of(cap)
    wide = n_ex * pad
    dma = pltpu.SemaphoreType.DMA
    vmem = pl.BlockSpec(memory_space=pltpu.VMEM)
    hbm = pl.BlockSpec(memory_space=pl.ANY)
    return pl.pallas_call(
        functools.partial(moe_kernel, n_ex, n_dp, cap),
        out_shape=jax.ShapeDtypeStruct(frames_in.shape, BF),
        in_specs=[vmem] * 5 + [hbm] * 2,
        out_specs=vmem,
        scratch_shapes=[
            pltpu.VMEM((tok + 2 * HALO, width), BF),
            pltpu.VMEM((tok + 2 * HALO, LANE), F32),
            pltpu.VMEM((tok, width), F32),
            pltpu.VMEM((2, n_dp, 8, tok), F32),
            pltpu.VMEM((slots, n_dp * tok), BF),
            pltpu.VMEM((n_dp, tok, slots), BF),
            pltpu.VMEM((cols, n_dp * tok, COL), BF),
            pltpu.VMEM((cols, slots, COL), BF),
            pltpu.VMEM((cols, slots, COL), BF),
            pltpu.VMEM((ffb, slots, FFB), F32),
            pltpu.VMEM((ffb, slots, FFB), BF),
            pltpu.VMEM((cols, slots, COL), BF),
            pltpu.VMEM((cols, slots, COL), BF),
            pltpu.VMEM((cols, n_dp, tok, COL), BF),
            pltpu.VMEM((cols, n_dp, tok, COL), BF),
            pltpu.VMEM((cols, ff, COL), BF),
            pltpu.VMEM((cols, ff, COL), BF),
            pltpu.VMEM((n_ex, tok), F32),
            pltpu.VMEM((8, tok), F32),
            pltpu.VMEM((wide, tok), BF),
            pltpu.VMEM((tok, wide), BF),
            pltpu.VMEM((n_dp * cap, n_dp * pad), BF),
            pltpu.VMEM((n_dp * pad, n_dp * cap), BF),
            pltpu.VMEM((wide, COL), BF),
            pltpu.VMEM((n_dp, wide, COL), BF),
            pltpu.VMEM((n_dp, wide, COL), BF),
            pltpu.VMEM((n_dp, wide, COL), BF),
            pltpu.VMEM((wide, COL), BF),
            pltpu.VMEM((wide, COL), BF),
            dma((cols,)), dma((cols,)),
            dma((2,)), dma((2,)),
            dma((2, n_dp)), dma((2, n_dp)),
            dma((cols, n_dp)), dma((cols, n_dp)),
            dma((cols, n_ex)), dma((cols, n_ex)),
            dma((cols, n_ex)), dma((cols, n_ex)),
            dma((cols, n_dp)), dma((cols, n_dp)),
            dma((n_ex,)), dma((n_ex,)), dma((n_dp,)), dma((n_dp,)),
            dma((n_dp,)), dma((n_dp,)), dma((n_ex,)), dma((n_ex,)),
        ],
        compiler_params=pltpu.CompilerParams(
            collective_id=0, has_side_effects=True, vmem_limit_bytes=56 * 2**20
        ),
    )(frames_in, conv_kernel, norm_gain[None], router.T, routes[0].T, w_in, w_out)


def kernel_fits(n_ex, n_dp, cap, tok, width, ff, top_k, kernel_len):
    seg = n_dp * cap
    return (
        n_ex == 8 and n_dp > 1 and top_k == 2 and tok % LANE == 0 and width % COL == 0 and width >= 4 * COL
        and ff % FFB == 0 and seg % 16 == 0 and (n_ex * seg) % 64 == 0
        and kernel_len < 2 * HALO and kernel_len % 2 == 1
        and 8 * n_ex * seg * (width + ff) + 4 * ff * width < 40 * 2**20
    )


def body(mesh, *args):
    frames_in, conv_kernel, w_in, routes = args[0], args[1], args[4], args[6]
    n_ex, n_dp = mesh.shape["expert"], mesh.shape["dp"]
    tok, width, top_k = frames_in.shape[1], frames_in.shape[2], routes.shape[2]
    cap = max(2, 9 * top_k * tok // (8 * n_ex))
    if kernel_fits(n_ex, n_dp, cap, tok, width, w_in.shape[1], top_k, conv_kernel.shape[0]):
        return kernel_shards(n_ex, n_dp, cap, *args)
    return shards(*args)


def solution(mesh):
    return jax.shard_map(
        functools.partial(body, mesh),
        mesh=mesh,
        in_specs=(
            P("expert", "dp", None),
            P(),
            P(),
            P(),
            P("expert", "dp", None),
            P("expert", "dp", None),
            P("expert", "dp", None),
        ),
        out_specs=P("expert", "dp", None),
        check_vma=False,
    )
```

```python
import functools

import jax
import jax.numpy as jnp
from jax import lax
from jax.experimental import pallas as pl
from jax.experimental.pallas import tpu as pltpu
from jax.sharding import PartitionSpec as P


def swapped(value, axis, distance):
    mask = 2**distance
    pairs = [(source, source ^ mask) for source in range(lax.axis_size(axis))]
    return lax.ppermute(value, axis, pairs)


def extended(block, sides, width):
    for axis, dim in sides:
        count = lax.axis_size(axis)
        forward = [(i, i + 1) for i in range(count - 1)]
        backward = [(target, source) for source, target in forward]
        low = lax.ppermute(
            lax.slice_in_dim(block, block.shape[dim] - width, None, axis=dim), axis, forward
        )
        high = lax.ppermute(lax.slice_in_dim(block, 0, width, axis=dim), axis, backward)
        block = jnp.concatenate([low, block, high], axis=dim)
    return block


def expert_block(rows, first_w, second_w, row_bits, bit_count):
    place = lax.axis_index("dp")
    for bit in range(row_bits):
        other = swapped(rows, "dp", bit)
        upper = place >> bit & 1 == 1
        rows = jnp.concatenate(
            [jnp.where(upper, other, rows), jnp.where(upper, rows, other)], axis=0
        )
    stacked = jnp.stack([first_w, second_w])
    for bit in range(row_bits, bit_count):
        other = swapped(stacked, "dp", bit)
        stacked = jnp.concatenate([stacked, other], axis=1)
    preact = lax.dot_general(
        rows, stacked[0], (((1,), (1,)), ((), ())), preferred_element_type=jnp.float32
    )
    hidden = jax.nn.silu(preact).astype(jnp.bfloat16)
    partial_value = jnp.dot(hidden, stacked[1], preferred_element_type=jnp.float32)
    for bit in reversed(range(row_bits)):
        half_rows = partial_value.shape[0] // 2
        first_half = partial_value[:half_rows]
        second_half = partial_value[half_rows:]
        upper = place >> bit & 1 == 1
        outgoing = jnp.where(upper, first_half, second_half)
        kept = jnp.where(upper, second_half, first_half)
        partial_value = kept + swapped(outgoing.astype(jnp.bfloat16), "dp", bit).astype(
            outgoing.dtype
        )
    return partial_value


def shards(frames_in, conv_kernel, norm_gain, router, w_in, w_out, routes):
    tok_rows = frames_in.shape[1]
    features = frames_in.shape[2]
    kernel_len = conv_kernel.shape[0]
    margin = (kernel_len - 1) // 2
    padded = extended(frames_in, (("dp", 1),), margin)
    frames_f = frames_in[0].astype(jnp.float32)
    convolved = jnp.zeros((tok_rows, features), jnp.float32)
    for offset in range(kernel_len):
        convolved = convolved + conv_kernel[offset].astype(jnp.float32) * padded[
            0, offset : offset + tok_rows
        ].astype(jnp.float32)
    residual = frames_f + jax.nn.silu(convolved)
    scale_rms = lax.rsqrt(jnp.mean(residual * residual, axis=-1, keepdims=True) + 1e-06)
    normed = (residual * scale_rms * norm_gain.astype(jnp.float32)).astype(jnp.bfloat16)
    logits = jnp.dot(normed, router, preferred_element_type=jnp.float32)
    expert_count = router.shape[1]
    chosen = routes[0]
    top_k = chosen.shape[1]
    onehot = (chosen[:, :, None] == jnp.arange(expert_count, dtype=jnp.int32)).astype(jnp.float32)
    gating = jax.nn.sigmoid(jnp.sum(onehot * logits[:, None, :], axis=-1))
    pair_count = tok_rows * top_k
    flat_hot = onehot.reshape(pair_count, expert_count)
    positions = jnp.arange(pair_count, dtype=jnp.int32)
    earlier = (positions[:, None] > positions[None, :]).astype(jnp.float32)
    counts = jnp.dot(earlier, flat_hot, precision=lax.Precision.HIGHEST)
    slot_of = jnp.sum(counts * flat_hot, axis=-1).astype(jnp.int32)
    capacity = max(2, 9 * top_k * tok_rows // (8 * lax.axis_size("expert")))
    target = chosen.reshape(pair_count) * capacity + slot_of
    placing = (
        jnp.arange(expert_count * capacity, dtype=jnp.int32)[:, None] == target[None, :]
    ).astype(jnp.bfloat16)
    normed_rep = jnp.repeat(normed, top_k, axis=0)
    sent_normed = (
        jnp.dot(placing, normed_rep, preferred_element_type=jnp.float32)
        .astype(jnp.bfloat16)
        .reshape(expert_count, capacity, features)
    )
    received = lax.all_to_all(sent_normed, "expert", split_axis=0, concat_axis=0, tiled=True)
    slot_block = received.reshape(expert_count * capacity, features)
    bit_count = lax.axis_size("dp").bit_length() - 1
    row_bits = bit_count // 2
    summed = expert_block(slot_block, w_in[0], w_out[0], row_bits, bit_count)
    expert_out = summed.astype(jnp.bfloat16).reshape(expert_count, capacity, features)
    returned = lax.all_to_all(
        expert_out, "expert", split_axis=0, concat_axis=0, tiled=True
    ).reshape(expert_count * capacity, features)
    pulled_back = lax.dot_general(
        placing, returned, (((0,), (0,)), ((), ())), preferred_element_type=jnp.float32
    )
    pulled_back = pulled_back.reshape(tok_rows, top_k, features)
    combined = (residual + jnp.sum(gating[:, :, None] * pulled_back, axis=1)).astype(jnp.bfloat16)
    return combined[None]


COL = 256
FFB = 256
LANE = 128
HALO = 16
BF = jnp.bfloat16
F32 = jnp.float32
MESH = pl.DeviceIdType.MESH


def silu(v):
    half = 0.5 * v
    return half + half * jnp.tanh(half)


def pad_of(cap):
    return -(-cap // 16) * 16


def moe_kernel(
    n_ex, n_dp, cap,
    x_ref, ck_ref, gain_ref, rout_ref, routes_ref, w_in_ref, w_out_ref,
    o_ref,
    xp, xf, res, info, place, gate, frames, rows_out, rows_in, acc, hid, part_out, part_in,
    comb_out, comb_in, w1, w2, logit,
    info2, place2, gate2, spread, gather, rows2_out, rows2_in, z2_out, z2_in, y2_out, y2_in,
    w1_sem, w2_sem, halo_s, halo_r, info_s, info_r, zs, zr, xs, xr, ys, yr, rs, rr,
    x2s, x2r, zxs, zxr, z2s, z2r, y2s, y2r, added, fs, ads, adr,
):
    tok, width = x_ref.shape[1], x_ref.shape[2]
    ff = w_in_ref.shape[1]
    cols = width // COL
    ffb = ff // FFB
    taps_count = ck_ref.shape[0]
    margin = (taps_count - 1) // 2
    seg = n_dp * cap
    slots = n_ex * seg
    ex = lax.axis_index("expert")
    dp = lax.axis_index("dp")
    blk = slots // 4
    pad = pad_of(cap)
    last = cols - 1

    def dp_peer(d):
        return lax.rem(dp + d, n_dp)

    def ex_peer(d):
        return lax.rem(ex + d, n_ex)

    def rem_copy(src, dst, ssem, rsem, e, v):
        return pltpu.make_async_remote_copy(
            src_ref=src, dst_ref=dst, send_sem=ssem, recv_sem=rsem,
            device_id=(e, v), device_id_type=MESH,
        )

    relay = n_dp == 4
    inner = jnp.logical_and(dp > 0, dp < n_dp - 1)
    outer = jnp.logical_not(inner)

    def unless_far(relayed, d, run):
        if relay and d == n_dp - 1:
            pl.when(jnp.logical_not(jnp.logical_and(relayed, dp == 0)))(run)
        elif relay and d == 1:
            pl.when(jnp.logical_not(jnp.logical_and(relayed, dp == n_dp - 1)))(run)
        else:
            run()

    barrier = pltpu.get_barrier_semaphore()
    for d in range(1, n_dp):
        pl.semaphore_signal(barrier, inc=1, device_id=(ex, dp_peer(d)), device_id_type=MESH)
    for d in range(1, n_ex):
        pl.semaphore_signal(barrier, inc=1, device_id=(ex_peer(d), dp), device_id_type=MESH)

    def w1_copy(k):
        return pltpu.make_async_copy(
            w_in_ref.at[0, :, pl.ds(k * COL, COL)], w1.at[k], w1_sem.at[k]
        )

    def w2_copy(k):
        return pltpu.make_async_copy(
            w_out_ref.at[0, :, pl.ds(k * COL, COL)], w2.at[k], w2_sem.at[k]
        )

    for k in range(cols):
        w1_copy(k).start()
        w2_copy(k).start()

    xp[HALO : HALO + tok, :] = x_ref[0]
    expert_of = lax.broadcasted_iota(jnp.int32, (n_ex, tok), 0)
    hot = [(expert_of == routes_ref[k : k + 1, :]).astype(F32) for k in range(2)]
    before = (
        lax.broadcasted_iota(jnp.int32, (tok, tok), 0)
        < lax.broadcasted_iota(jnp.int32, (tok, tok), 1)
    ).astype(BF)
    count = jnp.dot((hot[0] + hot[1]).astype(BF), before, preferred_element_type=F32)
    counts = [count, count + hot[0]]
    rows8 = lax.broadcasted_iota(jnp.int32, (8, tok), 0)
    slot = [jnp.sum(counts[k] * hot[k], axis=0, keepdims=True) for k in range(2)]
    named = [routes_ref[k : k + 1, :].astype(F32) for k in range(2)]
    targets = [named[k] * seg + (dp * cap).astype(F32) + slot[k] for k in range(2)]
    targets2 = [named[k] * pad + slot[k] for k in range(2)]
    info2[...] = jnp.where(rows8 == 0, targets2[0], targets2[1])
    index2 = lax.broadcasted_iota(jnp.int32, (n_ex * pad, tok), 0).astype(F32)
    place2[...] = (
        jnp.where(index2 == targets2[0], 1.0, 0.0) + jnp.where(index2 == targets2[1], 1.0, 0.0)
    ).astype(BF)

    def spread_of(shape, seg_dim):
        i = lax.broadcasted_iota(jnp.int32, shape, seg_dim)
        j = lax.broadcasted_iota(jnp.int32, shape, 1 - seg_dim)
        hits = jnp.zeros(shape, F32)
        for v in range(n_dp):
            inside = (i >= v * cap) & (i < (v + 1) * cap)
            hits = hits + jnp.where(inside & (j - i == v * (pad - cap)), 1.0, 0.0)
        return hits.astype(BF)

    spread[...] = spread_of((seg, n_dp * pad), 0)
    gather[...] = spread_of((n_dp * pad, seg), 1)
    info[0, dp] = jnp.where(rows8 == 0, targets[0], targets[1])

    def conv_rows(first, count):
        def step(c, carry):
            at = pl.ds(pl.multiple_of(c * LANE, LANE), LANE)
            span = count + 2 * HALO
            xf[0:span, :] = xp[first : first + span, at].astype(F32)
            taps = ck_ref[:, at].astype(F32)
            conv = jnp.zeros((count, LANE), F32)
            for r in range(8):
                begin = HALO - margin + r
                size = min(count + 24, span - begin)
                shifted = xf[begin : begin + size, :]
                for j in range(r, taps_count, 8):
                    conv = conv + taps[j : j + 1, :] * shifted[j - r : j - r + count, :]
            res[first : first + count, at] = xf[HALO : HALO + count, :] + silu(conv)
            return carry

        lax.fori_loop(0, width // LANE, step, 0)

    conv_rows(HALO, tok - 2 * HALO)

    pl.semaphore_wait(barrier, n_dp - 1 + n_ex - 1)

    def up_copy():
        return rem_copy(
            x_ref.at[0, pl.ds(tok - HALO, HALO)], xp.at[pl.ds(0, HALO)],
            halo_s.at[0], halo_r.at[0], ex, dp_peer(1),
        )

    def down_copy():
        return rem_copy(
            x_ref.at[0, pl.ds(0, HALO)], xp.at[pl.ds(HALO + tok, HALO)],
            halo_s.at[1], halo_r.at[1], ex, dp_peer(n_dp - 1),
        )

    @pl.when(dp < n_dp - 1)
    def _():
        up_copy().start()

    @pl.when(dp > 0)
    def _():
        down_copy().start()

    def info_copy(i, d, src):
        return rem_copy(
            info.at[i, src], info.at[i, src], info_s.at[i, d], info_r.at[i, d], ex, dp_peer(d)
        )

    for d in range(1, n_dp):
        info_copy(0, d, dp).start()

    @pl.when(dp == 0)
    def _():
        xp[0:HALO, :] = jnp.zeros((HALO, width), BF)

    @pl.when(dp == n_dp - 1)
    def _():
        xp[HALO + tok :, :] = jnp.zeros((HALO, width), BF)

    @pl.when(dp > 0)
    def _():
        up_copy().wait_recv()

    @pl.when(dp < n_dp - 1)
    def _():
        down_copy().wait_recv()

    conv_rows(0, HALO)
    conv_rows(tok - HALO, HALO)

    def square_step(k, total):
        at = pl.ds(pl.multiple_of(k * COL, COL), COL)
        return total + jnp.sum(res[:, at] * res[:, at], axis=1, keepdims=True)

    total = lax.fori_loop(0, cols, square_step, jnp.zeros((tok, 1), F32))
    scale = lax.rsqrt(total * (1.0 / width) + 1e-6)

    own = pl.ds(pl.multiple_of(dp * tok, tok), tok)

    def z_copy(k, d):
        return rem_copy(
            frames.at[k, own], frames.at[k, own], zs.at[k, d], zr.at[k, d], ex, dp_peer(d)
        )

    def z_start(k):
        for d in range(1, n_dp):
            unless_far(k >= 1, d, z_copy(k, d).start)

    def z_forward(k):
        block = pl.ds(pl.multiple_of((2 - dp) * 3 * tok, tok), tok)
        return rem_copy(
            frames.at[k, block], frames.at[k, block],
            fs.at[k], zr.at[k, 2 * dp - 1], ex, (dp - 1) * 3,
        )

    logit[...] = jnp.zeros_like(logit)
    ahead = 2

    def norm_step(k, carry):
        at = pl.ds(pl.multiple_of(k * COL, COL), COL)
        normed = (res[:, at] * scale * gain_ref[:, at].astype(F32)).astype(BF)
        frames[k, own] = normed

        @pl.when(k < ahead)
        def _():
            z_start(k)

        logit[...] += lax.dot_general(
            rout_ref[:, at], normed, (((1,), (1,)), ((), ())), preferred_element_type=F32
        )
        return carry

    lax.fori_loop(0, cols, norm_step, 0)
    mine_pad = pl.ds(pl.multiple_of(ex * pad, 16), pad)

    def pad_at(e):
        return pl.ds(pl.multiple_of(e * pad, 16), pad)

    def x2_copy(d):
        return rem_copy(
            rows2_out.at[pad_at(ex_peer(d))], rows2_in.at[dp, mine_pad],
            x2s.at[d], x2r.at[d], ex_peer(d), dp,
        )

    def zx_copy(d):
        return rem_copy(
            rows2_in.at[dp], rows2_in.at[dp], zxs.at[d], zxr.at[d], ex, dp_peer(d)
        )

    def z2_copy(d):
        return rem_copy(
            z2_out.at[dp_peer(d)], z2_in.at[dp], z2s.at[d], z2r.at[d], ex, dp_peer(d)
        )

    def y2_copy(d):
        return rem_copy(
            y2_out.at[pad_at(ex_peer(d))], y2_in.at[mine_pad],
            y2s.at[d], y2r.at[d], ex_peer(d), dp,
        )

    rows2_out[...] = jnp.dot(
        place2[...], frames[last, own], preferred_element_type=F32
    ).astype(BF)
    for d in range(1, n_ex):
        x2_copy(d).start()
    rows2_in[dp, mine_pad] = rows2_out[mine_pad, :]
    gating = [
        1.0 / (1.0 + jnp.exp(-jnp.sum(hot[k] * logit[...], axis=0, keepdims=True)))
        for k in range(2)
    ]
    info[1, dp] = jnp.where(rows8 == 0, gating[0], gating[1])
    for d in range(1, n_dp):
        info_copy(1, d, dp).start()
    for d in range(1, n_dp):
        info_copy(0, d, dp).wait_recv()

    def place_step(b, carry):
        at = pl.ds(pl.multiple_of(b * blk, 16), blk)
        index = (lax.broadcasted_iota(jnp.int32, (blk, tok), 0) + b * blk).astype(F32)
        for v in range(n_dp):
            first, second = info[0, v, 0:1, :], info[0, v, 1:2, :]
            hits = jnp.where(index == first, 1.0, 0.0) + jnp.where(index == second, 1.0, 0.0)
            place[at, v * tok : (v + 1) * tok] = hits.astype(BF)
        return carry

    lax.fori_loop(0, 4, place_step, 0)

    mine_seg = pl.ds(pl.multiple_of(ex * seg, 16), seg)

    def seg_of(e):
        return pl.ds(pl.multiple_of(e * seg, 16), seg)

    def x_copy(k, d):
        return rem_copy(
            rows_out.at[k, seg_of(ex_peer(d))], rows_in.at[k, mine_seg],
            xs.at[k, d], xr.at[k, d], ex_peer(d), dp,
        )

    def y_copy(k, d):
        return rem_copy(
            part_out.at[k, seg_of(ex_peer(d))], part_in.at[k, mine_seg],
            ys.at[k, d], yr.at[k, d], ex_peer(d), dp,
        )

    for k in range(cols):
        w1_copy(k).wait()
    lag = 2

    def first_matmul(k):
        def ff_step(n, c2):
            at = pl.ds(pl.multiple_of(n * FFB, FFB), FFB)
            got = lax.dot_general(
                rows_in[k], w1[k, at], (((1,), (1,)), ((), ())), preferred_element_type=F32
            )

            @pl.when(k == 0)
            def _():
                acc[n] = got

            @pl.when(k > 0)
            def _():
                acc[n] += got

            return c2

        lax.fori_loop(0, ffb, ff_step, 0)

    def in_step(s, carry):
        @pl.when(s < last)
        def _():
            for d in range(1, n_dp):
                z_copy(s, d).wait_recv()

            if relay:

                @pl.when(jnp.logical_and(inner, s >= 1))
                def _():
                    z_forward(s).start()

            @pl.when(s < last - ahead)
            def _():
                z_start(s + ahead)

            @pl.when(s == last - ahead - 1)
            def _():
                for d in range(1, n_ex):
                    x2_copy(d).wait_recv()
                for d in range(1, n_dp):
                    zx_copy(d).start()

            def rows_step(b, c2):
                at = pl.ds(pl.multiple_of(b * blk, 16), blk)
                rows_out[s, at] = jnp.dot(
                    place[at, :], frames[s], preferred_element_type=F32
                ).astype(BF)
                return c2

            lax.fori_loop(0, 4, rows_step, 0)
            for d in range(1, n_ex):
                x_copy(s, d).start()
            rows_in[s, mine_seg] = rows_out[s, mine_seg]

        @pl.when(s >= lag)
        def _():
            for d in range(1, n_ex):
                x_copy(s - lag, d).wait_recv()
            first_matmul(s - lag)

        return carry

    lax.fori_loop(0, last + lag, in_step, 0)
    for d in range(1, n_dp):
        zx_copy(d).wait_recv()

    def spread_step(u, carry):
        got = jnp.concatenate([rows2_in[v, pad_at(u)] for v in range(n_dp)], axis=0)
        rows_in[last, seg_of(u)] = jnp.dot(
            spread[...], got, preferred_element_type=F32
        ).astype(BF)
        return carry

    lax.fori_loop(0, n_ex, spread_step, 0)
    first_matmul(jnp.int32(last))

    def silu_step(b, carry):
        at = pl.ds(pl.multiple_of(b * blk, 16), blk)
        for n in range(ffb):
            hid[n, at] = silu(acc[n, at]).astype(BF)
        return carry

    lax.fori_loop(0, 4, silu_step, 0)

    for d in range(1, n_dp):
        info_copy(1, d, dp).wait_recv()
    eye = (
        lax.broadcasted_iota(jnp.int32, (tok, tok), 0)
        == lax.broadcasted_iota(jnp.int32, (tok, tok), 1)
    ).astype(F32)

    def gate_step(v, carry):
        turn = [
            lax.dot_general(
                eye, info[i, v], (((1,), (1,)), ((), ())),
                precision=lax.Precision.HIGHEST, preferred_element_type=F32,
            )
            for i in range(2)
        ]
        index = lax.broadcasted_iota(jnp.int32, (tok, slots), 1).astype(F32)
        gate[v] = (
            jnp.where(index == turn[0][:, 0:1], turn[1][:, 0:1], 0.0)
            + jnp.where(index == turn[0][:, 1:2], turn[1][:, 1:2], 0.0)
        ).astype(BF)
        return carry

    for k in range(cols):
        w2_copy(k).wait()

    def r_copy(k, d):
        return rem_copy(
            comb_out.at[k, dp_peer(d)], comb_in.at[k, dp], rs.at[k, d], rr.at[k, d],
            ex, dp_peer(d),
        )

    def add_copy(k):
        return rem_copy(
            comb_out.at[k, 3 - dp], added.at[k], ads.at[k], adr.at[k], ex, 1 + dp // 3
        )

    def r_start(k):
        for d in range(1, n_dp):
            if relay and d == 2:
                pl.when(jnp.logical_or(outer, k >= last - 1))(r_copy(k, d).start)
            else:
                unless_far(k < last - 1, d, r_copy(k, d).start)
        if relay:
            pl.when(jnp.logical_and(outer, k < last - 1))(add_copy(k).start)

    def r_late(k):
        add_copy(k).wait_recv()
        far = 3 * (2 - dp)
        comb_out[k, far] = (comb_out[k, far].astype(F32) + added[k].astype(F32)).astype(BF)
        r_copy(k, 2).start()

    def second_matmul(k):
        def rows_step(b, c2):
            at = pl.ds(pl.multiple_of(b * blk, 16), blk)
            value = jnp.dot(hid[0, at], w2[k, 0:FFB], preferred_element_type=F32)
            for n in range(1, ffb):
                value = value + jnp.dot(
                    hid[n, at], w2[k, n * FFB : (n + 1) * FFB], preferred_element_type=F32
                )
            part_out[k, at] = value.astype(BF)
            return c2

        lax.fori_loop(0, 4, rows_step, 0)

    def gather_step(u, carry):
        got = jnp.dot(
            gather[...], part_out[last, seg_of(u)], preferred_element_type=F32
        ).astype(BF)
        for v in range(n_dp):
            z2_out[v, pad_at(u)] = got[v * pad : (v + 1) * pad]
        return carry

    def out_step(s, carry):
        @pl.when(s < last)
        def _():
            second_matmul(s)
            for d in range(1, n_ex):
                y_copy(s, d).start()
            part_in[s, mine_seg] = part_out[s, mine_seg]

        @pl.when(s == 0)
        def _():
            second_matmul(jnp.int32(last))
            lax.fori_loop(0, n_ex, gather_step, 0)
            for d in range(1, n_dp):
                z2_copy(d).start()

        @pl.when(s == last - 1)
        def _():
            total2 = z2_out[dp].astype(F32)
            for d in range(1, n_dp):
                z2_copy(d).wait_recv()
            for d in range(1, n_dp):
                total2 = total2 + z2_in[dp_peer(d)].astype(F32)
            y2_out[...] = total2.astype(BF)
            for d in range(1, n_ex):
                y2_copy(d).start()
            y2_in[mine_pad, :] = y2_out[mine_pad, :]

        @pl.when(s == lag - 1)
        def _():
            lax.fori_loop(0, n_dp, gate_step, 0)
            turn = [
                lax.dot_general(
                    eye, mat, (((1,), (1,)), ((), ())),
                    precision=lax.Precision.HIGHEST, preferred_element_type=F32,
                )
                for mat in (info2[...], info[1, dp])
            ]
            across = lax.broadcasted_iota(jnp.int32, (tok, n_ex * pad), 1).astype(F32)
            gate2[...] = (
                jnp.where(across == turn[0][:, 0:1], turn[1][:, 0:1], 0.0)
                + jnp.where(across == turn[0][:, 1:2], turn[1][:, 1:2], 0.0)
            ).astype(BF)

        if relay:

            @pl.when(jnp.logical_and(inner, s > lag))
            def _():
                r_late(s - lag - 1)

        @pl.when(s >= lag)
        def _():
            k = s - lag
            at = pl.ds(pl.multiple_of(k * COL, COL), COL)
            for d in range(1, n_ex):
                y_copy(k, d).wait_recv()

            def comb_step(v, c2):
                value = jnp.dot(gate[v], part_in[k], preferred_element_type=F32)

                @pl.when(v == dp)
                def _():
                    res[:, at] += value

                @pl.when(v != dp)
                def _():
                    comb_out[k, v] = value.astype(BF)

                return c2

            lax.fori_loop(0, n_dp, comb_step, 0)
            r_start(k)

        return carry

    lax.fori_loop(0, last + lag, out_step, 0)
    for d in range(1, n_ex):
        y2_copy(d).wait_recv()
    ending = slice(last * COL, width)
    o_ref[0, :, ending] = (
        res[:, ending] + jnp.dot(gate2[...], y2_in[...], preferred_element_type=F32)
    ).astype(BF)

    def final_step(k, carry):
        at = pl.ds(pl.multiple_of(k * COL, COL), COL)

        def take(d):
            def run():
                r_copy(k, d).wait_recv()
                res[:, at] += comb_in[k, lax.rem(dp + n_dp - d, n_dp)].astype(F32)

            if relay and d == n_dp - 1:
                pl.when(jnp.logical_not(jnp.logical_and(k < last - 1, dp == n_dp - 1)))(run)
            elif relay and d == 1:
                pl.when(jnp.logical_not(jnp.logical_and(k < last - 1, dp == 0)))(run)
            else:
                run()

        for d in range(1, n_dp):
            take(d)
        o_ref[0, :, at] = res[:, at].astype(BF)
        for d in range(1, n_dp):
            unless_far(k >= 1, d, z_copy(k, d).wait_send)
            unless_far(k < last - 1, d, r_copy(k, d).wait_send)
        if relay:
            pl.when(jnp.logical_and(inner, k >= 1))(z_forward(k).wait_send)
            pl.when(jnp.logical_and(outer, k < last - 1))(add_copy(k).wait_send)
        for d in range(1, n_ex):
            x_copy(k, d).wait_send()
            y_copy(k, d).wait_send()
        return carry

    lax.fori_loop(0, last, final_step, 0)
    for d in range(1, n_dp):
        zx_copy(d).wait_send()
        z2_copy(d).wait_send()
    for d in range(1, n_ex):
        x2_copy(d).wait_send()
        y2_copy(d).wait_send()
    for d in range(1, n_dp):
        info_copy(0, d, dp).wait_send()
        info_copy(1, d, dp).wait_send()

    @pl.when(dp < n_dp - 1)
    def _():
        up_copy().wait_send()

    @pl.when(dp > 0)
    def _():
        down_copy().wait_send()


def kernel_shards(n_ex, n_dp, cap, frames_in, conv_kernel, norm_gain, router, w_in, w_out, routes):
    tok, width = frames_in.shape[1], frames_in.shape[2]
    ff = w_in.shape[1]
    cols, ffb = width // COL, ff // FFB
    slots = n_ex * n_dp * cap
    pad = pad_of(cap)
    wide = n_ex * pad
    dma = pltpu.SemaphoreType.DMA
    vmem = pl.BlockSpec(memory_space=pltpu.VMEM)
    hbm = pl.BlockSpec(memory_space=pl.ANY)
    return pl.pallas_call(
        functools.partial(moe_kernel, n_ex, n_dp, cap),
        out_shape=jax.ShapeDtypeStruct(frames_in.shape, BF),
        in_specs=[vmem] * 5 + [hbm] * 2,
        out_specs=vmem,
        scratch_shapes=[
            pltpu.VMEM((tok + 2 * HALO, width), BF),
            pltpu.VMEM((tok + 2 * HALO, LANE), F32),
            pltpu.VMEM((tok, width), F32),
            pltpu.VMEM((2, n_dp, 8, tok), F32),
            pltpu.VMEM((slots, n_dp * tok), BF),
            pltpu.VMEM((n_dp, tok, slots), BF),
            pltpu.VMEM((cols, n_dp * tok, COL), BF),
            pltpu.VMEM((cols, slots, COL), BF),
            pltpu.VMEM((cols, slots, COL), BF),
            pltpu.VMEM((ffb, slots, FFB), F32),
            pltpu.VMEM((ffb, slots, FFB), BF),
            pltpu.VMEM((cols, slots, COL), BF),
            pltpu.VMEM((cols, slots, COL), BF),
            pltpu.VMEM((cols, n_dp, tok, COL), BF),
            pltpu.VMEM((cols, n_dp, tok, COL), BF),
            pltpu.VMEM((cols, ff, COL), BF),
            pltpu.VMEM((cols, ff, COL), BF),
            pltpu.VMEM((n_ex, tok), F32),
            pltpu.VMEM((8, tok), F32),
            pltpu.VMEM((wide, tok), BF),
            pltpu.VMEM((tok, wide), BF),
            pltpu.VMEM((n_dp * cap, n_dp * pad), BF),
            pltpu.VMEM((n_dp * pad, n_dp * cap), BF),
            pltpu.VMEM((wide, COL), BF),
            pltpu.VMEM((n_dp, wide, COL), BF),
            pltpu.VMEM((n_dp, wide, COL), BF),
            pltpu.VMEM((n_dp, wide, COL), BF),
            pltpu.VMEM((wide, COL), BF),
            pltpu.VMEM((wide, COL), BF),
            dma((cols,)), dma((cols,)),
            dma((2,)), dma((2,)),
            dma((2, n_dp)), dma((2, n_dp)),
            dma((cols, n_dp)), dma((cols, n_dp)),
            dma((cols, n_ex)), dma((cols, n_ex)),
            dma((cols, n_ex)), dma((cols, n_ex)),
            dma((cols, n_dp)), dma((cols, n_dp)),
            dma((n_ex,)), dma((n_ex,)), dma((n_dp,)), dma((n_dp,)),
            dma((n_dp,)), dma((n_dp,)), dma((n_ex,)), dma((n_ex,)),
            pltpu.VMEM((cols, tok, COL), BF),
            dma((cols,)), dma((cols,)), dma((cols,)),
        ],
        compiler_params=pltpu.CompilerParams(
            collective_id=0, has_side_effects=True, vmem_limit_bytes=56 * 2**20
        ),
    )(frames_in, conv_kernel, norm_gain[None], router.T, routes[0].T, w_in, w_out)


def kernel_fits(n_ex, n_dp, cap, tok, width, ff, top_k, kernel_len):
    seg = n_dp * cap
    return (
        n_ex == 8 and n_dp > 1 and top_k == 2 and tok % LANE == 0 and width % COL == 0 and width >= 4 * COL
        and ff % FFB == 0 and seg % 16 == 0 and (n_ex * seg) % 64 == 0
        and kernel_len < 2 * HALO and kernel_len % 2 == 1
        and 8 * n_ex * seg * (width + ff) + 4 * ff * width < 40 * 2**20
    )


def body(mesh, *args):
    frames_in, conv_kernel, w_in, routes = args[0], args[1], args[4], args[6]
    n_ex, n_dp = mesh.shape["expert"], mesh.shape["dp"]
    tok, width, top_k = frames_in.shape[1], frames_in.shape[2], routes.shape[2]
    cap = max(2, 9 * top_k * tok // (8 * n_ex))
    if kernel_fits(n_ex, n_dp, cap, tok, width, w_in.shape[1], top_k, conv_kernel.shape[0]):
        return kernel_shards(n_ex, n_dp, cap, *args)
    return shards(*args)


def solution(mesh):
    return jax.shard_map(
        functools.partial(body, mesh),
        mesh=mesh,
        in_specs=(
            P("expert", "dp", None),
            P(),
            P(),
            P(),
            P("expert", "dp", None),
            P("expert", "dp", None),
            P("expert", "dp", None),
        ),
        out_specs=P("expert", "dp", None),
        check_vma=False,
    )
```

```python
import functools

import jax
import jax.numpy as jnp
from jax import lax
from jax.experimental import pallas as pl
from jax.experimental.pallas import tpu as pltpu
from jax.sharding import PartitionSpec as P


def swapped(value, axis, distance):
    mask = 2**distance
    pairs = [(source, source ^ mask) for source in range(lax.axis_size(axis))]
    return lax.ppermute(value, axis, pairs)


def extended(block, sides, width):
    for axis, dim in sides:
        count = lax.axis_size(axis)
        forward = [(i, i + 1) for i in range(count - 1)]
        backward = [(target, source) for source, target in forward]
        low = lax.ppermute(
            lax.slice_in_dim(block, block.shape[dim] - width, None, axis=dim), axis, forward
        )
        high = lax.ppermute(lax.slice_in_dim(block, 0, width, axis=dim), axis, backward)
        block = jnp.concatenate([low, block, high], axis=dim)
    return block


def expert_block(rows, first_w, second_w, row_bits, bit_count):
    place = lax.axis_index("dp")
    for bit in range(row_bits):
        other = swapped(rows, "dp", bit)
        upper = place >> bit & 1 == 1
        rows = jnp.concatenate(
            [jnp.where(upper, other, rows), jnp.where(upper, rows, other)], axis=0
        )
    stacked = jnp.stack([first_w, second_w])
    for bit in range(row_bits, bit_count):
        other = swapped(stacked, "dp", bit)
        stacked = jnp.concatenate([stacked, other], axis=1)
    preact = lax.dot_general(
        rows, stacked[0], (((1,), (1,)), ((), ())), preferred_element_type=jnp.float32
    )
    hidden = jax.nn.silu(preact).astype(jnp.bfloat16)
    partial_value = jnp.dot(hidden, stacked[1], preferred_element_type=jnp.float32)
    for bit in reversed(range(row_bits)):
        half_rows = partial_value.shape[0] // 2
        first_half = partial_value[:half_rows]
        second_half = partial_value[half_rows:]
        upper = place >> bit & 1 == 1
        outgoing = jnp.where(upper, first_half, second_half)
        kept = jnp.where(upper, second_half, first_half)
        partial_value = kept + swapped(outgoing.astype(jnp.bfloat16), "dp", bit).astype(
            outgoing.dtype
        )
    return partial_value


def shards(frames_in, conv_kernel, norm_gain, router, w_in, w_out, routes):
    tok_rows = frames_in.shape[1]
    features = frames_in.shape[2]
    kernel_len = conv_kernel.shape[0]
    margin = (kernel_len - 1) // 2
    padded = extended(frames_in, (("dp", 1),), margin)
    frames_f = frames_in[0].astype(jnp.float32)
    convolved = jnp.zeros((tok_rows, features), jnp.float32)
    for offset in range(kernel_len):
        convolved = convolved + conv_kernel[offset].astype(jnp.float32) * padded[
            0, offset : offset + tok_rows
        ].astype(jnp.float32)
    residual = frames_f + jax.nn.silu(convolved)
    scale_rms = lax.rsqrt(jnp.mean(residual * residual, axis=-1, keepdims=True) + 1e-06)
    normed = (residual * scale_rms * norm_gain.astype(jnp.float32)).astype(jnp.bfloat16)
    logits = jnp.dot(normed, router, preferred_element_type=jnp.float32)
    expert_count = router.shape[1]
    chosen = routes[0]
    top_k = chosen.shape[1]
    onehot = (chosen[:, :, None] == jnp.arange(expert_count, dtype=jnp.int32)).astype(jnp.float32)
    gating = jax.nn.sigmoid(jnp.sum(onehot * logits[:, None, :], axis=-1))
    pair_count = tok_rows * top_k
    flat_hot = onehot.reshape(pair_count, expert_count)
    positions = jnp.arange(pair_count, dtype=jnp.int32)
    earlier = (positions[:, None] > positions[None, :]).astype(jnp.float32)
    counts = jnp.dot(earlier, flat_hot, precision=lax.Precision.HIGHEST)
    slot_of = jnp.sum(counts * flat_hot, axis=-1).astype(jnp.int32)
    capacity = max(2, 9 * top_k * tok_rows // (8 * lax.axis_size("expert")))
    target = chosen.reshape(pair_count) * capacity + slot_of
    placing = (
        jnp.arange(expert_count * capacity, dtype=jnp.int32)[:, None] == target[None, :]
    ).astype(jnp.bfloat16)
    normed_rep = jnp.repeat(normed, top_k, axis=0)
    sent_normed = (
        jnp.dot(placing, normed_rep, preferred_element_type=jnp.float32)
        .astype(jnp.bfloat16)
        .reshape(expert_count, capacity, features)
    )
    received = lax.all_to_all(sent_normed, "expert", split_axis=0, concat_axis=0, tiled=True)
    slot_block = received.reshape(expert_count * capacity, features)
    bit_count = lax.axis_size("dp").bit_length() - 1
    row_bits = bit_count // 2
    summed = expert_block(slot_block, w_in[0], w_out[0], row_bits, bit_count)
    expert_out = summed.astype(jnp.bfloat16).reshape(expert_count, capacity, features)
    returned = lax.all_to_all(
        expert_out, "expert", split_axis=0, concat_axis=0, tiled=True
    ).reshape(expert_count * capacity, features)
    pulled_back = lax.dot_general(
        placing, returned, (((0,), (0,)), ((), ())), preferred_element_type=jnp.float32
    )
    pulled_back = pulled_back.reshape(tok_rows, top_k, features)
    combined = (residual + jnp.sum(gating[:, :, None] * pulled_back, axis=1)).astype(jnp.bfloat16)
    return combined[None]


COL = 256
FFB = 256
LANE = 128
HALO = 16
BF = jnp.bfloat16
F32 = jnp.float32
MESH = pl.DeviceIdType.MESH


def silu(v):
    half = 0.5 * v
    return half + half * jnp.tanh(half)


def pad_of(cap):
    return -(-cap // 16) * 16


def moe_kernel(
    n_ex, n_dp, cap,
    x_ref, ck_ref, gain_ref, rout_ref, routes_ref, w_in_ref, w_out_ref,
    o_ref,
    xp, xf, res, info, place, gate, frames, rows_out, rows_in, acc, hid, part_out, part_in,
    comb_out, comb_in, w1, w2, logit,
    info2, place2, gate2, spread, gather, rows2_out, rows2_in, z2_out, z2_in, y2_out, y2_in,
    w1_sem, w2_sem, halo_s, halo_r, info_s, info_r, zs, zr, xs, xr, ys, yr, rs, rr,
    x2s, x2r, zxs, zxr, z2s, z2r, y2s, y2r, added, fs, ads, adr,
):
    tok, width = x_ref.shape[1], x_ref.shape[2]
    ff = w_in_ref.shape[1]
    cols = width // COL
    ffb = ff // FFB
    taps_count = ck_ref.shape[0]
    margin = (taps_count - 1) // 2
    seg = n_dp * cap
    slots = n_ex * seg
    ex = lax.axis_index("expert")
    dp = lax.axis_index("dp")
    blk = slots // 4
    half = slots // 2
    pad = pad_of(cap)
    last = cols - 1

    def dp_peer(d):
        return lax.rem(dp + d, n_dp)

    def ex_peer(d):
        return lax.rem(ex + d, n_ex)

    def rem_copy(src, dst, ssem, rsem, e, v):
        return pltpu.make_async_remote_copy(
            src_ref=src, dst_ref=dst, send_sem=ssem, recv_sem=rsem,
            device_id=(e, v), device_id_type=MESH,
        )

    relay = n_dp == 4
    inner = jnp.logical_and(dp > 0, dp < n_dp - 1)
    outer = jnp.logical_not(inner)

    def unless_far(relayed, d, run):
        if relay and d == n_dp - 1:
            pl.when(jnp.logical_not(jnp.logical_and(relayed, dp == 0)))(run)
        elif relay and d == 1:
            pl.when(jnp.logical_not(jnp.logical_and(relayed, dp == n_dp - 1)))(run)
        else:
            run()

    barrier = pltpu.get_barrier_semaphore()
    for d in range(1, n_dp):
        pl.semaphore_signal(barrier, inc=1, device_id=(ex, dp_peer(d)), device_id_type=MESH)
    for d in range(1, n_ex):
        pl.semaphore_signal(barrier, inc=1, device_id=(ex_peer(d), dp), device_id_type=MESH)

    def w1_copy(k):
        return pltpu.make_async_copy(
            w_in_ref.at[0, :, pl.ds(k * COL, COL)], w1.at[k], w1_sem.at[k]
        )

    def w2_copy(k):
        return pltpu.make_async_copy(
            w_out_ref.at[0, :, pl.ds(k * COL, COL)], w2.at[k], w2_sem.at[k]
        )

    for k in range(cols):
        w1_copy(k).start()
        w2_copy(k).start()

    xp[HALO : HALO + tok, :] = x_ref[0]
    expert_of = lax.broadcasted_iota(jnp.int32, (n_ex, tok), 0)
    hot = [(expert_of == routes_ref[k : k + 1, :]).astype(F32) for k in range(2)]
    before = (
        lax.broadcasted_iota(jnp.int32, (tok, tok), 0)
        < lax.broadcasted_iota(jnp.int32, (tok, tok), 1)
    ).astype(BF)
    count = jnp.dot((hot[0] + hot[1]).astype(BF), before, preferred_element_type=F32)
    counts = [count, count + hot[0]]
    rows8 = lax.broadcasted_iota(jnp.int32, (8, tok), 0)
    slot = [jnp.sum(counts[k] * hot[k], axis=0, keepdims=True) for k in range(2)]
    named = [routes_ref[k : k + 1, :].astype(F32) for k in range(2)]
    targets = [named[k] * seg + (dp * cap).astype(F32) + slot[k] for k in range(2)]
    targets2 = [named[k] * pad + slot[k] for k in range(2)]
    info2[...] = jnp.where(rows8 == 0, targets2[0], targets2[1])
    index2 = lax.broadcasted_iota(jnp.int32, (n_ex * pad, tok), 0).astype(F32)
    place2[...] = (
        jnp.where(index2 == targets2[0], 1.0, 0.0) + jnp.where(index2 == targets2[1], 1.0, 0.0)
    ).astype(BF)

    def spread_of(shape, seg_dim):
        i = lax.broadcasted_iota(jnp.int32, shape, seg_dim)
        j = lax.broadcasted_iota(jnp.int32, shape, 1 - seg_dim)
        hits = jnp.zeros(shape, F32)
        for v in range(n_dp):
            inside = (i >= v * cap) & (i < (v + 1) * cap)
            hits = hits + jnp.where(inside & (j - i == v * (pad - cap)), 1.0, 0.0)
        return hits.astype(BF)

    spread[...] = spread_of((seg, n_dp * pad), 0)
    gather[...] = spread_of((n_dp * pad, seg), 1)
    info[0, dp] = jnp.where(rows8 == 0, targets[0], targets[1])

    def conv_rows(first, count):
        def step(c, carry):
            at = pl.ds(pl.multiple_of(c * LANE, LANE), LANE)
            span = count + 2 * HALO
            xf[0:span, :] = xp[first : first + span, at].astype(F32)
            taps = ck_ref[:, at].astype(F32)
            conv = jnp.zeros((count, LANE), F32)
            for r in range(8):
                begin = HALO - margin + r
                size = min(count + 24, span - begin)
                shifted = xf[begin : begin + size, :]
                for j in range(r, taps_count, 8):
                    conv = conv + taps[j : j + 1, :] * shifted[j - r : j - r + count, :]
            res[first : first + count, at] = xf[HALO : HALO + count, :] + silu(conv)
            return carry

        lax.fori_loop(0, width // LANE, step, 0)

    conv_rows(HALO, tok - 2 * HALO)

    pl.semaphore_wait(barrier, n_dp - 1 + n_ex - 1)

    def up_copy():
        return rem_copy(
            x_ref.at[0, pl.ds(tok - HALO, HALO)], xp.at[pl.ds(0, HALO)],
            halo_s.at[0], halo_r.at[0], ex, dp_peer(1),
        )

    def down_copy():
        return rem_copy(
            x_ref.at[0, pl.ds(0, HALO)], xp.at[pl.ds(HALO + tok, HALO)],
            halo_s.at[1], halo_r.at[1], ex, dp_peer(n_dp - 1),
        )

    @pl.when(dp < n_dp - 1)
    def _():
        up_copy().start()

    @pl.when(dp > 0)
    def _():
        down_copy().start()

    def info_copy(i, d, src):
        return rem_copy(
            info.at[i, src], info.at[i, src], info_s.at[i, d], info_r.at[i, d], ex, dp_peer(d)
        )

    for d in range(1, n_dp):
        info_copy(0, d, dp).start()

    @pl.when(dp == 0)
    def _():
        xp[0:HALO, :] = jnp.zeros((HALO, width), BF)

    @pl.when(dp == n_dp - 1)
    def _():
        xp[HALO + tok :, :] = jnp.zeros((HALO, width), BF)

    @pl.when(dp > 0)
    def _():
        up_copy().wait_recv()

    @pl.when(dp < n_dp - 1)
    def _():
        down_copy().wait_recv()

    conv_rows(0, HALO)
    conv_rows(tok - HALO, HALO)

    def square_step(k, total):
        at = pl.ds(pl.multiple_of(k * COL, COL), COL)
        return total + jnp.sum(res[:, at] * res[:, at], axis=1, keepdims=True)

    total = lax.fori_loop(0, cols, square_step, jnp.zeros((tok, 1), F32))
    scale = lax.rsqrt(total * (1.0 / width) + 1e-6)

    own = pl.ds(pl.multiple_of(dp * tok, tok), tok)

    def z_copy(k, d):
        return rem_copy(
            frames.at[k, own], frames.at[k, own], zs.at[k, d], zr.at[k, d], ex, dp_peer(d)
        )

    def z_start(k):
        for d in range(1, n_dp):
            unless_far(k >= 1, d, z_copy(k, d).start)

    def z_forward(k):
        block = pl.ds(pl.multiple_of((2 - dp) * 3 * tok, tok), tok)
        return rem_copy(
            frames.at[k, block], frames.at[k, block],
            fs.at[k], zr.at[k, 2 * dp - 1], ex, (dp - 1) * 3,
        )

    logit[...] = jnp.zeros_like(logit)
    ahead = 2

    def norm_step(k, carry):
        at = pl.ds(pl.multiple_of(k * COL, COL), COL)
        normed = (res[:, at] * scale * gain_ref[:, at].astype(F32)).astype(BF)
        frames[k, own] = normed

        @pl.when(k < ahead)
        def _():
            z_start(k)

        logit[...] += lax.dot_general(
            rout_ref[:, at], normed, (((1,), (1,)), ((), ())), preferred_element_type=F32
        )
        return carry

    lax.fori_loop(0, cols, norm_step, 0)
    mine_pad = pl.ds(pl.multiple_of(ex * pad, 16), pad)

    def pad_at(e):
        return pl.ds(pl.multiple_of(e * pad, 16), pad)

    def x2_copy(d):
        return rem_copy(
            rows2_out.at[pad_at(ex_peer(d))], rows2_in.at[dp, mine_pad],
            x2s.at[d], x2r.at[d], ex_peer(d), dp,
        )

    def zx_copy(d):
        return rem_copy(
            rows2_in.at[dp], rows2_in.at[dp], zxs.at[d], zxr.at[d], ex, dp_peer(d)
        )

    def zx_forward():
        block = (2 - dp) * 3
        return rem_copy(
            rows2_in.at[block], rows2_in.at[block],
            fs.at[last], zxr.at[2 * dp - 1], ex, (dp - 1) * 3,
        )

    def z2_copy(d):
        return rem_copy(
            z2_out.at[dp_peer(d)], z2_in.at[dp], z2s.at[d], z2r.at[d], ex, dp_peer(d)
        )

    def y2_copy(d):
        return rem_copy(
            y2_out.at[pad_at(ex_peer(d))], y2_in.at[mine_pad],
            y2s.at[d], y2r.at[d], ex_peer(d), dp,
        )

    rows2_out[...] = jnp.dot(
        place2[...], frames[last, own], preferred_element_type=F32
    ).astype(BF)
    for d in range(1, n_ex):
        x2_copy(d).start()
    rows2_in[dp, mine_pad] = rows2_out[mine_pad, :]
    gating = [
        1.0 / (1.0 + jnp.exp(-jnp.sum(hot[k] * logit[...], axis=0, keepdims=True)))
        for k in range(2)
    ]
    info[1, dp] = jnp.where(rows8 == 0, gating[0], gating[1])
    for d in range(1, n_dp):
        info_copy(1, d, dp).start()
    for d in range(1, n_dp):
        info_copy(0, d, dp).wait_recv()

    def place_step(b, carry):
        at = pl.ds(pl.multiple_of(b * blk, 16), blk)
        index = (lax.broadcasted_iota(jnp.int32, (blk, tok), 0) + b * blk).astype(F32)
        for v in range(n_dp):
            first, second = info[0, v, 0:1, :], info[0, v, 1:2, :]
            hits = jnp.where(index == first, 1.0, 0.0) + jnp.where(index == second, 1.0, 0.0)
            place[at, v * tok : (v + 1) * tok] = hits.astype(BF)
        return carry

    lax.fori_loop(0, 4, place_step, 0)

    mine_seg = pl.ds(pl.multiple_of(ex * seg, 16), seg)

    def seg_of(e):
        return pl.ds(pl.multiple_of(e * seg, 16), seg)

    def x_copy(k, d):
        return rem_copy(
            rows_out.at[k, seg_of(ex_peer(d))], rows_in.at[k, mine_seg],
            xs.at[k, d], xr.at[k, d], ex_peer(d), dp,
        )

    def y_copy(k, d):
        return rem_copy(
            part_out.at[k, seg_of(ex_peer(d))], part_in.at[k, mine_seg],
            ys.at[k, d], yr.at[k, d], ex_peer(d), dp,
        )

    for k in range(cols):
        w1_copy(k).wait()
    lag = 2

    def first_matmul(k):
        def ff_step(n, c2):
            at = pl.ds(pl.multiple_of(n * FFB, FFB), FFB)
            got = lax.dot_general(
                rows_in[k], w1[k, at], (((1,), (1,)), ((), ())), preferred_element_type=F32
            )

            @pl.when(k == 0)
            def _():
                acc[n] = got

            @pl.when(k > 0)
            def _():
                acc[n] += got

            return c2

        lax.fori_loop(0, ffb, ff_step, 0)

    def in_step(s, carry):
        @pl.when(s < last)
        def _():
            for d in range(1, n_dp):
                z_copy(s, d).wait_recv()

            if relay:

                @pl.when(jnp.logical_and(inner, s >= 1))
                def _():
                    z_forward(s).start()

            @pl.when(s < last - ahead)
            def _():
                z_start(s + ahead)

            @pl.when(s == last - ahead - 1)
            def _():
                for d in range(1, n_ex):
                    x2_copy(d).wait_recv()
                for d in range(1, n_dp):
                    unless_far(True, d, zx_copy(d).start)

            def rows_step(b, c2):
                at = pl.ds(pl.multiple_of(b * half, 16), half)
                rows_out[s, at] = jnp.dot(
                    place[at, :], frames[s], preferred_element_type=F32
                ).astype(BF)
                return c2

            lax.fori_loop(0, 2, rows_step, 0)
            for d in range(1, n_ex):
                x_copy(s, d).start()
            rows_in[s, mine_seg] = rows_out[s, mine_seg]

        if relay:

            @pl.when(jnp.logical_and(inner, s == last + lag - 1))
            def _():
                zx_copy(2).wait_recv()
                zx_forward().start()

        @pl.when(s >= lag)
        def _():
            for d in range(1, n_ex):
                x_copy(s - lag, d).wait_recv()
            first_matmul(s - lag)

        return carry

    lax.fori_loop(0, last + lag, in_step, 0)
    for d in range(1, n_dp):
        if relay and d == 2:
            pl.when(outer)(zx_copy(d).wait_recv)
        else:
            zx_copy(d).wait_recv()

    def spread_step(u, carry):
        got = jnp.concatenate([rows2_in[v, pad_at(u)] for v in range(n_dp)], axis=0)
        rows_in[last, seg_of(u)] = jnp.dot(
            spread[...], got, preferred_element_type=F32
        ).astype(BF)
        return carry

    lax.fori_loop(0, n_ex, spread_step, 0)
    first_matmul(jnp.int32(last))

    def silu_step(b, carry):
        at = pl.ds(pl.multiple_of(b * blk, 16), blk)
        for n in range(ffb):
            hid[n, at] = silu(acc[n, at]).astype(BF)
        return carry

    lax.fori_loop(0, 4, silu_step, 0)

    for d in range(1, n_dp):
        info_copy(1, d, dp).wait_recv()
    eye = (
        lax.broadcasted_iota(jnp.int32, (tok, tok), 0)
        == lax.broadcasted_iota(jnp.int32, (tok, tok), 1)
    ).astype(F32)

    def gate_step(v, carry):
        turn = [
            lax.dot_general(
                eye, info[i, v], (((1,), (1,)), ((), ())),
                precision=lax.Precision.HIGHEST, preferred_element_type=F32,
            )
            for i in range(2)
        ]
        index = lax.broadcasted_iota(jnp.int32, (tok, slots), 1).astype(F32)
        gate[pl.ds(pl.multiple_of(v * tok, tok), tok)] = (
            jnp.where(index == turn[0][:, 0:1], turn[1][:, 0:1], 0.0)
            + jnp.where(index == turn[0][:, 1:2], turn[1][:, 1:2], 0.0)
        ).astype(BF)
        return carry

    for k in range(cols):
        w2_copy(k).wait()

    def r_copy(k, d):
        return rem_copy(
            comb_out.at[k, dp_peer(d)], comb_in.at[k, dp], rs.at[k, d], rr.at[k, d],
            ex, dp_peer(d),
        )

    def add_copy(k):
        return rem_copy(
            comb_out.at[k, 3 - dp], added.at[k], ads.at[k], adr.at[k], ex, 1 + dp // 3
        )

    def r_start(k):
        for d in range(1, n_dp):
            if relay and d == 2:
                pl.when(jnp.logical_or(outer, k >= last - 1))(r_copy(k, d).start)
            else:
                unless_far(k < last - 1, d, r_copy(k, d).start)
        if relay:
            pl.when(jnp.logical_and(outer, k < last - 1))(add_copy(k).start)

    def r_late(k):
        add_copy(k).wait_recv()
        far = 3 * (2 - dp)
        comb_out[k, far] = (comb_out[k, far].astype(F32) + added[k].astype(F32)).astype(BF)
        r_copy(k, 2).start()

    def second_matmul(k):
        def rows_step(b, c2):
            at = pl.ds(pl.multiple_of(b * half, 16), half)
            value = jnp.dot(hid[0, at], w2[k, 0:FFB], preferred_element_type=F32)
            for n in range(1, ffb):
                value = value + jnp.dot(
                    hid[n, at], w2[k, n * FFB : (n + 1) * FFB], preferred_element_type=F32
                )
            part_out[k, at] = value.astype(BF)
            return c2

        lax.fori_loop(0, 2, rows_step, 0)

    def gather_step(u, carry):
        got = jnp.dot(
            gather[...], part_out[last, seg_of(u)], preferred_element_type=F32
        ).astype(BF)
        for v in range(n_dp):
            z2_out[v, pad_at(u)] = got[v * pad : (v + 1) * pad]
        return carry

    def out_step(s, carry):
        @pl.when(s < last)
        def _():
            second_matmul(s)
            for d in range(1, n_ex):
                y_copy(s, d).start()
            part_in[s, mine_seg] = part_out[s, mine_seg]

        @pl.when(s == 0)
        def _():
            second_matmul(jnp.int32(last))
            lax.fori_loop(0, n_ex, gather_step, 0)
            for d in range(1, n_dp):
                z2_copy(d).start()

        @pl.when(s == last - 1)
        def _():
            total2 = z2_out[dp].astype(F32)
            for d in range(1, n_dp):
                z2_copy(d).wait_recv()
            for d in range(1, n_dp):
                total2 = total2 + z2_in[dp_peer(d)].astype(F32)
            y2_out[...] = total2.astype(BF)
            for d in range(1, n_ex):
                y2_copy(d).start()
            y2_in[mine_pad, :] = y2_out[mine_pad, :]

        @pl.when(s == lag - 1)
        def _():
            lax.fori_loop(0, n_dp, gate_step, 0)
            turn = [
                lax.dot_general(
                    eye, mat, (((1,), (1,)), ((), ())),
                    precision=lax.Precision.HIGHEST, preferred_element_type=F32,
                )
                for mat in (info2[...], info[1, dp])
            ]
            across = lax.broadcasted_iota(jnp.int32, (tok, n_ex * pad), 1).astype(F32)
            gate2[...] = (
                jnp.where(across == turn[0][:, 0:1], turn[1][:, 0:1], 0.0)
                + jnp.where(across == turn[0][:, 1:2], turn[1][:, 1:2], 0.0)
            ).astype(BF)

        if relay:

            @pl.when(jnp.logical_and(inner, s > lag))
            def _():
                r_late(s - lag - 1)

        @pl.when(s >= lag)
        def _():
            k = s - lag
            at = pl.ds(pl.multiple_of(k * COL, COL), COL)
            for d in range(1, n_ex):
                y_copy(k, d).wait_recv()

            sums = jnp.dot(gate[...], part_in[k], preferred_element_type=F32)
            for v in range(n_dp):
                value = sums[v * tok : (v + 1) * tok]

                @pl.when(dp == v)
                def _(value=value):
                    res[:, at] += value

                @pl.when(dp != v)
                def _(v=v, value=value):
                    comb_out[k, v] = value.astype(BF)

            r_start(k)

        return carry

    lax.fori_loop(0, last + lag, out_step, 0)
    for d in range(1, n_ex):
        y2_copy(d).wait_recv()
    ending = slice(last * COL, width)
    o_ref[0, :, ending] = (
        res[:, ending] + jnp.dot(gate2[...], y2_in[...], preferred_element_type=F32)
    ).astype(BF)

    def final_step(k, carry):
        at = pl.ds(pl.multiple_of(k * COL, COL), COL)

        def take(d):
            def run():
                r_copy(k, d).wait_recv()
                res[:, at] += comb_in[k, lax.rem(dp + n_dp - d, n_dp)].astype(F32)

            if relay and d == n_dp - 1:
                pl.when(jnp.logical_not(jnp.logical_and(k < last - 1, dp == n_dp - 1)))(run)
            elif relay and d == 1:
                pl.when(jnp.logical_not(jnp.logical_and(k < last - 1, dp == 0)))(run)
            else:
                run()

        for d in range(1, n_dp):
            take(d)
        o_ref[0, :, at] = res[:, at].astype(BF)
        for d in range(1, n_dp):
            unless_far(k >= 1, d, z_copy(k, d).wait_send)
            unless_far(k < last - 1, d, r_copy(k, d).wait_send)
        if relay:
            pl.when(jnp.logical_and(inner, k >= 1))(z_forward(k).wait_send)
            pl.when(jnp.logical_and(outer, k < last - 1))(add_copy(k).wait_send)
        for d in range(1, n_ex):
            x_copy(k, d).wait_send()
            y_copy(k, d).wait_send()
        return carry

    lax.fori_loop(0, last, final_step, 0)
    for d in range(1, n_dp):
        unless_far(True, d, zx_copy(d).wait_send)
        z2_copy(d).wait_send()
    if relay:
        pl.when(inner)(zx_forward().wait_send)
    for d in range(1, n_ex):
        x2_copy(d).wait_send()
        y2_copy(d).wait_send()
    for d in range(1, n_dp):
        info_copy(0, d, dp).wait_send()
        info_copy(1, d, dp).wait_send()

    @pl.when(dp < n_dp - 1)
    def _():
        up_copy().wait_send()

    @pl.when(dp > 0)
    def _():
        down_copy().wait_send()


def kernel_shards(n_ex, n_dp, cap, frames_in, conv_kernel, norm_gain, router, w_in, w_out, routes):
    tok, width = frames_in.shape[1], frames_in.shape[2]
    ff = w_in.shape[1]
    cols, ffb = width // COL, ff // FFB
    slots = n_ex * n_dp * cap
    pad = pad_of(cap)
    wide = n_ex * pad
    dma = pltpu.SemaphoreType.DMA
    vmem = pl.BlockSpec(memory_space=pltpu.VMEM)
    hbm = pl.BlockSpec(memory_space=pl.ANY)
    return pl.pallas_call(
        functools.partial(moe_kernel, n_ex, n_dp, cap),
        out_shape=jax.ShapeDtypeStruct(frames_in.shape, BF),
        in_specs=[vmem] * 5 + [hbm] * 2,
        out_specs=vmem,
        scratch_shapes=[
            pltpu.VMEM((tok + 2 * HALO, width), BF),
            pltpu.VMEM((tok + 2 * HALO, LANE), F32),
            pltpu.VMEM((tok, width), F32),
            pltpu.VMEM((2, n_dp, 8, tok), F32),
            pltpu.VMEM((slots, n_dp * tok), BF),
            pltpu.VMEM((n_dp * tok, slots), BF),
            pltpu.VMEM((cols, n_dp * tok, COL), BF),
            pltpu.VMEM((cols, slots, COL), BF),
            pltpu.VMEM((cols, slots, COL), BF),
            pltpu.VMEM((ffb, slots, FFB), F32),
            pltpu.VMEM((ffb, slots, FFB), BF),
            pltpu.VMEM((cols, slots, COL), BF),
            pltpu.VMEM((cols, slots, COL), BF),
            pltpu.VMEM((cols, n_dp, tok, COL), BF),
            pltpu.VMEM((cols, n_dp, tok, COL), BF),
            pltpu.VMEM((cols, ff, COL), BF),
            pltpu.VMEM((cols, ff, COL), BF),
            pltpu.VMEM((n_ex, tok), F32),
            pltpu.VMEM((8, tok), F32),
            pltpu.VMEM((wide, tok), BF),
            pltpu.VMEM((tok, wide), BF),
            pltpu.VMEM((n_dp * cap, n_dp * pad), BF),
            pltpu.VMEM((n_dp * pad, n_dp * cap), BF),
            pltpu.VMEM((wide, COL), BF),
            pltpu.VMEM((n_dp, wide, COL), BF),
            pltpu.VMEM((n_dp, wide, COL), BF),
            pltpu.VMEM((n_dp, wide, COL), BF),
            pltpu.VMEM((wide, COL), BF),
            pltpu.VMEM((wide, COL), BF),
            dma((cols,)), dma((cols,)),
            dma((2,)), dma((2,)),
            dma((2, n_dp)), dma((2, n_dp)),
            dma((cols, n_dp)), dma((cols, n_dp)),
            dma((cols, n_ex)), dma((cols, n_ex)),
            dma((cols, n_ex)), dma((cols, n_ex)),
            dma((cols, n_dp)), dma((cols, n_dp)),
            dma((n_ex,)), dma((n_ex,)), dma((n_dp,)), dma((n_dp,)),
            dma((n_dp,)), dma((n_dp,)), dma((n_ex,)), dma((n_ex,)),
            pltpu.VMEM((cols, tok, COL), BF),
            dma((cols,)), dma((cols,)), dma((cols,)),
        ],
        compiler_params=pltpu.CompilerParams(
            collective_id=0, has_side_effects=True, vmem_limit_bytes=56 * 2**20
        ),
    )(frames_in, conv_kernel, norm_gain[None], router.T, routes[0].T, w_in, w_out)


def kernel_fits(n_ex, n_dp, cap, tok, width, ff, top_k, kernel_len):
    seg = n_dp * cap
    return (
        n_ex == 8 and n_dp > 1 and top_k == 2 and tok % LANE == 0 and width % COL == 0 and width >= 4 * COL
        and ff % FFB == 0 and seg % 16 == 0 and (n_ex * seg) % 64 == 0
        and kernel_len < 2 * HALO and kernel_len % 2 == 1
        and 8 * n_ex * seg * (width + ff) + 4 * ff * width < 40 * 2**20
    )


def body(mesh, *args):
    frames_in, conv_kernel, w_in, routes = args[0], args[1], args[4], args[6]
    n_ex, n_dp = mesh.shape["expert"], mesh.shape["dp"]
    tok, width, top_k = frames_in.shape[1], frames_in.shape[2], routes.shape[2]
    cap = max(2, 9 * top_k * tok // (8 * n_ex))
    if kernel_fits(n_ex, n_dp, cap, tok, width, w_in.shape[1], top_k, conv_kernel.shape[0]):
        return kernel_shards(n_ex, n_dp, cap, *args)
    return shards(*args)


def solution(mesh):
    return jax.shard_map(
        functools.partial(body, mesh),
        mesh=mesh,
        in_specs=(
            P("expert", "dp", None),
            P(),
            P(),
            P(),
            P("expert", "dp", None),
            P("expert", "dp", None),
            P("expert", "dp", None),
        ),
        out_specs=P("expert", "dp", None),
        check_vma=False,
    )
```

```python
import functools

import jax
import jax.numpy as jnp
from jax import lax
from jax.experimental import pallas as pl
from jax.experimental.pallas import tpu as pltpu
from jax.sharding import PartitionSpec as P


def swapped(value, axis, distance):
    mask = 2**distance
    pairs = [(source, source ^ mask) for source in range(lax.axis_size(axis))]
    return lax.ppermute(value, axis, pairs)


def extended(block, sides, width):
    for axis, dim in sides:
        count = lax.axis_size(axis)
        forward = [(i, i + 1) for i in range(count - 1)]
        backward = [(target, source) for source, target in forward]
        low = lax.ppermute(
            lax.slice_in_dim(block, block.shape[dim] - width, None, axis=dim), axis, forward
        )
        high = lax.ppermute(lax.slice_in_dim(block, 0, width, axis=dim), axis, backward)
        block = jnp.concatenate([low, block, high], axis=dim)
    return block


def expert_block(rows, first_w, second_w, row_bits, bit_count):
    place = lax.axis_index("dp")
    for bit in range(row_bits):
        other = swapped(rows, "dp", bit)
        upper = place >> bit & 1 == 1
        rows = jnp.concatenate(
            [jnp.where(upper, other, rows), jnp.where(upper, rows, other)], axis=0
        )
    stacked = jnp.stack([first_w, second_w])
    for bit in range(row_bits, bit_count):
        other = swapped(stacked, "dp", bit)
        stacked = jnp.concatenate([stacked, other], axis=1)
    preact = lax.dot_general(
        rows, stacked[0], (((1,), (1,)), ((), ())), preferred_element_type=jnp.float32
    )
    hidden = jax.nn.silu(preact).astype(jnp.bfloat16)
    partial_value = jnp.dot(hidden, stacked[1], preferred_element_type=jnp.float32)
    for bit in reversed(range(row_bits)):
        half_rows = partial_value.shape[0] // 2
        first_half = partial_value[:half_rows]
        second_half = partial_value[half_rows:]
        upper = place >> bit & 1 == 1
        outgoing = jnp.where(upper, first_half, second_half)
        kept = jnp.where(upper, second_half, first_half)
        partial_value = kept + swapped(outgoing.astype(jnp.bfloat16), "dp", bit).astype(
            outgoing.dtype
        )
    return partial_value


def shards(frames_in, conv_kernel, norm_gain, router, w_in, w_out, routes):
    tok_rows = frames_in.shape[1]
    features = frames_in.shape[2]
    kernel_len = conv_kernel.shape[0]
    margin = (kernel_len - 1) // 2
    padded = extended(frames_in, (("dp", 1),), margin)
    frames_f = frames_in[0].astype(jnp.float32)
    convolved = jnp.zeros((tok_rows, features), jnp.float32)
    for offset in range(kernel_len):
        convolved = convolved + conv_kernel[offset].astype(jnp.float32) * padded[
            0, offset : offset + tok_rows
        ].astype(jnp.float32)
    residual = frames_f + jax.nn.silu(convolved)
    scale_rms = lax.rsqrt(jnp.mean(residual * residual, axis=-1, keepdims=True) + 1e-06)
    normed = (residual * scale_rms * norm_gain.astype(jnp.float32)).astype(jnp.bfloat16)
    logits = jnp.dot(normed, router, preferred_element_type=jnp.float32)
    expert_count = router.shape[1]
    chosen = routes[0]
    top_k = chosen.shape[1]
    onehot = (chosen[:, :, None] == jnp.arange(expert_count, dtype=jnp.int32)).astype(jnp.float32)
    gating = jax.nn.sigmoid(jnp.sum(onehot * logits[:, None, :], axis=-1))
    pair_count = tok_rows * top_k
    flat_hot = onehot.reshape(pair_count, expert_count)
    positions = jnp.arange(pair_count, dtype=jnp.int32)
    earlier = (positions[:, None] > positions[None, :]).astype(jnp.float32)
    counts = jnp.dot(earlier, flat_hot, precision=lax.Precision.HIGHEST)
    slot_of = jnp.sum(counts * flat_hot, axis=-1).astype(jnp.int32)
    capacity = max(2, 9 * top_k * tok_rows // (8 * lax.axis_size("expert")))
    target = chosen.reshape(pair_count) * capacity + slot_of
    placing = (
        jnp.arange(expert_count * capacity, dtype=jnp.int32)[:, None] == target[None, :]
    ).astype(jnp.bfloat16)
    normed_rep = jnp.repeat(normed, top_k, axis=0)
    sent_normed = (
        jnp.dot(placing, normed_rep, preferred_element_type=jnp.float32)
        .astype(jnp.bfloat16)
        .reshape(expert_count, capacity, features)
    )
    received = lax.all_to_all(sent_normed, "expert", split_axis=0, concat_axis=0, tiled=True)
    slot_block = received.reshape(expert_count * capacity, features)
    bit_count = lax.axis_size("dp").bit_length() - 1
    row_bits = bit_count // 2
    summed = expert_block(slot_block, w_in[0], w_out[0], row_bits, bit_count)
    expert_out = summed.astype(jnp.bfloat16).reshape(expert_count, capacity, features)
    returned = lax.all_to_all(
        expert_out, "expert", split_axis=0, concat_axis=0, tiled=True
    ).reshape(expert_count * capacity, features)
    pulled_back = lax.dot_general(
        placing, returned, (((0,), (0,)), ((), ())), preferred_element_type=jnp.float32
    )
    pulled_back = pulled_back.reshape(tok_rows, top_k, features)
    combined = (residual + jnp.sum(gating[:, :, None] * pulled_back, axis=1)).astype(jnp.bfloat16)
    return combined[None]


COL = 256
FFB = 256
LANE = 128
HALO = 16
BF = jnp.bfloat16
F32 = jnp.float32
MESH = pl.DeviceIdType.MESH


def silu(v):
    half = 0.5 * v
    return half + half * jnp.tanh(half)


def pad_of(cap):
    return -(-cap // 16) * 16


def moe_kernel(
    n_ex, n_dp, cap,
    x_ref, ck_ref, gain_ref, rout_ref, routes_ref, w_in_ref, w_out_ref,
    o_ref,
    xp, xf, res, info, place, gate, frames, rows_out, rows_in, acc, hid, part_out, part_in,
    comb_out, comb_in, w1, w2, logit,
    info2, place2, gate2, spread, gather, rows2_out, rows2_in, z2_out, z2_in, y2_out, y2_in,
    w1_sem, w2_sem, halo_s, halo_r, info_s, info_r, zs, zr, xs, xr, ys, yr, rs, rr,
    x2s, x2r, zxs, zxr, z2s, z2r, y2s, y2r, added, fs, ads, adr,
):
    tok, width = x_ref.shape[1], x_ref.shape[2]
    ff = w_in_ref.shape[1]
    cols = width // COL
    ffb = ff // FFB
    taps_count = ck_ref.shape[0]
    margin = (taps_count - 1) // 2
    seg = n_dp * cap
    slots = n_ex * seg
    ex = lax.axis_index("expert")
    dp = lax.axis_index("dp")
    blk = slots // 4
    half = slots // 2
    pad = pad_of(cap)
    last = cols - 1

    def dp_peer(d):
        return lax.rem(dp + d, n_dp)

    def ex_peer(d):
        return lax.rem(ex + d, n_ex)

    def rem_copy(src, dst, ssem, rsem, e, v):
        return pltpu.make_async_remote_copy(
            src_ref=src, dst_ref=dst, send_sem=ssem, recv_sem=rsem,
            device_id=(e, v), device_id_type=MESH,
        )

    relay = n_dp == 4
    inner = jnp.logical_and(dp > 0, dp < n_dp - 1)
    outer = jnp.logical_not(inner)

    def unless_far(relayed, d, run):
        if relay and d == n_dp - 1:
            pl.when(jnp.logical_not(jnp.logical_and(relayed, dp == 0)))(run)
        elif relay and d == 1:
            pl.when(jnp.logical_not(jnp.logical_and(relayed, dp == n_dp - 1)))(run)
        else:
            run()

    barrier = pltpu.get_barrier_semaphore()
    for d in range(1, n_dp):
        pl.semaphore_signal(barrier, inc=1, device_id=(ex, dp_peer(d)), device_id_type=MESH)
    for d in range(1, n_ex):
        pl.semaphore_signal(barrier, inc=1, device_id=(ex_peer(d), dp), device_id_type=MESH)

    def w1_copy(k):
        return pltpu.make_async_copy(
            w_in_ref.at[0, :, pl.ds(k * COL, COL)], w1.at[k], w1_sem.at[k]
        )

    def w2_copy(k):
        return pltpu.make_async_copy(
            w_out_ref.at[0, :, pl.ds(k * COL, COL)], w2.at[k], w2_sem.at[k]
        )

    for k in range(cols):
        w1_copy(k).start()
        w2_copy(k).start()

    xp[HALO : HALO + tok, :] = x_ref[0]
    expert_of = lax.broadcasted_iota(jnp.int32, (n_ex, tok), 0)
    hot = [(expert_of == routes_ref[k : k + 1, :]).astype(F32) for k in range(2)]
    before = (
        lax.broadcasted_iota(jnp.int32, (tok, tok), 0)
        < lax.broadcasted_iota(jnp.int32, (tok, tok), 1)
    ).astype(BF)
    count = jnp.dot((hot[0] + hot[1]).astype(BF), before, preferred_element_type=F32)
    counts = [count, count + hot[0]]
    rows8 = lax.broadcasted_iota(jnp.int32, (8, tok), 0)
    slot = [jnp.sum(counts[k] * hot[k], axis=0, keepdims=True) for k in range(2)]
    named = [routes_ref[k : k + 1, :].astype(F32) for k in range(2)]
    targets = [named[k] * seg + (dp * cap).astype(F32) + slot[k] for k in range(2)]
    targets2 = [named[k] * pad + slot[k] for k in range(2)]
    info2[...] = jnp.where(rows8 == 0, targets2[0], targets2[1])
    index2 = lax.broadcasted_iota(jnp.int32, (n_ex * pad, tok), 0).astype(F32)
    place2[...] = (
        jnp.where(index2 == targets2[0], 1.0, 0.0) + jnp.where(index2 == targets2[1], 1.0, 0.0)
    ).astype(BF)

    def spread_of(shape, seg_dim):
        i = lax.broadcasted_iota(jnp.int32, shape, seg_dim)
        j = lax.broadcasted_iota(jnp.int32, shape, 1 - seg_dim)
        hits = jnp.zeros(shape, F32)
        for v in range(n_dp):
            inside = (i >= v * cap) & (i < (v + 1) * cap)
            hits = hits + jnp.where(inside & (j - i == v * (pad - cap)), 1.0, 0.0)
        return hits.astype(BF)

    spread[...] = spread_of((seg, n_dp * pad), 0)
    gather[...] = spread_of((n_dp * pad, seg), 1)
    info[0, dp] = jnp.where(rows8 == 0, targets[0], targets[1])

    def conv_rows(first, count):
        def step(c, carry):
            at = pl.ds(pl.multiple_of(c * LANE, LANE), LANE)
            span = count + 2 * HALO
            xf[0:span, :] = xp[first : first + span, at].astype(F32)
            taps = ck_ref[:, at].astype(F32)
            conv = jnp.zeros((count, LANE), F32)
            for r in range(8):
                begin = HALO - margin + r
                size = min(count + 24, span - begin)
                shifted = xf[begin : begin + size, :]
                for j in range(r, taps_count, 8):
                    conv = conv + taps[j : j + 1, :] * shifted[j - r : j - r + count, :]
            res[first : first + count, at] = xf[HALO : HALO + count, :] + silu(conv)
            return carry

        lax.fori_loop(0, width // LANE, step, 0)

    conv_rows(HALO, tok - 2 * HALO)

    pl.semaphore_wait(barrier, n_dp - 1 + n_ex - 1)

    def up_copy():
        return rem_copy(
            x_ref.at[0, pl.ds(tok - HALO, HALO)], xp.at[pl.ds(0, HALO)],
            halo_s.at[0], halo_r.at[0], ex, dp_peer(1),
        )

    def down_copy():
        return rem_copy(
            x_ref.at[0, pl.ds(0, HALO)], xp.at[pl.ds(HALO + tok, HALO)],
            halo_s.at[1], halo_r.at[1], ex, dp_peer(n_dp - 1),
        )

    @pl.when(dp < n_dp - 1)
    def _():
        up_copy().start()

    @pl.when(dp > 0)
    def _():
        down_copy().start()

    def info_copy(i, d, src):
        return rem_copy(
            info.at[i, src], info.at[i, src], info_s.at[i, d], info_r.at[i, d], ex, dp_peer(d)
        )

    for d in range(1, n_dp):
        info_copy(0, d, dp).start()

    @pl.when(dp == 0)
    def _():
        xp[0:HALO, :] = jnp.zeros((HALO, width), BF)

    @pl.when(dp == n_dp - 1)
    def _():
        xp[HALO + tok :, :] = jnp.zeros((HALO, width), BF)

    @pl.when(dp > 0)
    def _():
        up_copy().wait_recv()

    @pl.when(dp < n_dp - 1)
    def _():
        down_copy().wait_recv()

    conv_rows(0, HALO)
    conv_rows(tok - HALO, HALO)

    def square_step(k, total):
        at = pl.ds(pl.multiple_of(k * COL, COL), COL)
        return total + jnp.sum(res[:, at] * res[:, at], axis=1, keepdims=True)

    total = lax.fori_loop(0, cols, square_step, jnp.zeros((tok, 1), F32))
    scale = lax.rsqrt(total * (1.0 / width) + 1e-6)

    own = pl.ds(pl.multiple_of(dp * tok, tok), tok)

    def z_copy(k, d):
        return rem_copy(
            frames.at[k, own], frames.at[k, own], zs.at[k, d], zr.at[k, d], ex, dp_peer(d)
        )

    def z_start(k):
        for d in range(1, n_dp):
            unless_far(k >= 1, d, z_copy(k, d).start)

    def z_forward(k):
        block = pl.ds(pl.multiple_of((2 - dp) * 3 * tok, tok), tok)
        return rem_copy(
            frames.at[k, block], frames.at[k, block],
            fs.at[k], zr.at[k, 2 * dp - 1], ex, (dp - 1) * 3,
        )

    logit[...] = jnp.zeros_like(logit)
    ahead = 2

    def norm_step(k, carry):
        at = pl.ds(pl.multiple_of(k * COL, COL), COL)
        normed = (res[:, at] * scale * gain_ref[:, at].astype(F32)).astype(BF)
        frames[k, own] = normed

        @pl.when(k < ahead)
        def _():
            z_start(k)

        logit[...] += lax.dot_general(
            rout_ref[:, at], normed, (((1,), (1,)), ((), ())), preferred_element_type=F32
        )
        return carry

    lax.fori_loop(0, cols, norm_step, 0)
    mine_pad = pl.ds(pl.multiple_of(ex * pad, 16), pad)

    def pad_at(e):
        return pl.ds(pl.multiple_of(e * pad, 16), pad)

    def x2_copy(d):
        return rem_copy(
            rows2_out.at[pad_at(ex_peer(d))], rows2_in.at[dp, mine_pad],
            x2s.at[d], x2r.at[d], ex_peer(d), dp,
        )

    def zx_copy(d):
        return rem_copy(
            rows2_in.at[dp], rows2_in.at[dp], zxs.at[d], zxr.at[d], ex, dp_peer(d)
        )

    def zx_forward():
        block = (2 - dp) * 3
        return rem_copy(
            rows2_in.at[block], rows2_in.at[block],
            fs.at[last], zxr.at[2 * dp - 1], ex, (dp - 1) * 3,
        )

    def z2_copy(d):
        return rem_copy(
            z2_out.at[dp_peer(d)], z2_in.at[dp], z2s.at[d], z2r.at[d], ex, dp_peer(d)
        )

    def y2_copy(d):
        return rem_copy(
            y2_out.at[pad_at(ex_peer(d))], y2_in.at[mine_pad],
            y2s.at[d], y2r.at[d], ex_peer(d), dp,
        )

    rows2_out[...] = jnp.dot(
        place2[...], frames[last, own], preferred_element_type=F32
    ).astype(BF)
    for d in range(1, n_ex):
        x2_copy(d).start()
    rows2_in[dp, mine_pad] = rows2_out[mine_pad, :]
    gating = [
        1.0 / (1.0 + jnp.exp(-jnp.sum(hot[k] * logit[...], axis=0, keepdims=True)))
        for k in range(2)
    ]
    info[1, dp] = jnp.where(rows8 == 0, gating[0], gating[1])
    for d in range(1, n_dp):
        info_copy(1, d, dp).start()
    for d in range(1, n_dp):
        info_copy(0, d, dp).wait_recv()

    def place_step(b, carry):
        at = pl.ds(pl.multiple_of(b * blk, 16), blk)
        index = (lax.broadcasted_iota(jnp.int32, (blk, tok), 0) + b * blk).astype(F32)
        for v in range(n_dp):
            first, second = info[0, v, 0:1, :], info[0, v, 1:2, :]
            hits = jnp.where(index == first, 1.0, 0.0) + jnp.where(index == second, 1.0, 0.0)
            place[at, v * tok : (v + 1) * tok] = hits.astype(BF)
        return carry

    lax.fori_loop(0, 4, place_step, 0)

    mine_seg = pl.ds(pl.multiple_of(ex * seg, 16), seg)

    def seg_of(e):
        return pl.ds(pl.multiple_of(e * seg, 16), seg)

    def x_copy(k, d):
        return rem_copy(
            rows_out.at[k, seg_of(ex_peer(d))], rows_in.at[k, mine_seg],
            xs.at[k, d], xr.at[k, d], ex_peer(d), dp,
        )

    def y_copy(k, d):
        return rem_copy(
            part_out.at[k, seg_of(ex_peer(d))], part_in.at[k, mine_seg],
            ys.at[k, d], yr.at[k, d], ex_peer(d), dp,
        )

    for k in range(cols):
        w1_copy(k).wait()
    lag = 2

    def first_matmul(k):
        def ff_step(n, c2):
            at = pl.ds(pl.multiple_of(n * FFB, FFB), FFB)
            got = lax.dot_general(
                rows_in[k], w1[k, at], (((1,), (1,)), ((), ())), preferred_element_type=F32
            )

            @pl.when(k == 0)
            def _():
                acc[n] = got

            @pl.when(k > 0)
            def _():
                acc[n] += got

            return c2

        lax.fori_loop(0, ffb, ff_step, 0)

    def in_step(s, carry):
        @pl.when(s < last)
        def _():
            for d in range(1, n_dp):
                z_copy(s, d).wait_recv()

            if relay:

                @pl.when(jnp.logical_and(inner, s >= 1))
                def _():
                    z_forward(s).start()

            @pl.when(s < last - ahead)
            def _():
                z_start(s + ahead)

            @pl.when(s == last - ahead - 1)
            def _():
                for d in range(1, n_ex):
                    x2_copy(d).wait_recv()
                for d in range(1, n_dp):
                    unless_far(True, d, zx_copy(d).start)

            rows_out[s] = jnp.dot(
                place[...], frames[s], preferred_element_type=F32
            ).astype(BF)
            for d in range(1, n_ex):
                x_copy(s, d).start()
            rows_in[s, mine_seg] = rows_out[s, mine_seg]

        if relay:

            @pl.when(jnp.logical_and(inner, s == last + lag - 1))
            def _():
                zx_copy(2).wait_recv()
                zx_forward().start()

        @pl.when(s >= lag)
        def _():
            for d in range(1, n_ex):
                x_copy(s - lag, d).wait_recv()
            first_matmul(s - lag)

        return carry

    lax.fori_loop(0, last + lag, in_step, 0)
    for d in range(1, n_dp):
        if relay and d == 2:
            pl.when(outer)(zx_copy(d).wait_recv)
        else:
            zx_copy(d).wait_recv()

    def spread_step(u, carry):
        got = jnp.concatenate([rows2_in[v, pad_at(u)] for v in range(n_dp)], axis=0)
        rows_in[last, seg_of(u)] = jnp.dot(
            spread[...], got, preferred_element_type=F32
        ).astype(BF)
        return carry

    lax.fori_loop(0, n_ex, spread_step, 0)
    first_matmul(jnp.int32(last))

    def silu_step(b, carry):
        at = pl.ds(pl.multiple_of(b * blk, 16), blk)
        for n in range(ffb):
            hid[at, n * FFB : (n + 1) * FFB] = silu(acc[n, at]).astype(BF)
        return carry

    lax.fori_loop(0, 4, silu_step, 0)

    for d in range(1, n_dp):
        info_copy(1, d, dp).wait_recv()
    eye = (
        lax.broadcasted_iota(jnp.int32, (tok, tok), 0)
        == lax.broadcasted_iota(jnp.int32, (tok, tok), 1)
    ).astype(F32)

    def gate_step(v, carry):
        turn = [
            lax.dot_general(
                eye, info[i, v], (((1,), (1,)), ((), ())),
                precision=lax.Precision.HIGHEST, preferred_element_type=F32,
            )
            for i in range(2)
        ]
        index = lax.broadcasted_iota(jnp.int32, (tok, slots), 1).astype(F32)
        gate[pl.ds(pl.multiple_of(v * tok, tok), tok)] = (
            jnp.where(index == turn[0][:, 0:1], turn[1][:, 0:1], 0.0)
            + jnp.where(index == turn[0][:, 1:2], turn[1][:, 1:2], 0.0)
        ).astype(BF)
        return carry

    for k in range(cols):
        w2_copy(k).wait()

    def r_copy(k, d):
        return rem_copy(
            comb_out.at[k, dp_peer(d)], comb_in.at[k, dp], rs.at[k, d], rr.at[k, d],
            ex, dp_peer(d),
        )

    def add_copy(k):
        return rem_copy(
            comb_out.at[k, 3 - dp], added.at[k], ads.at[k], adr.at[k], ex, 1 + dp // 3
        )

    def r_start(k):
        for d in range(1, n_dp):
            if relay and d == 2:
                pl.when(jnp.logical_or(outer, k >= last - 1))(r_copy(k, d).start)
            else:
                unless_far(k < last - 1, d, r_copy(k, d).start)
        if relay:
            pl.when(jnp.logical_and(outer, k < last - 1))(add_copy(k).start)

    def r_late(k):
        add_copy(k).wait_recv()
        far = 3 * (2 - dp)
        comb_out[k, far] = (comb_out[k, far].astype(F32) + added[k].astype(F32)).astype(BF)
        r_copy(k, 2).start()

    def second_matmul(k):
        def rows_step(b, c2):
            at = pl.ds(pl.multiple_of(b * half, 16), half)
            value = jnp.dot(hid[at, :], w2[k], preferred_element_type=F32)
            part_out[k, at] = value.astype(BF)
            return c2

        lax.fori_loop(0, 2, rows_step, 0)

    def gather_step(u, carry):
        got = jnp.dot(
            gather[...], part_out[last, seg_of(u)], preferred_element_type=F32
        ).astype(BF)
        for v in range(n_dp):
            z2_out[v, pad_at(u)] = got[v * pad : (v + 1) * pad]
        return carry

    def out_step(s, carry):
        @pl.when(s < last)
        def _():
            second_matmul(s)
            for d in range(1, n_ex):
                y_copy(s, d).start()
            part_in[s, mine_seg] = part_out[s, mine_seg]

        @pl.when(s == 0)
        def _():
            second_matmul(jnp.int32(last))
            lax.fori_loop(0, n_ex, gather_step, 0)
            for d in range(1, n_dp):
                z2_copy(d).start()

        @pl.when(s == last - 1)
        def _():
            total2 = z2_out[dp].astype(F32)
            for d in range(1, n_dp):
                z2_copy(d).wait_recv()
            for d in range(1, n_dp):
                total2 = total2 + z2_in[dp_peer(d)].astype(F32)
            y2_out[...] = total2.astype(BF)
            for d in range(1, n_ex):
                y2_copy(d).start()
            y2_in[mine_pad, :] = y2_out[mine_pad, :]

        @pl.when(s == lag - 1)
        def _():
            lax.fori_loop(0, n_dp, gate_step, 0)
            turn = [
                lax.dot_general(
                    eye, mat, (((1,), (1,)), ((), ())),
                    precision=lax.Precision.HIGHEST, preferred_element_type=F32,
                )
                for mat in (info2[...], info[1, dp])
            ]
            across = lax.broadcasted_iota(jnp.int32, (tok, n_ex * pad), 1).astype(F32)
            gate2[...] = (
                jnp.where(across == turn[0][:, 0:1], turn[1][:, 0:1], 0.0)
                + jnp.where(across == turn[0][:, 1:2], turn[1][:, 1:2], 0.0)
            ).astype(BF)

        if relay:

            @pl.when(jnp.logical_and(inner, s > lag))
            def _():
                r_late(s - lag - 1)

        @pl.when(s >= lag)
        def _():
            k = s - lag
            at = pl.ds(pl.multiple_of(k * COL, COL), COL)
            for d in range(1, n_ex):
                y_copy(k, d).wait_recv()

            sums = jnp.dot(gate[...], part_in[k], preferred_element_type=F32)
            for v in range(n_dp):
                value = sums[v * tok : (v + 1) * tok]

                @pl.when(dp == v)
                def _(value=value):
                    res[:, at] += value

                @pl.when(dp != v)
                def _(v=v, value=value):
                    comb_out[k, v] = value.astype(BF)

            r_start(k)

        return carry

    lax.fori_loop(0, last + lag, out_step, 0)
    for d in range(1, n_ex):
        y2_copy(d).wait_recv()
    ending = slice(last * COL, width)
    o_ref[0, :, ending] = (
        res[:, ending] + jnp.dot(gate2[...], y2_in[...], preferred_element_type=F32)
    ).astype(BF)

    def final_step(k, carry):
        at = pl.ds(pl.multiple_of(k * COL, COL), COL)

        def take(d):
            def run():
                r_copy(k, d).wait_recv()
                res[:, at] += comb_in[k, lax.rem(dp + n_dp - d, n_dp)].astype(F32)

            if relay and d == n_dp - 1:
                pl.when(jnp.logical_not(jnp.logical_and(k < last - 1, dp == n_dp - 1)))(run)
            elif relay and d == 1:
                pl.when(jnp.logical_not(jnp.logical_and(k < last - 1, dp == 0)))(run)
            else:
                run()

        for d in range(1, n_dp):
            take(d)
        o_ref[0, :, at] = res[:, at].astype(BF)
        for d in range(1, n_dp):
            unless_far(k >= 1, d, z_copy(k, d).wait_send)
            unless_far(k < last - 1, d, r_copy(k, d).wait_send)
        if relay:
            pl.when(jnp.logical_and(inner, k >= 1))(z_forward(k).wait_send)
            pl.when(jnp.logical_and(outer, k < last - 1))(add_copy(k).wait_send)
        for d in range(1, n_ex):
            x_copy(k, d).wait_send()
            y_copy(k, d).wait_send()
        return carry

    lax.fori_loop(0, last, final_step, 0)
    for d in range(1, n_dp):
        unless_far(True, d, zx_copy(d).wait_send)
        z2_copy(d).wait_send()
    if relay:
        pl.when(inner)(zx_forward().wait_send)
    for d in range(1, n_ex):
        x2_copy(d).wait_send()
        y2_copy(d).wait_send()
    for d in range(1, n_dp):
        info_copy(0, d, dp).wait_send()
        info_copy(1, d, dp).wait_send()

    @pl.when(dp < n_dp - 1)
    def _():
        up_copy().wait_send()

    @pl.when(dp > 0)
    def _():
        down_copy().wait_send()


def kernel_shards(n_ex, n_dp, cap, frames_in, conv_kernel, norm_gain, router, w_in, w_out, routes):
    tok, width = frames_in.shape[1], frames_in.shape[2]
    ff = w_in.shape[1]
    cols, ffb = width // COL, ff // FFB
    slots = n_ex * n_dp * cap
    pad = pad_of(cap)
    wide = n_ex * pad
    dma = pltpu.SemaphoreType.DMA
    vmem = pl.BlockSpec(memory_space=pltpu.VMEM)
    hbm = pl.BlockSpec(memory_space=pl.ANY)
    return pl.pallas_call(
        functools.partial(moe_kernel, n_ex, n_dp, cap),
        out_shape=jax.ShapeDtypeStruct(frames_in.shape, BF),
        in_specs=[vmem] * 5 + [hbm] * 2,
        out_specs=vmem,
        scratch_shapes=[
            pltpu.VMEM((tok + 2 * HALO, width), BF),
            pltpu.VMEM((tok + 2 * HALO, LANE), F32),
            pltpu.VMEM((tok, width), F32),
            pltpu.VMEM((2, n_dp, 8, tok), F32),
            pltpu.VMEM((slots, n_dp * tok), BF),
            pltpu.VMEM((n_dp * tok, slots), BF),
            pltpu.VMEM((cols, n_dp * tok, COL), BF),
            pltpu.VMEM((cols, slots, COL), BF),
            pltpu.VMEM((cols, slots, COL), BF),
            pltpu.VMEM((ffb, slots, FFB), F32),
            pltpu.VMEM((slots, ff), BF),
            pltpu.VMEM((cols, slots, COL), BF),
            pltpu.VMEM((cols, slots, COL), BF),
            pltpu.VMEM((cols, n_dp, tok, COL), BF),
            pltpu.VMEM((cols, n_dp, tok, COL), BF),
            pltpu.VMEM((cols, ff, COL), BF),
            pltpu.VMEM((cols, ff, COL), BF),
            pltpu.VMEM((n_ex, tok), F32),
            pltpu.VMEM((8, tok), F32),
            pltpu.VMEM((wide, tok), BF),
            pltpu.VMEM((tok, wide), BF),
            pltpu.VMEM((n_dp * cap, n_dp * pad), BF),
            pltpu.VMEM((n_dp * pad, n_dp * cap), BF),
            pltpu.VMEM((wide, COL), BF),
            pltpu.VMEM((n_dp, wide, COL), BF),
            pltpu.VMEM((n_dp, wide, COL), BF),
            pltpu.VMEM((n_dp, wide, COL), BF),
            pltpu.VMEM((wide, COL), BF),
            pltpu.VMEM((wide, COL), BF),
            dma((cols,)), dma((cols,)),
            dma((2,)), dma((2,)),
            dma((2, n_dp)), dma((2, n_dp)),
            dma((cols, n_dp)), dma((cols, n_dp)),
            dma((cols, n_ex)), dma((cols, n_ex)),
            dma((cols, n_ex)), dma((cols, n_ex)),
            dma((cols, n_dp)), dma((cols, n_dp)),
            dma((n_ex,)), dma((n_ex,)), dma((n_dp,)), dma((n_dp,)),
            dma((n_dp,)), dma((n_dp,)), dma((n_ex,)), dma((n_ex,)),
            pltpu.VMEM((cols, tok, COL), BF),
            dma((cols,)), dma((cols,)), dma((cols,)),
        ],
        compiler_params=pltpu.CompilerParams(
            collective_id=0, has_side_effects=True, vmem_limit_bytes=56 * 2**20
        ),
    )(frames_in, conv_kernel, norm_gain[None], router.T, routes[0].T, w_in, w_out)


def kernel_fits(n_ex, n_dp, cap, tok, width, ff, top_k, kernel_len):
    seg = n_dp * cap
    return (
        n_ex == 8 and n_dp > 1 and top_k == 2 and tok % LANE == 0 and width % COL == 0 and width >= 4 * COL
        and ff % FFB == 0 and seg % 16 == 0 and (n_ex * seg) % 64 == 0
        and kernel_len < 2 * HALO and kernel_len % 2 == 1
        and 8 * n_ex * seg * (width + ff) + 4 * ff * width < 40 * 2**20
    )


def body(mesh, *args):
    frames_in, conv_kernel, w_in, routes = args[0], args[1], args[4], args[6]
    n_ex, n_dp = mesh.shape["expert"], mesh.shape["dp"]
    tok, width, top_k = frames_in.shape[1], frames_in.shape[2], routes.shape[2]
    cap = max(2, 9 * top_k * tok // (8 * n_ex))
    if kernel_fits(n_ex, n_dp, cap, tok, width, w_in.shape[1], top_k, conv_kernel.shape[0]):
        return kernel_shards(n_ex, n_dp, cap, *args)
    return shards(*args)


def solution(mesh):
    return jax.shard_map(
        functools.partial(body, mesh),
        mesh=mesh,
        in_specs=(
            P("expert", "dp", None),
            P(),
            P(),
            P(),
            P("expert", "dp", None),
            P("expert", "dp", None),
            P("expert", "dp", None),
        ),
        out_specs=P("expert", "dp", None),
        check_vma=False,
    )
```

```python
import functools

import jax
import jax.numpy as jnp
from jax import lax
from jax.experimental import pallas as pl
from jax.experimental.pallas import tpu as pltpu
from jax.sharding import PartitionSpec as P


def swapped(value, axis, distance):
    mask = 2**distance
    pairs = [(source, source ^ mask) for source in range(lax.axis_size(axis))]
    return lax.ppermute(value, axis, pairs)


def extended(block, sides, width):
    for axis, dim in sides:
        count = lax.axis_size(axis)
        forward = [(i, i + 1) for i in range(count - 1)]
        backward = [(target, source) for source, target in forward]
        low = lax.ppermute(
            lax.slice_in_dim(block, block.shape[dim] - width, None, axis=dim), axis, forward
        )
        high = lax.ppermute(lax.slice_in_dim(block, 0, width, axis=dim), axis, backward)
        block = jnp.concatenate([low, block, high], axis=dim)
    return block


def expert_block(rows, first_w, second_w, row_bits, bit_count):
    place = lax.axis_index("dp")
    for bit in range(row_bits):
        other = swapped(rows, "dp", bit)
        upper = place >> bit & 1 == 1
        rows = jnp.concatenate(
            [jnp.where(upper, other, rows), jnp.where(upper, rows, other)], axis=0
        )
    stacked = jnp.stack([first_w, second_w])
    for bit in range(row_bits, bit_count):
        other = swapped(stacked, "dp", bit)
        stacked = jnp.concatenate([stacked, other], axis=1)
    preact = lax.dot_general(
        rows, stacked[0], (((1,), (1,)), ((), ())), preferred_element_type=jnp.float32
    )
    hidden = jax.nn.silu(preact).astype(jnp.bfloat16)
    partial_value = jnp.dot(hidden, stacked[1], preferred_element_type=jnp.float32)
    for bit in reversed(range(row_bits)):
        half_rows = partial_value.shape[0] // 2
        first_half = partial_value[:half_rows]
        second_half = partial_value[half_rows:]
        upper = place >> bit & 1 == 1
        outgoing = jnp.where(upper, first_half, second_half)
        kept = jnp.where(upper, second_half, first_half)
        partial_value = kept + swapped(outgoing.astype(jnp.bfloat16), "dp", bit).astype(
            outgoing.dtype
        )
    return partial_value


def shards(frames_in, conv_kernel, norm_gain, router, w_in, w_out, routes):
    tok_rows = frames_in.shape[1]
    features = frames_in.shape[2]
    kernel_len = conv_kernel.shape[0]
    margin = (kernel_len - 1) // 2
    padded = extended(frames_in, (("dp", 1),), margin)
    frames_f = frames_in[0].astype(jnp.float32)
    convolved = jnp.zeros((tok_rows, features), jnp.float32)
    for offset in range(kernel_len):
        convolved = convolved + conv_kernel[offset].astype(jnp.float32) * padded[
            0, offset : offset + tok_rows
        ].astype(jnp.float32)
    residual = frames_f + jax.nn.silu(convolved)
    scale_rms = lax.rsqrt(jnp.mean(residual * residual, axis=-1, keepdims=True) + 1e-06)
    normed = (residual * scale_rms * norm_gain.astype(jnp.float32)).astype(jnp.bfloat16)
    logits = jnp.dot(normed, router, preferred_element_type=jnp.float32)
    expert_count = router.shape[1]
    chosen = routes[0]
    top_k = chosen.shape[1]
    onehot = (chosen[:, :, None] == jnp.arange(expert_count, dtype=jnp.int32)).astype(jnp.float32)
    gating = jax.nn.sigmoid(jnp.sum(onehot * logits[:, None, :], axis=-1))
    pair_count = tok_rows * top_k
    flat_hot = onehot.reshape(pair_count, expert_count)
    positions = jnp.arange(pair_count, dtype=jnp.int32)
    earlier = (positions[:, None] > positions[None, :]).astype(jnp.float32)
    counts = jnp.dot(earlier, flat_hot, precision=lax.Precision.HIGHEST)
    slot_of = jnp.sum(counts * flat_hot, axis=-1).astype(jnp.int32)
    capacity = max(2, 9 * top_k * tok_rows // (8 * lax.axis_size("expert")))
    target = chosen.reshape(pair_count) * capacity + slot_of
    placing = (
        jnp.arange(expert_count * capacity, dtype=jnp.int32)[:, None] == target[None, :]
    ).astype(jnp.bfloat16)
    normed_rep = jnp.repeat(normed, top_k, axis=0)
    sent_normed = (
        jnp.dot(placing, normed_rep, preferred_element_type=jnp.float32)
        .astype(jnp.bfloat16)
        .reshape(expert_count, capacity, features)
    )
    received = lax.all_to_all(sent_normed, "expert", split_axis=0, concat_axis=0, tiled=True)
    slot_block = received.reshape(expert_count * capacity, features)
    bit_count = lax.axis_size("dp").bit_length() - 1
    row_bits = bit_count // 2
    summed = expert_block(slot_block, w_in[0], w_out[0], row_bits, bit_count)
    expert_out = summed.astype(jnp.bfloat16).reshape(expert_count, capacity, features)
    returned = lax.all_to_all(
        expert_out, "expert", split_axis=0, concat_axis=0, tiled=True
    ).reshape(expert_count * capacity, features)
    pulled_back = lax.dot_general(
        placing, returned, (((0,), (0,)), ((), ())), preferred_element_type=jnp.float32
    )
    pulled_back = pulled_back.reshape(tok_rows, top_k, features)
    combined = (residual + jnp.sum(gating[:, :, None] * pulled_back, axis=1)).astype(jnp.bfloat16)
    return combined[None]


COL = 256
FFB = 256
LANE = 128
HALO = 16
BF = jnp.bfloat16
F32 = jnp.float32
MESH = pl.DeviceIdType.MESH


def silu(v):
    half = 0.5 * v
    return half + half * jnp.tanh(half)


def pad_of(cap):
    return -(-cap // 16) * 16


def moe_kernel(
    n_ex, n_dp, cap,
    x_ref, ck_ref, gain_ref, rout_ref, routes_ref, w_in_ref, w_out_ref,
    o_ref,
    xp, xf, res, info, place, gate, frames, rows_out, rows_in, acc, hid, part_out, part_in,
    comb_out, comb_in, w1, w2, logit,
    info2, place2, gate2, spread, gather, rows2_out, rows2_in, z2_out, z2_in, y2_out, y2_in,
    w1_sem, w2_sem, halo_s, halo_r, info_s, info_r, zs, zr, xs, xr, ys, yr, rs, rr,
    x2s, x2r, zxs, zxr, z2s, z2r, y2s, y2r, added, fs, ads, adr,
):
    tok, width = x_ref.shape[1], x_ref.shape[2]
    ff = w_in_ref.shape[1]
    cols = width // COL
    ffb = ff // FFB
    taps_count = ck_ref.shape[0]
    margin = (taps_count - 1) // 2
    seg = n_dp * cap
    slots = n_ex * seg
    ex = lax.axis_index("expert")
    dp = lax.axis_index("dp")
    blk = slots // 4
    half = slots // 2
    pad = pad_of(cap)
    last = cols - 1

    def dp_peer(d):
        return lax.rem(dp + d, n_dp)

    def ex_peer(d):
        return lax.rem(ex + d, n_ex)

    def rem_copy(src, dst, ssem, rsem, e, v):
        return pltpu.make_async_remote_copy(
            src_ref=src, dst_ref=dst, send_sem=ssem, recv_sem=rsem,
            device_id=(e, v), device_id_type=MESH,
        )

    relay = n_dp == 4
    inner = jnp.logical_and(dp > 0, dp < n_dp - 1)
    outer = jnp.logical_not(inner)

    def unless_far(relayed, d, run):
        if relay and d == n_dp - 1:
            pl.when(jnp.logical_not(jnp.logical_and(relayed, dp == 0)))(run)
        elif relay and d == 1:
            pl.when(jnp.logical_not(jnp.logical_and(relayed, dp == n_dp - 1)))(run)
        else:
            run()

    barrier = pltpu.get_barrier_semaphore()
    for d in range(1, n_dp):
        pl.semaphore_signal(barrier, inc=1, device_id=(ex, dp_peer(d)), device_id_type=MESH)
    for d in range(1, n_ex):
        pl.semaphore_signal(barrier, inc=1, device_id=(ex_peer(d), dp), device_id_type=MESH)

    def w1_copy(k):
        return pltpu.make_async_copy(
            w_in_ref.at[0, :, pl.ds(k * COL, COL)], w1.at[k], w1_sem.at[k]
        )

    def w2_copy(k):
        return pltpu.make_async_copy(
            w_out_ref.at[0, :, pl.ds(k * COL, COL)], w2.at[k], w2_sem.at[k]
        )

    for k in range(cols):
        w1_copy(k).start()
        w2_copy(k).start()

    xp[HALO : HALO + tok, :] = x_ref[0]
    expert_of = lax.broadcasted_iota(jnp.int32, (n_ex, tok), 0)
    hot = [(expert_of == routes_ref[k : k + 1, :]).astype(F32) for k in range(2)]
    before = (
        lax.broadcasted_iota(jnp.int32, (tok, tok), 0)
        < lax.broadcasted_iota(jnp.int32, (tok, tok), 1)
    ).astype(BF)
    count = jnp.dot((hot[0] + hot[1]).astype(BF), before, preferred_element_type=F32)
    counts = [count, count + hot[0]]
    rows8 = lax.broadcasted_iota(jnp.int32, (8, tok), 0)
    slot = [jnp.sum(counts[k] * hot[k], axis=0, keepdims=True) for k in range(2)]
    named = [routes_ref[k : k + 1, :].astype(F32) for k in range(2)]
    targets = [named[k] * seg + (dp * cap).astype(F32) + slot[k] for k in range(2)]
    targets2 = [named[k] * pad + slot[k] for k in range(2)]
    info2[...] = jnp.where(rows8 == 0, targets2[0], targets2[1])
    index2 = lax.broadcasted_iota(jnp.int32, (n_ex * pad, tok), 0).astype(F32)
    place2[...] = (
        jnp.where(index2 == targets2[0], 1.0, 0.0) + jnp.where(index2 == targets2[1], 1.0, 0.0)
    ).astype(BF)

    def spread_of(shape, seg_dim):
        i = lax.broadcasted_iota(jnp.int32, shape, seg_dim)
        j = lax.broadcasted_iota(jnp.int32, shape, 1 - seg_dim)
        hits = jnp.zeros(shape, F32)
        for v in range(n_dp):
            inside = (i >= v * cap) & (i < (v + 1) * cap)
            hits = hits + jnp.where(inside & (j - i == v * (pad - cap)), 1.0, 0.0)
        return hits.astype(BF)

    spread[...] = spread_of((seg, n_dp * pad), 0)
    gather[...] = spread_of((n_dp * pad, seg), 1)
    info[0, dp] = jnp.where(rows8 == 0, targets[0], targets[1])

    def conv_rows(first, count):
        def step(c, carry):
            at = pl.ds(pl.multiple_of(c * LANE, LANE), LANE)
            span = count + 2 * HALO
            xf[0:span, :] = xp[first : first + span, at].astype(F32)
            taps = ck_ref[:, at].astype(F32)
            conv = jnp.zeros((count, LANE), F32)
            for r in range(8):
                begin = HALO - margin + r
                size = min(count + 24, span - begin)
                shifted = xf[begin : begin + size, :]
                for j in range(r, taps_count, 8):
                    conv = conv + taps[j : j + 1, :] * shifted[j - r : j - r + count, :]
            res[first : first + count, at] = xf[HALO : HALO + count, :] + silu(conv)
            return carry

        lax.fori_loop(0, width // LANE, step, 0)

    conv_rows(HALO, tok - 2 * HALO)

    pl.semaphore_wait(barrier, n_dp - 1 + n_ex - 1)

    def up_copy():
        return rem_copy(
            x_ref.at[0, pl.ds(tok - HALO, HALO)], xp.at[pl.ds(0, HALO)],
            halo_s.at[0], halo_r.at[0], ex, dp_peer(1),
        )

    def down_copy():
        return rem_copy(
            x_ref.at[0, pl.ds(0, HALO)], xp.at[pl.ds(HALO + tok, HALO)],
            halo_s.at[1], halo_r.at[1], ex, dp_peer(n_dp - 1),
        )

    @pl.when(dp < n_dp - 1)
    def _():
        up_copy().start()

    @pl.when(dp > 0)
    def _():
        down_copy().start()

    def info_copy(i, d, src):
        return rem_copy(
            info.at[i, src], info.at[i, src], info_s.at[i, d], info_r.at[i, d], ex, dp_peer(d)
        )

    for d in range(1, n_dp):
        info_copy(0, d, dp).start()

    @pl.when(dp == 0)
    def _():
        xp[0:HALO, :] = jnp.zeros((HALO, width), BF)

    @pl.when(dp == n_dp - 1)
    def _():
        xp[HALO + tok :, :] = jnp.zeros((HALO, width), BF)

    @pl.when(dp > 0)
    def _():
        up_copy().wait_recv()

    @pl.when(dp < n_dp - 1)
    def _():
        down_copy().wait_recv()

    conv_rows(0, HALO)
    conv_rows(tok - HALO, HALO)

    def square_step(k, total):
        at = pl.ds(pl.multiple_of(k * COL, COL), COL)
        return total + jnp.sum(res[:, at] * res[:, at], axis=1, keepdims=True)

    total = lax.fori_loop(0, cols, square_step, jnp.zeros((tok, 1), F32))
    scale = lax.rsqrt(total * (1.0 / width) + 1e-6)

    own = pl.ds(pl.multiple_of(dp * tok, tok), tok)

    def z_copy(k, d):
        return rem_copy(
            frames.at[k, own], frames.at[k, own], zs.at[k, d], zr.at[k, d], ex, dp_peer(d)
        )

    def z_start(k):
        for d in range(1, n_dp):
            unless_far(k >= 1, d, z_copy(k, d).start)

    def z_forward(k):
        block = pl.ds(pl.multiple_of((2 - dp) * 3 * tok, tok), tok)
        return rem_copy(
            frames.at[k, block], frames.at[k, block],
            fs.at[k], zr.at[k, 2 * dp - 1], ex, (dp - 1) * 3,
        )

    logit[...] = jnp.zeros_like(logit)
    ahead = 3

    def norm_step(k, carry):
        at = pl.ds(pl.multiple_of(k * COL, COL), COL)
        normed = (res[:, at] * scale * gain_ref[:, at].astype(F32)).astype(BF)
        frames[k, own] = normed

        @pl.when(k < ahead)
        def _():
            z_start(k)

        logit[...] += lax.dot_general(
            rout_ref[:, at], normed, (((1,), (1,)), ((), ())), preferred_element_type=F32
        )
        return carry

    lax.fori_loop(0, cols, norm_step, 0)
    mine_pad = pl.ds(pl.multiple_of(ex * pad, 16), pad)

    def pad_at(e):
        return pl.ds(pl.multiple_of(e * pad, 16), pad)

    def x2_copy(d):
        return rem_copy(
            rows2_out.at[pad_at(ex_peer(d))], rows2_in.at[dp, mine_pad],
            x2s.at[d], x2r.at[d], ex_peer(d), dp,
        )

    def zx_copy(d):
        return rem_copy(
            rows2_in.at[dp], rows2_in.at[dp], zxs.at[d], zxr.at[d], ex, dp_peer(d)
        )

    def zx_forward():
        block = (2 - dp) * 3
        return rem_copy(
            rows2_in.at[block], rows2_in.at[block],
            fs.at[last], zxr.at[2 * dp - 1], ex, (dp - 1) * 3,
        )

    def z2_copy(d):
        return rem_copy(
            z2_out.at[dp_peer(d)], z2_in.at[dp], z2s.at[d], z2r.at[d], ex, dp_peer(d)
        )

    def y2_copy(d):
        return rem_copy(
            y2_out.at[pad_at(ex_peer(d))], y2_in.at[mine_pad],
            y2s.at[d], y2r.at[d], ex_peer(d), dp,
        )

    rows2_out[...] = jnp.dot(
        place2[...], frames[last, own], preferred_element_type=F32
    ).astype(BF)
    for d in range(1, n_ex):
        x2_copy(d).start()
    rows2_in[dp, mine_pad] = rows2_out[mine_pad, :]
    gating = [
        1.0 / (1.0 + jnp.exp(-jnp.sum(hot[k] * logit[...], axis=0, keepdims=True)))
        for k in range(2)
    ]
    info[1, dp] = jnp.where(rows8 == 0, gating[0], gating[1])
    for d in range(1, n_dp):
        info_copy(1, d, dp).start()
    for d in range(1, n_dp):
        info_copy(0, d, dp).wait_recv()

    def place_step(b, carry):
        at = pl.ds(pl.multiple_of(b * blk, 16), blk)
        index = (lax.broadcasted_iota(jnp.int32, (blk, tok), 0) + b * blk).astype(F32)
        for v in range(n_dp):
            first, second = info[0, v, 0:1, :], info[0, v, 1:2, :]
            hits = jnp.where(index == first, 1.0, 0.0) + jnp.where(index == second, 1.0, 0.0)
            place[at, v * tok : (v + 1) * tok] = hits.astype(BF)
        return carry

    lax.fori_loop(0, 4, place_step, 0)

    mine_seg = pl.ds(pl.multiple_of(ex * seg, 16), seg)

    def seg_of(e):
        return pl.ds(pl.multiple_of(e * seg, 16), seg)

    def x_copy(k, d):
        return rem_copy(
            rows_out.at[k, seg_of(ex_peer(d))], rows_in.at[k, mine_seg],
            xs.at[k, d], xr.at[k, d], ex_peer(d), dp,
        )

    def y_copy(k, d):
        return rem_copy(
            part_out.at[k, seg_of(ex_peer(d))], part_in.at[k, mine_seg],
            ys.at[k, d], yr.at[k, d], ex_peer(d), dp,
        )

    for k in range(cols):
        w1_copy(k).wait()
    lag = 2

    def first_matmul(k):
        def ff_step(n, c2):
            at = pl.ds(pl.multiple_of(n * FFB, FFB), FFB)
            got = lax.dot_general(
                rows_in[k], w1[k, at], (((1,), (1,)), ((), ())), preferred_element_type=F32
            )

            @pl.when(k == 0)
            def _():
                acc[n] = got

            @pl.when(k > 0)
            def _():
                acc[n] += got

            return c2

        lax.fori_loop(0, ffb, ff_step, 0)

    def in_step(s, carry):
        @pl.when(s < last)
        def _():
            for d in range(1, n_dp):
                z_copy(s, d).wait_recv()

            if relay:

                @pl.when(jnp.logical_and(inner, s >= 1))
                def _():
                    z_forward(s).start()

            @pl.when(s < last - ahead)
            def _():
                z_start(s + ahead)

            @pl.when(s == last - ahead - 1)
            def _():
                for d in range(1, n_ex):
                    x2_copy(d).wait_recv()
                for d in range(1, n_dp):
                    unless_far(True, d, zx_copy(d).start)

            rows_out[s] = jnp.dot(
                place[...], frames[s], preferred_element_type=F32
            ).astype(BF)
            for d in range(1, n_ex):
                x_copy(s, d).start()
            rows_in[s, mine_seg] = rows_out[s, mine_seg]

        if relay:

            @pl.when(jnp.logical_and(inner, s == last + lag - 1))
            def _():
                zx_copy(2).wait_recv()
                zx_forward().start()

        @pl.when(s >= lag)
        def _():
            for d in range(1, n_ex):
                x_copy(s - lag, d).wait_recv()
            first_matmul(s - lag)

        return carry

    lax.fori_loop(0, last + lag, in_step, 0)
    for d in range(1, n_dp):
        if relay and d == 2:
            pl.when(outer)(zx_copy(d).wait_recv)
        else:
            zx_copy(d).wait_recv()

    def spread_step(u, carry):
        got = jnp.concatenate([rows2_in[v, pad_at(u)] for v in range(n_dp)], axis=0)
        rows_in[last, seg_of(u)] = jnp.dot(
            spread[...], got, preferred_element_type=F32
        ).astype(BF)
        return carry

    lax.fori_loop(0, n_ex, spread_step, 0, unroll=True)
    first_matmul(jnp.int32(last))

    def silu_step(b, carry):
        at = pl.ds(pl.multiple_of(b * blk, 16), blk)
        for n in range(ffb):
            hid[at, n * FFB : (n + 1) * FFB] = silu(acc[n, at]).astype(BF)
        return carry

    lax.fori_loop(0, 4, silu_step, 0)

    for d in range(1, n_dp):
        info_copy(1, d, dp).wait_recv()
    eye = (
        lax.broadcasted_iota(jnp.int32, (tok, tok), 0)
        == lax.broadcasted_iota(jnp.int32, (tok, tok), 1)
    ).astype(F32)

    def gate_step(v, carry):
        turn = [
            lax.dot_general(
                eye, info[i, v], (((1,), (1,)), ((), ())),
                precision=lax.Precision.HIGHEST, preferred_element_type=F32,
            )
            for i in range(2)
        ]
        index = lax.broadcasted_iota(jnp.int32, (tok, slots), 1).astype(F32)
        gate[pl.ds(pl.multiple_of(v * tok, tok), tok)] = (
            jnp.where(index == turn[0][:, 0:1], turn[1][:, 0:1], 0.0)
            + jnp.where(index == turn[0][:, 1:2], turn[1][:, 1:2], 0.0)
        ).astype(BF)
        return carry

    for k in range(cols):
        w2_copy(k).wait()

    def r_copy(k, d):
        return rem_copy(
            comb_out.at[k, dp_peer(d)], comb_in.at[k, dp], rs.at[k, d], rr.at[k, d],
            ex, dp_peer(d),
        )

    def add_copy(k):
        return rem_copy(
            comb_out.at[k, 3 - dp], added.at[k], ads.at[k], adr.at[k], ex, 1 + dp // 3
        )

    def r_start(k):
        for d in range(1, n_dp):
            if relay and d == 2:
                pl.when(jnp.logical_or(outer, k >= last - 1))(r_copy(k, d).start)
            else:
                unless_far(k < last - 1, d, r_copy(k, d).start)
        if relay:
            pl.when(jnp.logical_and(outer, k < last - 1))(add_copy(k).start)

    def r_late(k):
        add_copy(k).wait_recv()
        far = 3 * (2 - dp)
        comb_out[k, far] = (comb_out[k, far].astype(F32) + added[k].astype(F32)).astype(BF)
        r_copy(k, 2).start()

    def second_matmul(k):
        def rows_step(b, c2):
            at = pl.ds(pl.multiple_of(b * half, 16), half)
            value = jnp.dot(hid[at, :], w2[k], preferred_element_type=F32)
            part_out[k, at] = value.astype(BF)
            return c2

        lax.fori_loop(0, 2, rows_step, 0)

    def gather_step(u, carry):
        got = jnp.dot(
            gather[...], part_out[last, seg_of(u)], preferred_element_type=F32
        ).astype(BF)
        for v in range(n_dp):
            z2_out[v, pad_at(u)] = got[v * pad : (v + 1) * pad]
        return carry

    def out_step(s, carry):
        @pl.when(s < last)
        def _():
            second_matmul(s)
            for d in range(1, n_ex):
                y_copy(s, d).start()
            part_in[s, mine_seg] = part_out[s, mine_seg]

        @pl.when(s == 0)
        def _():
            second_matmul(jnp.int32(last))
            lax.fori_loop(0, n_ex, gather_step, 0, unroll=True)
            for d in range(1, n_dp):
                z2_copy(d).start()

        @pl.when(s == last - 1)
        def _():
            total2 = z2_out[dp].astype(F32)
            for d in range(1, n_dp):
                z2_copy(d).wait_recv()
            for d in range(1, n_dp):
                total2 = total2 + z2_in[dp_peer(d)].astype(F32)
            y2_out[...] = total2.astype(BF)
            for d in range(1, n_ex):
                y2_copy(d).start()
            y2_in[mine_pad, :] = y2_out[mine_pad, :]

        @pl.when(s == lag - 1)
        def _():
            lax.fori_loop(0, n_dp, gate_step, 0)
            turn = [
                lax.dot_general(
                    eye, mat, (((1,), (1,)), ((), ())),
                    precision=lax.Precision.HIGHEST, preferred_element_type=F32,
                )
                for mat in (info2[...], info[1, dp])
            ]
            across = lax.broadcasted_iota(jnp.int32, (tok, n_ex * pad), 1).astype(F32)
            gate2[...] = (
                jnp.where(across == turn[0][:, 0:1], turn[1][:, 0:1], 0.0)
                + jnp.where(across == turn[0][:, 1:2], turn[1][:, 1:2], 0.0)
            ).astype(BF)

        if relay:

            @pl.when(jnp.logical_and(inner, s > lag))
            def _():
                r_late(s - lag - 1)

        @pl.when(s >= lag)
        def _():
            k = s - lag
            at = pl.ds(pl.multiple_of(k * COL, COL), COL)
            for d in range(1, n_ex):
                y_copy(k, d).wait_recv()

            sums = jnp.dot(gate[...], part_in[k], preferred_element_type=F32)
            for v in range(n_dp):
                value = sums[v * tok : (v + 1) * tok]

                @pl.when(dp == v)
                def _(value=value):
                    res[:, at] += value

                @pl.when(dp != v)
                def _(v=v, value=value):
                    comb_out[k, v] = value.astype(BF)

            r_start(k)

        return carry

    lax.fori_loop(0, last + lag, out_step, 0)
    for d in range(1, n_ex):
        y2_copy(d).wait_recv()
    ending = slice(last * COL, width)
    o_ref[0, :, ending] = (
        res[:, ending] + jnp.dot(gate2[...], y2_in[...], preferred_element_type=F32)
    ).astype(BF)

    def final_step(k, carry):
        at = pl.ds(pl.multiple_of(k * COL, COL), COL)

        def take(d):
            def run():
                r_copy(k, d).wait_recv()
                res[:, at] += comb_in[k, lax.rem(dp + n_dp - d, n_dp)].astype(F32)

            if relay and d == n_dp - 1:
                pl.when(jnp.logical_not(jnp.logical_and(k < last - 1, dp == n_dp - 1)))(run)
            elif relay and d == 1:
                pl.when(jnp.logical_not(jnp.logical_and(k < last - 1, dp == 0)))(run)
            else:
                run()

        for d in range(1, n_dp):
            take(d)
        o_ref[0, :, at] = res[:, at].astype(BF)
        for d in range(1, n_dp):
            unless_far(k >= 1, d, z_copy(k, d).wait_send)
            unless_far(k < last - 1, d, r_copy(k, d).wait_send)
        if relay:
            pl.when(jnp.logical_and(inner, k >= 1))(z_forward(k).wait_send)
            pl.when(jnp.logical_and(outer, k < last - 1))(add_copy(k).wait_send)
        for d in range(1, n_ex):
            x_copy(k, d).wait_send()
            y_copy(k, d).wait_send()
        return carry

    lax.fori_loop(0, last, final_step, 0)
    for d in range(1, n_dp):
        unless_far(True, d, zx_copy(d).wait_send)
        z2_copy(d).wait_send()
    if relay:
        pl.when(inner)(zx_forward().wait_send)
    for d in range(1, n_ex):
        x2_copy(d).wait_send()
        y2_copy(d).wait_send()
    for d in range(1, n_dp):
        info_copy(0, d, dp).wait_send()
        info_copy(1, d, dp).wait_send()

    @pl.when(dp < n_dp - 1)
    def _():
        up_copy().wait_send()

    @pl.when(dp > 0)
    def _():
        down_copy().wait_send()


def kernel_shards(n_ex, n_dp, cap, frames_in, conv_kernel, norm_gain, router, w_in, w_out, routes):
    tok, width = frames_in.shape[1], frames_in.shape[2]
    ff = w_in.shape[1]
    cols, ffb = width // COL, ff // FFB
    slots = n_ex * n_dp * cap
    pad = pad_of(cap)
    wide = n_ex * pad
    dma = pltpu.SemaphoreType.DMA
    vmem = pl.BlockSpec(memory_space=pltpu.VMEM)
    hbm = pl.BlockSpec(memory_space=pl.ANY)
    return pl.pallas_call(
        functools.partial(moe_kernel, n_ex, n_dp, cap),
        out_shape=jax.ShapeDtypeStruct(frames_in.shape, BF),
        in_specs=[vmem] * 5 + [hbm] * 2,
        out_specs=vmem,
        scratch_shapes=[
            pltpu.VMEM((tok + 2 * HALO, width), BF),
            pltpu.VMEM((tok + 2 * HALO, LANE), F32),
            pltpu.VMEM((tok, width), F32),
            pltpu.VMEM((2, n_dp, 8, tok), F32),
            pltpu.VMEM((slots, n_dp * tok), BF),
            pltpu.VMEM((n_dp * tok, slots), BF),
            pltpu.VMEM((cols, n_dp * tok, COL), BF),
            pltpu.VMEM((cols, slots, COL), BF),
            pltpu.VMEM((cols, slots, COL), BF),
            pltpu.VMEM((ffb, slots, FFB), F32),
            pltpu.VMEM((slots, ff), BF),
            pltpu.VMEM((cols, slots, COL), BF),
            pltpu.VMEM((cols, slots, COL), BF),
            pltpu.VMEM((cols, n_dp, tok, COL), BF),
            pltpu.VMEM((cols, n_dp, tok, COL), BF),
            pltpu.VMEM((cols, ff, COL), BF),
            pltpu.VMEM((cols, ff, COL), BF),
            pltpu.VMEM((n_ex, tok), F32),
            pltpu.VMEM((8, tok), F32),
            pltpu.VMEM((wide, tok), BF),
            pltpu.VMEM((tok, wide), BF),
            pltpu.VMEM((n_dp * cap, n_dp * pad), BF),
            pltpu.VMEM((n_dp * pad, n_dp * cap), BF),
            pltpu.VMEM((wide, COL), BF),
            pltpu.VMEM((n_dp, wide, COL), BF),
            pltpu.VMEM((n_dp, wide, COL), BF),
            pltpu.VMEM((n_dp, wide, COL), BF),
            pltpu.VMEM((wide, COL), BF),
            pltpu.VMEM((wide, COL), BF),
            dma((cols,)), dma((cols,)),
            dma((2,)), dma((2,)),
            dma((2, n_dp)), dma((2, n_dp)),
            dma((cols, n_dp)), dma((cols, n_dp)),
            dma((cols, n_ex)), dma((cols, n_ex)),
            dma((cols, n_ex)), dma((cols, n_ex)),
            dma((cols, n_dp)), dma((cols, n_dp)),
            dma((n_ex,)), dma((n_ex,)), dma((n_dp,)), dma((n_dp,)),
            dma((n_dp,)), dma((n_dp,)), dma((n_ex,)), dma((n_ex,)),
            pltpu.VMEM((cols, tok, COL), BF),
            dma((cols,)), dma((cols,)), dma((cols,)),
        ],
        compiler_params=pltpu.CompilerParams(
            collective_id=0, has_side_effects=True, vmem_limit_bytes=56 * 2**20
        ),
    )(frames_in, conv_kernel, norm_gain[None], router.T, routes[0].T, w_in, w_out)


def kernel_fits(n_ex, n_dp, cap, tok, width, ff, top_k, kernel_len):
    seg = n_dp * cap
    return (
        n_ex == 8 and n_dp > 1 and top_k == 2 and tok % LANE == 0 and width % COL == 0 and width >= 4 * COL
        and ff % FFB == 0 and seg % 16 == 0 and (n_ex * seg) % 64 == 0
        and kernel_len < 2 * HALO and kernel_len % 2 == 1
        and 8 * n_ex * seg * (width + ff) + 4 * ff * width < 40 * 2**20
    )


def body(mesh, *args):
    frames_in, conv_kernel, w_in, routes = args[0], args[1], args[4], args[6]
    n_ex, n_dp = mesh.shape["expert"], mesh.shape["dp"]
    tok, width, top_k = frames_in.shape[1], frames_in.shape[2], routes.shape[2]
    cap = max(2, 9 * top_k * tok // (8 * n_ex))
    if kernel_fits(n_ex, n_dp, cap, tok, width, w_in.shape[1], top_k, conv_kernel.shape[0]):
        return kernel_shards(n_ex, n_dp, cap, *args)
    return shards(*args)


def solution(mesh):
    return jax.shard_map(
        functools.partial(body, mesh),
        mesh=mesh,
        in_specs=(
            P("expert", "dp", None),
            P(),
            P(),
            P(),
            P("expert", "dp", None),
            P("expert", "dp", None),
            P("expert", "dp", None),
        ),
        out_specs=P("expert", "dp", None),
        check_vma=False,
    )
```
